128 devices in a mesh: row: 8 (over x, z_lo), col: 16 (over y, z_hi, core).
Axes of the slice: x: 4, y: 4, z: 4 (z_hi: 2, z_lo: 2; z = z_hi * 2 + z_lo), core: 2. Of those that a mesh axis runs over, the one named last changes fastest.
Arguments:
- features: bfloat16 [64, 256, 8, 64], P('row', 'col'), may hold values from -6 to 6
- block_active: int32 [8, 32, 1], P('row', 'col'), may hold values 0 or 1
- encode_fine: bfloat16 [3, 3, 3, 64, 64], replicated, may hold values from -0.15625 to 0.15625
- encode_coarse: bfloat16 [3, 3, 3, 64, 128], replicated, may hold values from -0.15625 to 0.15625
- decode_coarse: bfloat16 [3, 3, 3, 128, 128], replicated, may hold values from -0.109375 to 0.109375
- decode_fine: bfloat16 [3, 3, 3, 192, 64], replicated, may hold values from -0.078125 to 0.078125
- out_cotangent: bfloat16 [64, 256, 8, 64], P('row', 'col'), may hold values from -6 to 6
Outputs:
- decoded: bfloat16 [64, 256, 8, 64], P('row', 'col')
- grad_encode_fine: float32 [3, 3, 3, 64, 64], replicated
- grad_encode_coarse: float32 [3, 3, 3, 64, 128], replicated
- grad_decode_coarse: float32 [3, 3, 3, 128, 128], replicated
- grad_decode_fine: float32 [3, 3, 3, 192, 64], replicated
The draws below stay inside these ranges and needn't reach their ends.
All inputs are finite; a program needn't handle non-finite values. No bound on the sum of `block_active` on one device may be relied on, other than what follows from the above.
Results may differ from the reference program's by a relative error of at most 0.013.
Values may be sent and summed in bfloat16 or wider, within the bound.
No kernel may reach another device: no remote copies, remote signals or barrier semaphores. Data moves between devices by JAX's collectives and lax.ppermute only.
A program may use at most 128 MiB of HBM per device.

```python
import jax
import jax.numpy as jnp
from jax import lax

C0 = 64
C1 = 128
BLOCK = 8
BZ = 1
NBX = 8
NBY = 32
NX = 64
NY = 256
NZ = 8


def with_ends(entries, stream_key, least, largest):
    longest = entries.shape.index(max(entries.shape))
    spots = []
    for shift in (0, 1):
        where = [jax.random.randint(jax.random.fold_in(stream_key, axis), (), 0, length) for axis, length in enumerate(entries.shape)]
        where[longest] = (where[longest] + shift) % entries.shape[longest]
        spots.append(tuple(where))
    return entries.at[spots[0]].set(least).at[spots[1]].set(largest)


def block_scale(stream_key, shape, pieces, least, high):
    def one(axis_at, shards_of):
        steps = jax.random.uniform(jax.random.fold_in(jax.random.fold_in(stream_key, 6), axis_at), (shards_of,), jnp.float32, least / len(pieces), high / len(pieces))
        return jnp.repeat(jnp.exp(steps), shape[axis_at] // shards_of).reshape((-1,) + (1,) * (len(shape) - axis_at - 1))

    gain = one(*pieces[0])
    for cut in pieces[1:]:
        gain = gain * one(*cut)
    return gain


def noise(stream_key, shape, width, limit, pieces=(), dtype=jnp.bfloat16):
    drawn = width * jax.random.normal(stream_key, shape, jnp.float32)
    if pieces:
        drawn = drawn * block_scale(stream_key, shape, pieces, -0.22, 0.18)
    return jnp.clip(drawn, -limit, limit).astype(dtype)


def setup_inputs(seed: int = 0) -> dict:
    streams_of = jax.random.split(jax.random.key(seed), 8)
    return {
        "features": noise(streams_of[0], (NX, NY, NZ, C0), 1.0, 6.0, ((0, 8), (1, 16))),
        "block_active": with_ends((jax.random.randint(streams_of[1], (NBX, NBY, BZ), 0, 5) < 3).astype(jnp.int32), jax.random.fold_in(streams_of[1], 1), 0, 1),
        "encode_fine": noise(streams_of[2], (3, 3, 3, C0, C0), (27 * C0) ** -0.5, 0.15625),
        "encode_coarse": noise(streams_of[3], (3, 3, 3, C0, C1), (27 * C0) ** -0.5, 0.15625),
        "decode_coarse": noise(streams_of[4], (3, 3, 3, C1, C1), (27 * C1) ** -0.5, 0.109375),
        "decode_fine": noise(streams_of[5], (3, 3, 3, C1 + C0, C0), (27 * (C1 + C0)) ** -0.5, 0.078125),
        "out_cotangent": noise(streams_of[6], (NX, NY, NZ, C0), 1.0, 6.0, ((0, 8), (1, 16))),
    }


def silu_slope(values):
    sigma = jax.nn.sigmoid(values)
    return sigma * (1.0 + values * (1.0 - sigma))


def widen_mask(active, factor):
    return jnp.repeat(jnp.repeat(jnp.repeat(active, factor, 0), factor, 1), factor, 2)


def refine(volume):
    return jnp.repeat(jnp.repeat(jnp.repeat(volume, 2, 0), 2, 1), 2, 2)


def children_sum(volume):
    extent_x, extent_y, extent_z, depth = volume.shape
    grouped = volume.reshape(extent_x // 2, 2, extent_y // 2, 2, extent_z // 2, 2, depth)
    return jnp.sum(grouped, axis=(1, 3, 5))


def transpose_kernel(kernel):
    return jnp.transpose(kernel[::-1, ::-1, ::-1], (0, 1, 2, 4, 3))


def pad_all(volume):
    return jnp.pad(volume, ((1, 1), (1, 1), (1, 1), (0, 0)))


def correlate(padded, kernel):
    extent_x = padded.shape[0] - 2
    extent_y = padded.shape[1] - 2
    extent_z = padded.shape[2] - 2
    total = jnp.zeros((extent_x * extent_y * extent_z, kernel.shape[4]), jnp.float32)
    for offset in range(27):
        offset_x, offset_y, offset_z = offset // 9, (offset // 3) % 3, offset % 3
        window = padded[offset_x:offset_x + extent_x, offset_y:offset_y + extent_y, offset_z:offset_z + extent_z]
        total = total + jnp.dot(window.reshape(-1, padded.shape[3]), kernel[offset_x, offset_y, offset_z], preferred_element_type=jnp.float32)
    return total.reshape(extent_x, extent_y, extent_z, kernel.shape[4])


def weight_term(padded, grad):
    extent_x, extent_y, extent_z, depth = grad.shape
    rows = grad.reshape(-1, depth)
    parts = []
    for offset in range(27):
        offset_x, offset_y, offset_z = offset // 9, (offset // 3) % 3, offset % 3
        window = padded[offset_x:offset_x + extent_x, offset_y:offset_y + extent_y, offset_z:offset_z + extent_z]
        parts.append(lax.dot_general(window.reshape(-1, padded.shape[3]), rows, (((0,), (0,)), ((), ())), preferred_element_type=jnp.float32))
    return jnp.stack(parts).reshape(3, 3, 3, padded.shape[3], depth)


def reference(features, block_active, encode_fine, encode_coarse, decode_coarse, decode_fine, out_cotangent):
    factor = (NX * NY * NZ) ** -0.5
    active = block_active.astype(jnp.float32)
    mask_fine = widen_mask(active, BLOCK)[..., None]
    mask_coarse = widen_mask(active, BLOCK // 2)[..., None]
    masked_input = features * mask_fine.astype(jnp.bfloat16)
    input_pad = pad_all(masked_input)
    pre_ef = correlate(input_pad, encode_fine)
    enc_fine = (mask_fine * jax.nn.silu(pre_ef)).astype(jnp.bfloat16)
    pooled = (children_sum(enc_fine.astype(jnp.float32)) * 0.125).astype(jnp.bfloat16)
    pooled_pad = pad_all(pooled)
    pre_ec = correlate(pooled_pad, encode_coarse)
    enc_coarse = (mask_coarse * jax.nn.silu(pre_ec)).astype(jnp.bfloat16)
    enc_coarse_pad = pad_all(enc_coarse)
    pre_dc = correlate(enc_coarse_pad, decode_coarse)
    dec_coarse = (mask_coarse * jax.nn.silu(pre_dc)).astype(jnp.bfloat16)
    joined_pad = pad_all(jnp.concatenate([refine(dec_coarse), enc_fine], axis=3))
    pre_df = correlate(joined_pad, decode_fine)
    decoded = (mask_fine * jax.nn.silu(pre_df)).astype(jnp.bfloat16)
    g_df = (out_cotangent.astype(jnp.float32) * mask_fine * silu_slope(pre_df)).astype(jnp.bfloat16)
    grad_decode_fine = factor * weight_term(joined_pad, g_df)
    g_joined = correlate(pad_all(g_df), transpose_kernel(decode_fine))
    channels_up = decode_coarse.shape[4]
    g_lifted = g_joined[..., :channels_up]
    g_skip = g_joined[..., channels_up:]
    g_dc = (children_sum(g_lifted) * mask_coarse * silu_slope(pre_dc)).astype(jnp.bfloat16)
    grad_decode_coarse = factor * weight_term(enc_coarse_pad, g_dc)
    g_ec = (correlate(pad_all(g_dc), transpose_kernel(decode_coarse)) * mask_coarse * silu_slope(pre_ec)).astype(jnp.bfloat16)
    grad_encode_coarse = factor * weight_term(pooled_pad, g_ec)
    g_pooled = correlate(pad_all(g_ec), transpose_kernel(encode_coarse))
    g_ef = ((g_skip + 0.125 * refine(g_pooled)) * mask_fine * silu_slope(pre_ef)).astype(jnp.bfloat16)
    grad_encode_fine = factor * weight_term(input_pad, g_ef)
    return decoded, grad_encode_fine, grad_encode_coarse, grad_decode_coarse, grad_decode_fine
```

```python
import functools
import math

import jax
import jax.numpy as jnp
from jax import lax
from jax.experimental import pallas as pl
from jax.experimental.pallas import tpu as pltpu
from jax.sharding import Mesh, PartitionSpec as P

F32 = jnp.float32
BF16 = jnp.bfloat16
VMEM_LIMIT = 50 * 1024 * 1024
VM = pl.BlockSpec(memory_space=pltpu.VMEM)
SM = pl.BlockSpec(memory_space=pltpu.SMEM)
FACTOR = 1.0 / math.sqrt(64 * 256 * 8)
CHUNK = 72


def call(kernel, outs, scratch=(), flops=0, n_scalar=1, n_in=0):
    return pl.pallas_call(
        kernel,
        out_shape=[jax.ShapeDtypeStruct(s, d) for s, d in outs],
        in_specs=[SM] * n_scalar + [VM] * (n_in - n_scalar),
        out_specs=[VM] * len(outs),
        scratch_shapes=list(scratch),
        compiler_params=pltpu.CompilerParams(vmem_limit_bytes=VMEM_LIMIT),
        cost_estimate=pl.CostEstimate(flops=flops, bytes_accessed=4_000_000, transcendentals=0),
    )


def dot(lhs, rhs):
    return jnp.dot(lhs, rhs, preferred_element_type=F32)


def dot_t(lhs, rhs):
    return lax.dot_general(lhs, rhs, (((0,), (0,)), ((), ())), preferred_element_type=F32)


def bround(v):
    return v.astype(BF16).astype(F32)


def z_of(shape):
    return lax.broadcasted_iota(jnp.int32, shape, len(shape) - 2)


def z_later(v):
    return jnp.where(z_of(v.shape) > 0, pltpu.roll(v, 1, 1), 0.0)


def z_earlier(v):
    return jnp.where(z_of(v.shape) < 7, pltpu.roll(v, 7, 1), 0.0)


def fold64(acc):
    rows = acc.shape[0]
    cube = acc.reshape(rows // 8, 8, 192)
    ends, middle = cube[..., :128], cube[..., 128:]
    lane = lax.broadcasted_iota(jnp.int32, ends.shape, 2)
    z = z_of(ends.shape)
    low = lane < 64
    moved = jnp.where(low, pltpu.roll(ends, 1, 1), pltpu.roll(ends, 7, 1))
    moved = jnp.where(z == jnp.where(low, 0, 7), 0.0, moved)
    return moved[..., :64] + moved[..., 64:] + middle


def fold128(acc):
    rows = acc.shape[0]
    cube = acc.reshape(rows // 8, 8, 384)
    return z_later(cube[..., :128]) + cube[..., 128:256] + z_earlier(cube[..., 256:])


def taps_y(v, count):
    depth = v.shape[2]
    wide = jnp.concatenate([v[b : b + count] for b in range(3)], axis=2)
    return wide.reshape(count * 8, 3 * depth).astype(BF16)


def taps_z(g):
    wide = jnp.concatenate([z_earlier(g), g, z_later(g)], axis=2)
    return wide.reshape(g.shape[0] * 8, 3 * g.shape[2]).astype(BF16)


def halve_z(s):
    pair = s + pltpu.roll(s, 7, 1)
    z = z_of(s.shape)
    out = jnp.where(z == 0, pair, 0.0)
    for zc in (1, 2, 3):
        out = jnp.where(z == zc, pltpu.roll(pair, 8 - zc, 1), out)
    return out


def double_z(u):
    z = z_of(u.shape)
    out = u
    for shift in (1, 2, 3, 4):
        out = jnp.where((z + 1) // 2 == shift, pltpu.roll(u, shift, 1), out)
    return out


def silu_parts(v):
    sigma = jax.nn.sigmoid(v)
    act = v * sigma
    return act, sigma + act * (1.0 - sigma)


def mask_rows(sc):
    row = lax.broadcasted_iota(jnp.int32, (128, 64), 0)
    return jnp.where(row < 64, sc[6], sc[7]).astype(F32)


def pack_x(sc, feat, cot, p1, p2):
    mask = mask_rows(sc)
    for p, odd in ((p1, sc[0]), (p2, 1 - sc[0])):
        first = 1 - odd
        for k in range(7):
            p[k] = (feat[first + k].astype(F32) * mask).astype(BF16)
        p[7] = cot[7 * first]
        p[8] = mask.astype(BF16)


def pack_y(sc, feat, cot, rz, rxz, xall, p3, p4):
    mask = mask_rows(sc)
    odd = sc[0] == 1
    v_lo, v_hi = sc[1].astype(F32), sc[2].astype(F32)

    def lo(k):
        return jnp.where(odd, rz[k].astype(F32), rxz[k].astype(F32)) * v_lo

    def hi(k):
        return jnp.where(odd, rxz[k].astype(F32), rz[k].astype(F32)) * v_hi

    for k in range(7):
        xall[k] = lo(k).astype(BF16)
        xall[15 + k] = hi(k).astype(BF16)
    for k in range(8):
        xall[7 + k] = (feat[k].astype(F32) * mask).astype(BF16)
        xall[23 + k] = cot[k]
    xall[22] = lo(7).astype(BF16)
    xall[31] = hi(7).astype(BF16)
    xall[32] = lo(8).astype(BF16)
    xall[33] = mask.astype(BF16)
    xall[34] = hi(8).astype(BF16)
    odd_c = sc[3] == 1
    for p, low in ((p3, odd_c), (p4, jnp.logical_not(odd_c))):
        for k in range(22):
            p[k] = jnp.where(low, xall[k, 0:64].astype(F32), xall[k, 64:128].astype(F32)).astype(BF16)
        cols = []
        for k in range(22, 35):
            slab = xall[k].astype(F32)
            cols.append(jnp.where(low, slab[0:8], slab[120:128]))
        cols += [jnp.zeros((24, 64), F32)]
        extra = jnp.concatenate(cols, axis=0).astype(BF16)
        p[22] = extra[0:64]
        p[23] = extra[64:128]


def forward(
    sc, xall, r3, r4, w1, w2, w3, w4l, w4e, w5,
    decoded, slope_ef, g_skip, slope_ec, g_dc, s_in, s_pool, s_ec, s_lift, s_skip, gz,
    ff, mm, cc, s1, ee, po, s2, ec, s3, slope_dc, gd, s4,
):
    odd = sc[3] == 1
    v_lo, v_hi = sc[4].astype(F32), sc[5].astype(F32)

    def lo(k):
        return jnp.where(odd, r3[k].astype(F32), r4[k].astype(F32)) * v_lo

    def hi(k):
        return jnp.where(odd, r4[k].astype(F32), r3[k].astype(F32)) * v_hi

    def gather(x, _):
        ff[x, 0:8] = lo(x).reshape(8, 8, 64)
        ff[x, 8:24] = xall[x].astype(F32).reshape(16, 8, 64)
        ff[x, 24:32] = hi(x).reshape(8, 8, 64)
        return 0

    lax.fori_loop(0, 22, gather, 0)
    extra_lo = jnp.concatenate([lo(22), lo(23)], axis=0).reshape(16, 8, 64)
    extra_hi = jnp.concatenate([hi(22), hi(23)], axis=0).reshape(16, 8, 64)
    for k in range(10):
        cc[k, 0] = extra_lo[k]
        cc[k, 1:17] = xall[22 + k].astype(F32).reshape(16, 8, 64)
        cc[k, 17] = extra_hi[k]
    for k in range(3):
        mm[k, 0:8] = jnp.broadcast_to(extra_lo[10 + k][None], (8, 8, 64))
        mm[k, 8:24] = xall[32 + k].astype(F32).reshape(16, 8, 64)
        mm[k, 24:32] = jnp.broadcast_to(extra_hi[10 + k][None], (8, 8, 64))

    def spread(x, _):
        v = ff[x]
        zero = jnp.zeros((1, 8, 64), F32)
        s1[x] = taps_y(jnp.concatenate([zero, v, zero], axis=0), 32)
        return 0

    lax.fori_loop(0, 22, spread, 0)

    def encode(x, _):
        acc = dot(s1[x], w1[0]) + dot(s1[x + 1], w1[1]) + dot(s1[x + 2], w1[2])
        pre = fold64(acc)
        mask = mm[jnp.where(x < 6, 0, jnp.where(x < 14, 1, 2))]
        act, slope = silu_parts(pre)
        ee[x] = bround(act * mask)

        @pl.when(jnp.logical_and(x >= 6, x < 14))
        def _():
            slope_ef[x - 6] = (slope * mask)[8:24].reshape(128, 64)

        return 0

    lax.fori_loop(0, 20, encode, 0)
    for x in range(10):
        s_in[x] = taps_y(ff[6 + x, 7:25], 16)

    def pool(x, _):
        s = (ee[2 * x] + ee[2 * x + 1]).reshape(16, 2, 8, 64)
        v = bround(halve_z(s[:, 0] + s[:, 1]) * 0.125)
        po[x] = v
        zero = jnp.zeros((1, 8, 64), F32)
        s2[x] = taps_y(jnp.concatenate([zero, v, zero], axis=0), 16)
        return 0

    lax.fori_loop(0, 10, pool, 0)
    for x in range(6):
        s_pool[x] = taps_y(po[2 + x, 3:13], 8)

    def mask_coarse(block):
        m = mm[block].reshape(16, 2, 8, 64)[:, 0]
        m = jnp.concatenate([m, m], axis=2)
        return jnp.where(z_of(m.shape) < 4, m, 0.0)

    def encode2(x, _):
        acc = dot(s2[x], w2[0]) + dot(s2[x + 1], w2[1]) + dot(s2[x + 2], w2[2])
        mask = mask_coarse(jnp.where(x < 2, 0, jnp.where(x < 6, 1, 2)))
        act, slope = silu_parts(fold128(acc))
        v = bround(act * mask)
        ec[x] = v
        zero = jnp.zeros((1, 8, 128), F32)
        s3[x] = taps_y(jnp.concatenate([zero, v, zero], axis=0), 16)

        @pl.when(jnp.logical_and(x >= 1, x < 7))
        def _():
            slope_ec[x - 1] = (slope * mask)[3:13].reshape(80, 128)

        return 0

    lax.fori_loop(0, 8, encode2, 0)
    for x in range(6):
        s_ec[x] = taps_y(ec[1 + x, 3:13], 8)

    def decode2(x, _):
        acc = dot(s3[x], w3[0]) + dot(s3[x + 1], w3[1]) + dot(s3[x + 2], w3[2])
        mask = mask_coarse(jnp.where(x < 1, 0, jnp.where(x < 5, 1, 2)))
        act, slope = silu_parts(fold128(acc))
        v = double_z(bround(act * mask)[3:13])
        up = jnp.concatenate([v[:, None], v[:, None]], axis=1).reshape(20, 8, 128)
        wide = taps_y(up, 18)
        s_lift[2 * x] = wide
        s_lift[2 * x + 1] = wide

        @pl.when(jnp.logical_and(x >= 1, x < 5))
        def _():
            slope_dc[x - 1] = (slope * mask)[4:12]

        return 0

    lax.fori_loop(0, 6, decode2, 0)

    def skip(x, _):
        s_skip[x] = taps_y(ee[x + 4, 6:26], 18)
        return 0

    lax.fori_loop(0, 12, skip, 0)

    def decode(i, _):
        acc = jnp.zeros((288, 192), F32)
        for a in range(3):
            acc += dot(s_lift[pl.ds(2 * i + a, 2)].reshape(288, 384), w4l[a])
            acc += dot(s_skip[pl.ds(2 * i + a, 2)].reshape(288, 192), w4e[a])
        pre = fold64(acc).reshape(2, 18, 8, 64)
        for k in range(2):
            x = 2 * i + k
            mask = mm[jnp.where(x < 1, 0, jnp.where(x < 9, 1, 2)), 7:25]
            act, slope = silu_parts(pre[k])
            g = bround(cc[x] * mask * slope)
            gd[x] = g
            s4[x] = taps_y(g, 16)

            @pl.when(jnp.logical_and(x >= 1, x < 9))
            def _():
                decoded[x - 1] = (act * mask)[1:17].reshape(128, 64).astype(BF16)
                zero = jnp.zeros((1, 8, 64), F32)
                gz[x - 1] = taps_z(jnp.concatenate([zero, g[1:17], zero], axis=0))

        return 0

    lax.fori_loop(0, 5, decode, 0)

    def back(i, _):
        acc = jnp.zeros((256, 576), F32)
        for a in range(3):
            acc += dot(s4[pl.ds(2 * i + a, 2)].reshape(256, 192), w5[a])
        g_skip[pl.ds(2 * i, 2)] = fold64(acc[:, 384:]).reshape(2, 128, 64)
        up = acc[:, :384].reshape(2, 8, 2, 8, 384)
        up = up[0] + up[1]
        up = fold128((up[:, 0] + up[:, 1]).reshape(64, 384))
        g = halve_z(up) * slope_dc[i]
        g_dc[i] = g.reshape(64, 128).astype(BF16)
        return 0

    lax.fori_loop(0, 4, back, 0)


def wire64(res, rows):
    out = res.reshape(3, rows, 192)
    tail = out[..., 128:]
    return out[..., :128].astype(BF16), jnp.concatenate([tail[:, : rows // 2], tail[:, rows // 2 :]], axis=2).astype(BF16)


def weights_decode(sc, s_lift, s_skip, gz, s_ec, g_dc, wd1, wd2, wc):
    grad = gz[...].reshape(1152, 192)
    gc = taps_z(g_dc[...].astype(F32).reshape(32, 8, 128))
    for a in range(3):
        up = (dot_t(s_lift[a + 1 : a + 9].reshape(1152, 384), grad) * FACTOR).reshape(3, 128, 192)
        same = (dot_t(s_skip[a + 1 : a + 9].reshape(1152, 192), grad) * FACTOR).reshape(3, 64, 192)
        both = jnp.concatenate([up, same], axis=1).reshape(576, 192)
        wd1[3 * a : 3 * a + 3], wd2[3 * a : 3 * a + 3] = wire64(both, 192)
        res = dot_t(s_ec[a : a + 4].reshape(256, 384), gc) * FACTOR
        for b in range(3):
            for c in range(3):
                wc[9 * a + 3 * b + c] = res[128 * b : 128 * b + 128, 128 * c : 128 * c + 128].astype(BF16)


def back_encode(sc, gx, slope_ec, s_pool, s_in, g_skip, slope_ef, w6, w7, we1, we2, wec, s5, ge, gz):
    def spread(x, _):
        s5[x] = taps_y(gx[x].astype(F32).reshape(12, 8, 128), 10)
        return 0

    lax.fori_loop(0, 8, spread, 0)
    acc = jnp.zeros((480, 384), F32)
    for a in range(3):
        acc += dot(s5[a : a + 6].reshape(480, 384), w6[a])
    g_ec = bround(fold128(acc) * slope_ec[...].reshape(60, 8, 128)).reshape(6, 10, 8, 128)
    for x in range(6):
        ge[x] = taps_y(g_ec[x], 8)
    gc = taps_z(g_ec[1:5, 1:9].reshape(32, 8, 128))
    acc = jnp.zeros((256, 192), F32)
    for a in range(3):
        acc += dot(ge[a : a + 4].reshape(256, 384), w7[a])
    up = double_z(fold64(acc) * 0.125)
    up = jnp.concatenate([up[:, None], up[:, None]], axis=1).reshape(4, 16, 8, 64)
    for x in range(8):
        g = (g_skip[x].reshape(16, 8, 64) + up[x // 2]) * slope_ef[x].reshape(16, 8, 64)
        gz[x] = taps_z(bround(g))
    gf = gz[...].reshape(1024, 192)
    for a in range(3):
        res = dot_t(s_in[a : a + 8].reshape(1024, 192), gf) * FACTOR
        we1[3 * a : 3 * a + 3], we2[3 * a : 3 * a + 3] = wire64(res, 64)
        res = dot_t(s_pool[a : a + 4].reshape(256, 192), gc) * FACTOR
        for b in range(3):
            for c in range(3):
                wec[9 * a + 3 * b + c] = res[64 * b : 64 * b + 64, 128 * c : 128 * c + 128].astype(BF16)


def unpack(sc, wd1, wd2, wc, we1, we2, wec, d_df, d_dc, d_ef, d_ec):
    for first, second, out, rows in ((wd1, wd2, d_df, 192), (we1, we2, d_ef, 64)):
        for k in range(9):
            both = first[k].astype(F32)
            tail = second[k].astype(F32)
            out[3 * k] = both[:, :64]
            out[3 * k + 1] = both[:, 64:]
            out[3 * k + 2] = jnp.concatenate([tail[:, :64], tail[:, 64:]], axis=0)
    d_dc[...] = wc[...].astype(F32)
    d_ec[...] = wec[...].astype(F32)


def side(v, order):
    return jnp.concatenate([v[..., c, :] for c in order], axis=-1)


def forward_weight(kernel, order):
    t = jnp.transpose(kernel, (0, 1, 3, 2, 4))
    return side(t, order)


def backward_weight(kernel, order):
    t = jnp.transpose(kernel[::-1, ::-1, ::-1], (0, 1, 4, 2, 3))
    return side(t, order)


def swap(v, pairs):
    return lax.ppermute(v, ("row", "colh", "core"), pairs)


def body(
    features, block_active, encode_fine, encode_coarse, decode_coarse, decode_fine, out_cotangent
):
    row = lax.axis_index("row")
    core = lax.axis_index("core")
    col = 2 * lax.axis_index("colh") + core
    at = [(r, c) for r in range(8) for c in range(16)]

    def up(i, n):
        return (i + 1) % n if i % 2 else (i - 1) % n

    swap_z = [(16 * r + c, 16 * (r ^ 1) + c) for r, c in at]
    swap_xz = [(16 * r + c, 16 * up(r, 8) + c) for r, c in at]
    swap_core = [(16 * r + c, 16 * r + (c ^ 1)) for r, c in at]
    swap_yz = [(16 * r + c, 16 * r + up(c, 16)) for r, c in at]

    odd_r, odd_c = row % 2, core
    sc = jnp.stack(
        [odd_r, row > 0, row < 7, odd_c, col > 0, col < 15, block_active[0, 0, 0], block_active[0, 1, 0]]
    ).astype(jnp.int32)

    order = (0, 2, 1)
    natural = (0, 1, 2)
    w1 = forward_weight(encode_fine, order).reshape(3, 192, 192)
    w2 = forward_weight(encode_coarse, natural).reshape(3, 192, 384)
    w3 = forward_weight(decode_coarse, natural).reshape(3, 384, 384)
    w4l = forward_weight(decode_fine[..., :128, :], order).reshape(3, 384, 192)
    w4e = forward_weight(decode_fine[..., 128:, :], order).reshape(3, 192, 192)
    w5 = jnp.concatenate(
        [backward_weight(decode_fine[..., :128, :], natural), backward_weight(decode_fine[..., 128:, :], order)],
        axis=-1,
    ).reshape(3, 192, 576)
    w6 = backward_weight(decode_coarse, natural).reshape(3, 384, 384)
    w7 = backward_weight(encode_coarse, order).reshape(3, 384, 192)

    feat = features.reshape(8, 128, 64)
    cot = out_cotangent.reshape(8, 128, 64)
    p1, p2 = call(pack_x, [((9, 128, 64), BF16)] * 2, n_in=3)(sc, feat, cot)
    rz, rxz = swap(p1, swap_z), swap(p2, swap_xz)
    xall, p3, p4 = call(
        pack_y, [((35, 128, 64), BF16), ((24, 64, 64), BF16), ((24, 64, 64), BF16)], n_in=5
    )(sc, feat, cot, rz, rxz)
    r3, r4 = swap(p3, swap_core), swap(p4, swap_yz)

    decoded, slope_ef, g_skip, slope_ec, g_dc, s_in, s_pool, s_ec, s_lift, s_skip, gz = call(
        forward,
        [
            ((8, 128, 64), BF16),
            ((8, 128, 64), F32),
            ((8, 128, 64), F32),
            ((6, 80, 128), F32),
            ((4, 64, 128), BF16),
            ((10, 128, 192), BF16),
            ((6, 64, 192), BF16),
            ((6, 64, 384), BF16),
            ((12, 144, 384), BF16),
            ((12, 144, 192), BF16),
            ((8, 144, 192), BF16),
        ],
        scratch=[
            pltpu.VMEM((22, 32, 8, 64), F32),
            pltpu.VMEM((3, 32, 8, 64), F32),
            pltpu.VMEM((10, 18, 8, 64), F32),
            pltpu.VMEM((22, 256, 192), BF16),
            pltpu.VMEM((20, 32, 8, 64), F32),
            pltpu.VMEM((10, 16, 8, 64), F32),
            pltpu.VMEM((10, 128, 192), BF16),
            pltpu.VMEM((8, 16, 8, 128), F32),
            pltpu.VMEM((8, 128, 384), BF16),
            pltpu.VMEM((4, 8, 8, 128), F32),
            pltpu.VMEM((10, 18, 8, 64), F32),
            pltpu.VMEM((10, 128, 192), BF16),
        ],
        n_in=10,
        flops=4_000_000_000,
    )(sc, xall, r3, r4, w1, w2, w3, w4l, w4e, w5)

    is_odd = odd_r == 1
    q1 = swap(jnp.where(is_odd, g_dc[:2], g_dc[2:]), swap_z)
    q2 = swap(jnp.where(is_odd, g_dc[2:], g_dc[:2]), swap_xz)
    zero = jnp.zeros_like(q1)
    before = jnp.where(row > 0, jnp.where(is_odd, q1, q2), zero)
    after = jnp.where(row < 7, jnp.where(is_odd, q2, q1), zero)
    gx = jnp.concatenate([before, g_dc, after], axis=0)
    is_odd = odd_c == 1
    q3 = swap(jnp.where(is_odd, gx[:, :16], gx[:, 48:]), swap_core)
    q4 = swap(jnp.where(is_odd, gx[:, 48:], gx[:, :16]), swap_yz)
    zero = jnp.zeros_like(q3)
    before = jnp.where(col > 0, jnp.where(is_odd, q3, q4), zero)
    after = jnp.where(col < 15, jnp.where(is_odd, q4, q3), zero)
    gx = jnp.concatenate([before, gx, after], axis=1)

    wd1, wd2, wc = call(
        weights_decode,
        [((9, 192, 128), BF16), ((9, 96, 128), BF16), ((27, 128, 128), BF16)],
        n_in=6,
        flops=1_000_000_000,
    )(sc, s_lift, s_skip, gz, s_ec, g_dc)

    we1, we2, wec = call(
        back_encode,
        [((9, 64, 128), BF16), ((9, 32, 128), BF16), ((27, 64, 128), BF16)],
        scratch=[
            pltpu.VMEM((8, 80, 384), BF16),
            pltpu.VMEM((6, 64, 384), BF16),
            pltpu.VMEM((8, 128, 192), BF16),
        ],
        n_in=9,
        flops=500_000_000,
    )(sc, gx, slope_ec, s_pool, s_in, g_skip, slope_ef, w6, w7)

    parts = [wd1, wd2, wc, we1, we2, wec]
    flat = jnp.concatenate([p.reshape(-1, 128) for p in parts], axis=0)
    flat = jnp.pad(flat, ((0, 128 * CHUNK - flat.shape[0]), (0, 0))).reshape(2, 64, CHUNK, 128)
    mine = lax.dynamic_index_in_dim(flat, core, 0, keepdims=False)
    other = lax.dynamic_index_in_dim(flat, 1 - core, 0, keepdims=False)
    mine = (mine.astype(F32) + swap(other, swap_core).astype(F32)).astype(BF16)
    terms = lax.all_to_all(mine, ("row", "colh"), 0, 0, tiled=True)
    total = jnp.sum(terms.astype(F32), axis=0).astype(BF16)
    mine = lax.all_to_all(jnp.broadcast_to(total[None], terms.shape), ("row", "colh"), 0, 0, tiled=True)
    other = swap(mine, swap_core)
    first = jnp.where(core == 0, mine, other)
    second = jnp.where(core == 0, other, mine)
    flat = jnp.concatenate([first.reshape(-1, 128), second.reshape(-1, 128)], axis=0)
    pieces, start = [], 0
    for p in parts:
        rows = p.size // 128
        pieces.append(flat[start : start + rows].reshape(p.shape))
        start += rows
    d_df, d_dc, d_ef, d_ec = call(
        unpack,
        [((27, 192, 64), F32), ((27, 128, 128), F32), ((27, 64, 64), F32), ((27, 64, 128), F32)],
        n_in=7,
    )(sc, *pieces)
    return (
        decoded.reshape(8, 16, 8, 64),
        d_ef.reshape(3, 3, 3, 64, 64),
        d_ec.reshape(3, 3, 3, 64, 128),
        d_dc.reshape(3, 3, 3, 128, 128),
        d_df.reshape(3, 3, 3, 192, 64),
    )


def solution(mesh):
    split = Mesh(mesh.devices.reshape(8, 8, 2), ("row", "colh", "core"))
    field = P("row", ("colh", "core"), None, None)
    return jax.shard_map(
        body,
        mesh=split,
        in_specs=(field, P("row", ("colh", "core"), None), P(), P(), P(), P(), field),
        out_specs=(field, P(), P(), P(), P()),
        check_vma=False,
    )
```

```python
import functools
import math

import jax
import jax.numpy as jnp
from jax import lax
from jax.experimental import pallas as pl
from jax.experimental.pallas import tpu as pltpu
from jax.sharding import Mesh, PartitionSpec as P

F32 = jnp.float32
BF16 = jnp.bfloat16
VMEM_LIMIT = 50 * 1024 * 1024
VM = pl.BlockSpec(memory_space=pltpu.VMEM)
SM = pl.BlockSpec(memory_space=pltpu.SMEM)
FACTOR = 1.0 / math.sqrt(64 * 256 * 8)
CHUNK = 72
ROWS_A, ROWS_B = 6144, 3072


def call(kernel, outs, scratch=(), flops=0, n_scalar=0, n_in=0):
    return pl.pallas_call(
        kernel,
        out_shape=[jax.ShapeDtypeStruct(s, d) for s, d in outs],
        in_specs=[SM] * n_scalar + [VM] * (n_in - n_scalar),
        out_specs=[VM] * len(outs),
        scratch_shapes=list(scratch),
        compiler_params=pltpu.CompilerParams(vmem_limit_bytes=VMEM_LIMIT),
        cost_estimate=pl.CostEstimate(flops=flops, bytes_accessed=4_000_000, transcendentals=0),
    )


def dot(lhs, rhs):
    return jnp.dot(lhs, rhs, preferred_element_type=F32)


def dot_n(lhs, rhs):
    return lax.dot_general(lhs, rhs, (((1,), (1,)), ((), ())), preferred_element_type=F32)


def dot_t(lhs, rhs):
    return lax.dot_general(lhs, rhs, (((0,), (0,)), ((), ())), preferred_element_type=F32)


def bround(v):
    return v.astype(BF16).astype(F32)


def z_of(shape):
    return lax.broadcasted_iota(jnp.int32, shape, len(shape) - 2)


def z_later(v):
    return jnp.where(z_of(v.shape) > 0, pltpu.roll(v, 1, 1), 0.0)


def z_earlier(v):
    return jnp.where(z_of(v.shape) < 7, pltpu.roll(v, 7, 1), 0.0)


def fold128(acc):
    rows = acc.shape[0]
    cube = acc.reshape(rows // 8, 8, 384)
    return z_later(cube[..., :128]) + cube[..., 128:256] + z_earlier(cube[..., 256:])


def taps_y(v, count):
    depth = v.shape[2]
    wide = jnp.concatenate([v[b : b + count] for b in range(3)], axis=2)
    return wide.reshape(count * 8, 3 * depth).astype(BF16)


def taps_z(g):
    wide = jnp.concatenate([z_earlier(g), g, z_later(g)], axis=2)
    return wide.reshape(g.shape[0] * 8, 3 * g.shape[2]).astype(BF16)


def halve_z(s):
    pair = s + pltpu.roll(s, 7, 1)
    z = z_of(s.shape)
    out = jnp.where(z == 0, pair, 0.0)
    for zc in (1, 2, 3):
        out = jnp.where(z == zc, pltpu.roll(pair, 8 - zc, 1), out)
    return out


def double_z(u):
    z = z_of(u.shape)
    out = u
    for shift in (1, 2, 3, 4):
        out = jnp.where((z + 1) // 2 == shift, pltpu.roll(u, shift, 1), out)
    return out


def silu_parts(v):
    sigma = jax.nn.sigmoid(v)
    act = v * sigma
    return act, sigma + act * (1.0 - sigma)


def place(axis):
    at = lax.axis_index("row") if axis == 0 else 2 * lax.axis_index("colh") + lax.axis_index("core")
    last = 7 if axis == 0 else 15
    return at % 2 == 1, (at > 0).astype(F32), (at < last).astype(F32)


def beside(first, second):
    return jnp.concatenate([first.astype(F32), second.astype(F32)], axis=1)


def pack_x(active, feat, cot, p1, p2):
    row = lax.broadcasted_iota(jnp.int32, (128, 64), 0)
    mask = jnp.where(row < 64, active[0], active[1]).astype(F32)
    row = lax.broadcasted_iota(jnp.int32, (16, 128), 0)
    ends = jnp.where(row < 8, active[0], active[1]).astype(F32).astype(BF16)
    odd, _, _ = place(0)
    for k in range(3):
        pair = beside(feat[2 * k + 1].astype(F32) * mask, feat[2 * k + 2].astype(F32) * mask).astype(BF16)
        p1[128 * k : 128 * k + 128] = pair
        p2[128 * k : 128 * k + 128] = pair
    for p, edge in ((p1, jnp.where(odd, 0, 7)), (p2, jnp.where(odd, 7, 0))):
        p[384:512] = beside(feat[edge].astype(F32) * mask, cot[edge]).astype(BF16)
        p[512:528] = ends


def pack_y(active, feat, cot, rz, rxz, xall, xmask, p3, p4):
    row = lax.broadcasted_iota(jnp.int32, (128, 64), 0)
    mask = jnp.where(row < 64, active[0], active[1]).astype(F32)
    row = lax.broadcasted_iota(jnp.int32, (16, 128), 0)
    odd, v_lo, v_hi = place(0)

    def lo(rows):
        return jnp.where(odd, rz[rows].astype(F32), rxz[rows].astype(F32)) * v_lo

    def hi(rows):
        return jnp.where(odd, rxz[rows].astype(F32), rz[rows].astype(F32)) * v_hi

    def own(k):
        return feat[k].astype(F32) * mask

    for k in range(3):
        slab = slice(128 * k, 128 * k + 128)
        xall[k] = lo(slab).astype(BF16)
        xall[4 + k] = beside(own(2 * k + 1), own(2 * k + 2)).astype(BF16)
        xall[8 + k] = hi(slab).astype(BF16)
        xall[12 + k] = beside(cot[2 * k + 1], cot[2 * k + 2]).astype(BF16)
    edge_lo, edge_hi = lo(slice(384, 512)), hi(slice(384, 512))
    xall[3] = beside(edge_lo[:, :64], own(0)).astype(BF16)
    xall[7] = beside(own(7), edge_hi[:, :64]).astype(BF16)
    xall[11] = beside(edge_lo[:, 64:], cot[0]).astype(BF16)
    xall[15] = beside(cot[7], edge_hi[:, 64:]).astype(BF16)
    xmask[0] = lo(slice(512, 528))
    xmask[1] = jnp.where(row < 8, active[0], active[1]).astype(F32)
    xmask[2] = hi(slice(512, 528))
    odd_c, _, _ = place(1)
    for p, low in ((p3, odd_c), (p4, jnp.logical_not(odd_c))):
        for k in range(11):
            near = jnp.where(low, xall[k, 0:64].astype(F32), xall[k, 64:128].astype(F32))
            p[64 * k : 64 * k + 64] = near.astype(BF16)
        cols = []
        for k in range(11, 16):
            slab = xall[k].astype(F32)
            cols.append(jnp.where(low, slab[0:8], slab[120:128]))
        for k in range(3):
            cols.append(jnp.where(low, xmask[k, 0:8], xmask[k, 8:16]))
        p[704:768] = jnp.concatenate(cols, axis=0).astype(BF16)


def forward(
    xall, xmask, r3, r4, w1, w2, w3, w4l, w4e, w5l, w5s,
    decoded, slope_ef, g_skip, slope_ec, g_dc, s_in, s_pool, s_ec, s_lift, s_skip, gz,
    mm, cc, s1, ee, s2, s3, slope_dc, s4, acc,
):
    odd, v_lo, v_hi = place(1)

    def lo(at, rows):
        at = pl.ds(at, rows)
        return (jnp.where(odd, r3[at].astype(F32), r4[at].astype(F32)) * v_lo).reshape(rows // 8, 8, 128)

    def hi(at, rows):
        at = pl.ds(at, rows)
        return (jnp.where(odd, r4[at].astype(F32), r3[at].astype(F32)) * v_hi).reshape(rows // 8, 8, 128)

    extra_lo, extra_hi = lo(704, 64), hi(704, 64)
    for k in range(5):
        cc[k, 0] = extra_lo[k]
        cc[k, 1:17] = xall[11 + k].astype(F32).reshape(16, 8, 128)
        cc[k, 17] = extra_hi[k]
    for k in range(3):
        mm[k, 0:6] = jnp.broadcast_to(extra_lo[5 + k][None], (6, 8, 128))
        mm[k, 6:14] = jnp.broadcast_to(xmask[k, 0:8][None], (8, 8, 128))
        mm[k, 14:22] = jnp.broadcast_to(xmask[k, 8:16][None], (8, 8, 128))
        mm[k, 22:28] = jnp.broadcast_to(extra_hi[5 + k][None], (6, 8, 128))

    def spread(i, _):
        at = pl.multiple_of(64 * i, 64)
        v = jnp.concatenate([lo(at, 64), xall[i].astype(F32).reshape(16, 8, 128), hi(at, 64)], axis=0)
        s1[i] = taps_y(v[1:31], 28)

        @pl.when(jnp.logical_and(i >= 3, i < 8))
        def _():
            s_in[i - 3] = taps_y(v[7:25], 16)

        return 0

    lax.fori_loop(0, 11, spread, 0)

    def encode(i, _):
        pre = fold128(dot(jnp.concatenate([s1[i], s1[i + 1]], axis=1), w1[...]))
        mask = mm[jnp.where(i < 3, 0, jnp.where(i < 7, 1, 2))]
        act, slope = silu_parts(pre)
        v = bround(act * mask)
        ee[i] = v

        @pl.when(jnp.logical_and(i >= 3, i < 7))
        def _():
            slope_ef[i - 3] = (slope * mask)[6:22].reshape(128, 128)

        s = v.reshape(14, 2, 8, 128)
        s = s[:, 0] + s[:, 1]
        s = s[..., :64] + s[..., 64:]
        v = bround(halve_z(s) * 0.125)
        s2[i] = taps_y(v, 12)

        @pl.when(jnp.logical_and(i >= 2, i < 8))
        def _():
            s_pool[i - 2] = taps_y(v[2:12], 8)

        return 0

    lax.fori_loop(0, 10, encode, 0)

    def mask_coarse(block, first, count):
        m = mm[block].reshape(14, 2, 8, 128)[first : first + count, 0]
        return jnp.where(z_of(m.shape) < 4, m, 0.0)

    def encode2(i, _):
        pre = jnp.zeros((384, 384), F32)
        for a in range(3):
            pre += dot(s2[pl.ds(4 * i + a, 4)].reshape(384, 192), w2[a])
        pre = fold128(pre).reshape(4, 12, 8, 128)
        for k in range(4):
            x = 4 * i + k
            mask = mask_coarse(jnp.where(x < 2, 0, jnp.where(x < 6, 1, 2)), 1, 12)
            act, slope = silu_parts(pre[k])
            v = bround(act * mask)
            s3[x] = taps_y(v, 10)

            @pl.when(jnp.logical_and(x >= 1, x < 7))
            def _():
                slope_ec[x - 1] = (slope * mask)[1:11].reshape(80, 128)
                s_ec[x - 1] = taps_y(v[1:11], 8)

        return 0

    lax.fori_loop(0, 2, encode2, 0)

    def decode2(i, _):
        pre = jnp.zeros((240, 384), F32)
        for a in range(3):
            pre += dot(s3[pl.ds(3 * i + a, 3)].reshape(240, 384), w3[a])
        pre = fold128(pre).reshape(3, 10, 8, 128)
        for k in range(3):
            x = 3 * i + k
            mask = mask_coarse(jnp.where(x < 1, 0, jnp.where(x < 5, 1, 2)), 2, 10)
            act, slope = silu_parts(pre[k])
            v = double_z(bround(act * mask))
            up = jnp.concatenate([v[:, None], v[:, None]], axis=1).reshape(20, 8, 128)
            s_lift[x] = taps_y(up, 18)

            @pl.when(jnp.logical_and(x >= 1, x < 5))
            def _():
                slope_dc[x - 1] = (slope * mask)[1:9]

        return 0

    lax.fori_loop(0, 2, decode2, 0)

    def skip(i, _):
        s_skip[i] = taps_y(ee[i + 2, 4:24], 18)
        return 0

    lax.fori_loop(0, 6, skip, 0)

    first, second = s_lift[0:5].reshape(720, 384), s_lift[1:6].reshape(720, 384)
    acc[...] = dot_n(first, w4l[0]) + dot_n(first, w4l[1]) + dot_n(second, w4l[2]) + dot_n(second, w4l[3])
    acc[...] += dot_n(s_skip[0:5].reshape(720, 384), w4e[0]) + dot_n(s_skip[1:6].reshape(720, 384), w4e[1])

    def decode(i, _):
        pre = fold128(acc[pl.ds(pl.multiple_of(144 * i, 144), 144)])
        lane = lax.broadcasted_iota(jnp.int32, (18, 8, 128), 2)
        before, after = jnp.where(i < 1, 0, 1), jnp.where(i < 4, 1, 2)
        mask = jnp.where(lane < 64, mm[before, 5:23], mm[after, 5:23])
        act, slope = silu_parts(pre)
        g = bround(cc[i] * mask * slope)
        s4[i] = taps_y(g, 16)
        out = (act * mask)[1:17].reshape(128, 128).astype(BF16)

        @pl.when(i > 0)
        def _():
            decoded[2 * i - 1] = out[:, :64]

        @pl.when(i < 4)
        def _():
            decoded[2 * i] = out[:, 64:]

        own = jnp.logical_and(jnp.logical_or(lane >= 64, i > 0), jnp.logical_or(lane < 64, i < 4))
        g = jnp.where(own, g, 0.0)
        zero = jnp.zeros((1, 8, 128), F32)
        gz[i] = taps_z(jnp.concatenate([zero, g[1:17], zero], axis=0))
        return 0

    lax.fori_loop(0, 5, decode, 0)

    def back(i, _):
        wide = jnp.concatenate([s4[pl.ds(2 * i, 2)], s4[pl.ds(2 * i + 1, 2)]], axis=2).reshape(256, 768)
        g_skip[pl.ds(2 * i, 2)] = fold128(dot(wide, w5s[...])).reshape(2, 128, 128)
        up = (dot(wide, w5l[0]) + dot(wide, w5l[1])).reshape(16, 2, 8, 384)
        g = halve_z(fold128((up[:, 0] + up[:, 1]).reshape(128, 384)))
        g = g.reshape(2, 8, 8, 128) * slope_dc[pl.ds(2 * i, 2)]
        g_dc[pl.ds(2 * i, 2)] = g.reshape(2, 64, 128).astype(BF16)
        return 0

    lax.fori_loop(0, 2, back, 0)


def unhalve(both):
    return jnp.concatenate([both[:, :64], both[:, 64:]], axis=0)


def split_wire(wire, keep, send):
    rows = wire.shape[0] // 2
    core = lax.axis_index("core")
    keep[...] = wire[pl.ds(pl.multiple_of(core * rows, rows), rows)]
    send[...] = wire[pl.ds(pl.multiple_of((1 - core) * rows, rows), rows)]


A_SKIP, A_SKIP2, A_COARSE, A_END = 1728, 2304, 2592, 6048
B_FINE2, B_COARSE, B_END = 576, 864, 2592


def weights_decode(s_lift, s_skip, gz, s_ec, g_dc, keep, send, wire):
    grad = gz[...].reshape(720, 384)
    gc = taps_z(g_dc[...].astype(F32).reshape(32, 8, 128))
    wire[A_END:] = jnp.zeros((wire.shape[0] - A_END, 128), BF16)
    up = [(dot_t(grad, s_lift[p : p + 5].reshape(720, 384)) * FACTOR).reshape(3, 2, 64, 384) for p in range(2)]
    same = [(dot_t(grad, s_skip[p : p + 5].reshape(720, 384)) * FACTOR).reshape(3, 2, 64, 384) for p in range(2)]
    for a, (p, q) in enumerate(((0, 0), (0, 1), (1, 0))):
        p2, q2 = (0, 1) if a == 0 else (1, a - 1)
        lifted = (up[p][:, 0] + up[p2][:, 1]).reshape(192, 384).astype(BF16)
        for b in range(3):
            at = 64 * (9 * a + 3 * b)
            wire[at : at + 192] = lifted[:, 128 * b : 128 * b + 128]
        taps = []
        for b in range(3):
            lanes = slice(128 * b, 128 * b + 128)
            taps.append(add_halves(same[p][:, 0, :, lanes].reshape(192, 128), q, same[p2][:, 1, :, lanes].reshape(192, 128), q2))
        put_three(wire, A_SKIP + 192 * a, A_SKIP2 + 96 * a, taps)
        res = (dot_t(s_ec[a : a + 4].reshape(256, 384), gc) * FACTOR).astype(BF16)
        for b in range(3):
            for c in range(3):
                at = A_COARSE + 128 * (9 * a + 3 * b + c)
                wire[at : at + 128] = res[128 * b : 128 * b + 128, 128 * c : 128 * c + 128]
    split_wire(wire, keep, send)


def add_halves(first, q, second, q2):
    low = (first if q == 0 else pltpu.roll(first, 64, 1)) + (second if q2 == 0 else pltpu.roll(second, 64, 1))
    high = (first if q == 1 else pltpu.roll(first, 64, 1)) + (second if q2 == 1 else pltpu.roll(second, 64, 1))
    return low, high


def put_three(wire, at, at2, taps):
    lane = lax.broadcasted_iota(jnp.int32, (192, 128), 1)
    wire[at : at + 192] = jnp.where(lane < 64, taps[0][0], taps[1][1]).astype(BF16)
    wire[at2 : at2 + 96] = jnp.where(lane[:96] < 64, taps[2][0][:96], taps[2][1][96:]).astype(BF16)


def back_encode(gx, slope_ec, s_pool, s_in, g_skip, slope_ef, w6, w7, keep, send, s5, ge, gz, wire):
    def spread(x, _):
        s5[x] = taps_y(gx[x].astype(F32).reshape(12, 8, 128), 10)
        return 0

    lax.fori_loop(0, 8, spread, 0)
    acc = jnp.zeros((480, 384), F32)
    for a in range(3):
        acc += dot_n(s5[a : a + 6].reshape(480, 384), w6[a])
    g_ec = bround(fold128(acc) * slope_ec[...].reshape(60, 8, 128)).reshape(6, 10, 8, 128)
    for x in range(6):
        ge[x] = taps_y(g_ec[x], 8)
    gc = taps_z(g_ec[1:5, 1:9].reshape(32, 8, 128))
    acc = jnp.zeros((256, 384), F32)
    for a in range(3):
        acc += dot_n(ge[a : a + 4].reshape(256, 384), w7[a])
    up = double_z(fold128(acc) * 0.125)
    up = jnp.concatenate([up[:, None], up[:, None]], axis=1).reshape(4, 16, 8, 128)
    for x in range(4):
        g = (g_skip[x].reshape(16, 8, 128) + up[x]) * slope_ef[x].reshape(16, 8, 128)
        gz[x] = taps_z(bround(g))
    gf = gz[...].reshape(512, 384)
    wire[B_END:] = jnp.zeros((wire.shape[0] - B_END, 128), BF16)
    parts = [(dot_t(s_in[p : p + 4].reshape(512, 384), gf) * FACTOR).reshape(3, 2, 64, 384) for p in range(2)]
    for a, (p, q) in enumerate(((0, 0), (0, 1), (1, 0))):
        p2, q2 = (0, 1) if a == 0 else (1, a - 1)
        taps = []
        for c in range(3):
            lanes = slice(128 * c, 128 * c + 128)
            taps.append(add_halves(parts[p][:, q, :, lanes].reshape(192, 128), 0, parts[p2][:, q2, :, lanes].reshape(192, 128), 1))
        put_three(wire, 192 * a, B_FINE2 + 96 * a, taps)
        res = (dot_t(s_pool[a : a + 4].reshape(256, 192), gc) * FACTOR).astype(BF16)
        for b in range(3):
            for c in range(3):
                at = B_COARSE + 64 * (9 * a + 3 * b + c)
                wire[at : at + 64] = res[64 * b : 64 * b + 64, 128 * c : 128 * c + 128]
    split_wire(wire, keep, send)


def unpack(mine, other, d_df, d_dc, d_ef, d_ec, wire_a, wire_b):
    core = lax.axis_index("core")
    for wire, first in ((wire_a, 0), (wire_b, ROWS_A // 128)):
        rows = wire.shape[0] // 2
        each = rows // 64
        here = pl.ds(pl.multiple_of(core * rows, rows), rows)
        there = pl.ds(pl.multiple_of((1 - core) * rows, rows), rows)
        wire[here] = mine[:, first : first + each].reshape(rows, 128)
        wire[there] = other[:, first : first + each].reshape(rows, 128)
    d_dc[...] = wire_a[A_COARSE:A_END].astype(F32).reshape(27, 128, 128)
    d_ec[...] = wire_b[B_COARSE:B_END].astype(F32).reshape(27, 64, 128)
    for a in range(3):
        two = wire_a[A_SKIP + 192 * a : A_SKIP + 192 * a + 192].astype(F32)
        three = unhalve(wire_a[A_SKIP2 + 96 * a : A_SKIP2 + 96 * a + 96].astype(F32))
        skip = (two[:, :64], two[:, 64:], three)
        two = wire_b[192 * a : 192 * a + 192].astype(F32)
        three = unhalve(wire_b[B_FINE2 + 96 * a : B_FINE2 + 96 * a + 96].astype(F32))
        fine = (two[:, :64], two[:, 64:], three)
        for b in range(3):
            for c in range(3):
                k = 9 * a + 3 * b + c
                d_df[k, :, :128] = wire_a[64 * k : 64 * k + 64].astype(F32)
                d_df[k, :, 128:] = skip[b][64 * c : 64 * c + 64]
                d_ef[k] = fine[c][64 * b : 64 * b + 64]


def arrange(e1, e2, d3, d4, w1, w2, w3, w4l, w4e, w5l, w5s, w6, w7):
    for a in range(3):
        for b in range(3):
            fine, coarse = slice(64 * b, 64 * b + 64), slice(128 * b, 128 * b + 128)
            for c in range(3):
                k = 9 * a + 3 * b + c
                lanes = slice(128 * c, 128 * c + 128)
                w2[a, fine, lanes] = e2[k]
                w3[a, coarse, lanes] = d3[k]
                w6[a, lanes, coarse] = d3[26 - k]
                w7[a, 128 * c : 128 * c + 64, coarse] = e2[26 - k]
                w7[a, 128 * c + 64 : 128 * c + 128, coarse] = e2[26 - k]
    none = jnp.zeros((64, 64), F32)

    def tap(ref, a, rest, lanes, turned=False):
        if a < 0 or a > 2:
            return none
        k = 9 * a + rest
        return ref[26 - k if turned else k, :, lanes].astype(F32)

    all_, low, high = slice(0, 64), slice(0, 128), slice(128, 192)
    for p in range(2):
        for b in range(3):
            for c in range(3):
                rest = 3 * b + c
                lanes = slice(128 * c, 128 * c + 128)
                for q in range(2):
                    rows = slice(384 * p + 128 * b + 64 * q, 384 * p + 128 * b + 64 * q + 64)
                    a = 2 * p + q
                    w1[rows, lanes] = beside(tap(e1, a, rest, all_), tap(e1, a - 1, rest, all_)).astype(BF16)
                    w5s[rows, lanes] = beside(
                        tap(d4, a, rest, high, True), tap(d4, a - 1, rest, high, True)
                    ).astype(BF16)
                    for o in range(2):
                        cols = slice(128 * c + 64 * o, 128 * c + 64 * o + 64)
                        coarse = slice(128 * b, 128 * b + 128)
                        if 0 <= a - o <= 2:
                            w5l[o, rows, lanes] = d4[26 - 9 * (a - o) - rest, :, low]
                            w4l[2 * p + q, cols, coarse] = d4[9 * (a - o) + rest, :, low]
                        else:
                            w5l[o, rows, lanes] = jnp.zeros((64, 128), BF16)
                            w4l[2 * p + q, cols, coarse] = jnp.zeros((64, 128), BF16)
                for o in range(2):
                    cols = slice(128 * c + 64 * o, 128 * c + 64 * o + 64)
                    w4e[p, cols, 128 * b : 128 * b + 128] = beside(
                        tap(d4, 2 * p - o, rest, high), tap(d4, 2 * p + 1 - o, rest, high)
                    ).astype(BF16)


def swap(v, pairs):
    return lax.ppermute(v, ("row", "colh", "core"), pairs)


def body(
    features, block_active, encode_fine, encode_coarse, decode_coarse, decode_fine, out_cotangent
):
    row = lax.axis_index("row")
    core = lax.axis_index("core")
    col = 2 * lax.axis_index("colh") + core
    at = [(r, c) for r in range(8) for c in range(16)]

    def up(i, n):
        return (i + 1) % n if i % 2 else (i - 1) % n

    swap_z = [(16 * r + c, 16 * (r ^ 1) + c) for r, c in at]
    swap_xz = [(16 * r + c, 16 * up(r, 8) + c) for r, c in at]
    swap_core = [(16 * r + c, 16 * r + (c ^ 1)) for r, c in at]
    swap_yz = [(16 * r + c, 16 * r + up(c, 16)) for r, c in at]

    odd_r, odd_c = row % 2, core
    active = block_active.reshape(2)
    w1, w2, w3, w4l, w4e, w5l, w5s, w6, w7 = call(
        arrange,
        [
            ((768, 384), BF16),
            ((3, 192, 384), BF16),
            ((3, 384, 384), BF16),
            ((4, 384, 384), BF16),
            ((2, 384, 384), BF16),
            ((2, 768, 384), BF16),
            ((768, 384), BF16),
            ((3, 384, 384), BF16),
            ((3, 384, 384), BF16),
        ],
        n_in=4,
    )(
        encode_fine.reshape(27, 64, 64),
        encode_coarse.reshape(27, 64, 128),
        decode_coarse.reshape(27, 128, 128),
        jnp.transpose(decode_fine, (0, 1, 2, 4, 3)).reshape(27, 64, 192),
    )

    feat = features.reshape(8, 128, 64)
    cot = out_cotangent.reshape(8, 128, 64)
    p1, p2 = call(pack_x, [((528, 128), BF16)] * 2, n_in=3, n_scalar=1)(active, feat, cot)
    rz, rxz = swap(p1, swap_z), swap(p2, swap_xz)
    xall, xmask, p3, p4 = call(
        pack_y,
        [((16, 128, 128), BF16), ((3, 16, 128), F32), ((768, 128), BF16), ((768, 128), BF16)],
        n_in=5,
        n_scalar=1,
    )(active, feat, cot, rz, rxz)
    r3, r4 = swap(p3, swap_core), swap(p4, swap_yz)

    decoded, slope_ef, g_skip, slope_ec, g_dc, s_in, s_pool, s_ec, s_lift, s_skip, gz = call(
        forward,
        [
            ((8, 128, 64), BF16),
            ((4, 128, 128), F32),
            ((4, 128, 128), F32),
            ((6, 80, 128), F32),
            ((4, 64, 128), BF16),
            ((5, 128, 384), BF16),
            ((6, 64, 192), BF16),
            ((6, 64, 384), BF16),
            ((6, 144, 384), BF16),
            ((6, 144, 384), BF16),
            ((5, 144, 384), BF16),
        ],
        scratch=[
            pltpu.VMEM((3, 28, 8, 128), F32),
            pltpu.VMEM((5, 18, 8, 128), F32),
            pltpu.VMEM((11, 224, 384), BF16),
            pltpu.VMEM((10, 28, 8, 128), F32),
            pltpu.VMEM((10, 96, 192), BF16),
            pltpu.VMEM((8, 80, 384), BF16),
            pltpu.VMEM((4, 8, 8, 128), F32),
            pltpu.VMEM((5, 128, 384), BF16),
            pltpu.VMEM((720, 384), F32),
        ],
        n_in=11,
        flops=4_000_000_000,
    )(xall, xmask, r3, r4, w1, w2, w3, w4l, w4e, w5l, w5s)

    is_odd = odd_r == 1
    q1 = swap(jnp.where(is_odd, g_dc[:2], g_dc[2:]), swap_z)
    q2 = swap(jnp.where(is_odd, g_dc[2:], g_dc[:2]), swap_xz)
    zero = jnp.zeros_like(q1)
    before = jnp.where(row > 0, jnp.where(is_odd, q1, q2), zero)
    after = jnp.where(row < 7, jnp.where(is_odd, q2, q1), zero)
    gx = jnp.concatenate([before, g_dc, after], axis=0)
    is_odd = odd_c == 1
    q3 = swap(jnp.where(is_odd, gx[:, :16], gx[:, 48:]), swap_core)
    q4 = swap(jnp.where(is_odd, gx[:, 48:], gx[:, :16]), swap_yz)
    zero = jnp.zeros_like(q3)
    before = jnp.where(col > 0, jnp.where(is_odd, q3, q4), zero)
    after = jnp.where(col < 15, jnp.where(is_odd, q4, q3), zero)
    gx = jnp.concatenate([before, gx, after], axis=1)

    keep_a, send_a = call(
        weights_decode,
        [((ROWS_A // 2, 128), BF16)] * 2,
        scratch=[pltpu.VMEM((ROWS_A, 128), BF16)],
        n_in=5,
        flops=1_000_000_000,
    )(s_lift, s_skip, gz, s_ec, g_dc)
    got_a = swap(send_a, swap_core)

    keep_b, send_b = call(
        back_encode,
        [((ROWS_B // 2, 128), BF16)] * 2,
        scratch=[
            pltpu.VMEM((8, 80, 384), BF16),
            pltpu.VMEM((6, 64, 384), BF16),
            pltpu.VMEM((4, 128, 384), BF16),
            pltpu.VMEM((ROWS_B, 128), BF16),
        ],
        n_in=8,
        flops=500_000_000,
    )(gx, slope_ec, s_pool, s_in, g_skip, slope_ef, w6, w7)
    got_b = swap(send_b, swap_core)

    chips = ("row", "colh")
    half = jnp.concatenate(
        [
            (keep.astype(F32) + got.astype(F32)).astype(BF16).reshape(64, -1, 128)
            for keep, got in ((keep_a, got_a), (keep_b, got_b))
        ],
        axis=1,
    )
    terms = lax.all_to_all(half, chips, 0, 0, tiled=True)
    total = jnp.sum(terms.astype(F32), axis=0).astype(BF16)
    mine = lax.all_to_all(jnp.broadcast_to(total[None], (64, CHUNK, 128)), chips, 0, 0, tiled=True)
    other = swap(mine, swap_core)
    d_df, d_dc, d_ef, d_ec = call(
        unpack,
        [((27, 64, 192), F32), ((27, 128, 128), F32), ((27, 64, 64), F32), ((27, 64, 128), F32)],
        scratch=[pltpu.VMEM((ROWS_A, 128), BF16), pltpu.VMEM((ROWS_B, 128), BF16)],
        n_in=2,
    )(mine, other)
    return (
        decoded.reshape(8, 16, 8, 64),
        d_ef.reshape(3, 3, 3, 64, 64),
        d_ec.reshape(3, 3, 3, 64, 128),
        d_dc.reshape(3, 3, 3, 128, 128),
        jnp.transpose(d_df.reshape(3, 3, 3, 64, 192), (0, 1, 2, 4, 3)),
    )


def solution(mesh):
    split = Mesh(mesh.devices.reshape(8, 8, 2), ("row", "colh", "core"))
    field = P("row", ("colh", "core"), None, None)
    return jax.shard_map(
        body,
        mesh=split,
        in_specs=(field, P("row", ("colh", "core"), None), P(), P(), P(), P(), field),
        out_specs=(field, P(), P(), P(), P()),
        check_vma=False,
    )
```

```python
import functools
import math

import jax
import jax.numpy as jnp
from jax import lax
from jax.experimental import pallas as pl
from jax.experimental.pallas import tpu as pltpu
from jax.sharding import Mesh, PartitionSpec as P

F32 = jnp.float32
BF16 = jnp.bfloat16
MIB = 1024 * 1024
VM = pl.BlockSpec(memory_space=pltpu.VMEM)
HB = pl.BlockSpec(memory_space=pltpu.HBM)
FACTOR = 1.0 / math.sqrt(64 * 256 * 8)
CHUNK = 72
ROWS_A, ROWS_B = 6144, 3072


def call(kernel, outs, ins, scratch=(), flops=0, limit=58):
    return pl.pallas_call(
        kernel,
        out_shape=[jax.ShapeDtypeStruct(o[0], o[1]) for o in outs],
        in_specs=list(ins),
        out_specs=[o[2] if len(o) > 2 else VM for o in outs],
        scratch_shapes=list(scratch),
        compiler_params=pltpu.CompilerParams(vmem_limit_bytes=int(limit * MIB)),
        cost_estimate=pl.CostEstimate(flops=flops, bytes_accessed=4_000_000, transcendentals=0),
    )


def dot(lhs, rhs):
    return jnp.dot(lhs, rhs, preferred_element_type=F32)


def dot_n(lhs, rhs):
    return lax.dot_general(lhs, rhs, (((1,), (1,)), ((), ())), preferred_element_type=F32)


def dot_t(lhs, rhs):
    return lax.dot_general(lhs, rhs, (((0,), (0,)), ((), ())), preferred_element_type=F32)


def bround(v):
    return v.astype(BF16).astype(F32)


def z_of(shape):
    return lax.broadcasted_iota(jnp.int32, shape, len(shape) - 2)


def z_later(v):
    return jnp.where(z_of(v.shape) > 0, pltpu.roll(v, 1, 1), 0.0)


def z_earlier(v):
    return jnp.where(z_of(v.shape) < 7, pltpu.roll(v, 7, 1), 0.0)


def fold128(acc):
    rows = acc.shape[0]
    cube = acc.reshape(rows // 8, 8, 384)
    return z_later(cube[..., :128]) + cube[..., 128:256] + z_earlier(cube[..., 256:])


def taps_y(v, count):
    depth = v.shape[2]
    wide = jnp.concatenate([v[b : b + count] for b in range(3)], axis=2)
    return wide.reshape(count * 8, 3 * depth).astype(BF16)


def taps_z(g):
    wide = jnp.concatenate([z_earlier(g), g, z_later(g)], axis=2)
    return wide.reshape(g.shape[0] * 8, 3 * g.shape[2]).astype(BF16)


def halve_z(s):
    pair = s + pltpu.roll(s, 7, 1)
    z = z_of(s.shape)
    out = jnp.where(z == 0, pair, 0.0)
    for zc in (1, 2, 3):
        out = jnp.where(z == zc, pltpu.roll(pair, 8 - zc, 1), out)
    return out


def double_z(u):
    z = z_of(u.shape)
    out = u
    for shift in (1, 2, 3, 4):
        out = jnp.where((z + 1) // 2 == shift, pltpu.roll(u, shift, 1), out)
    return out


def silu_parts(v):
    sigma = 0.5 * jnp.tanh(0.5 * v) + 0.5
    act = v * sigma
    return act, lambda: sigma + act * (1.0 - sigma)


W1, W2, W3, W4L, W4E, W5L, W5S, WF = 0, 768, 1344, 2496, 4032, 4800, 6336, 7104
W6, W7, WB = 0, 1152, 2304
LIFT, SKIP, GRAD, COARSE, KEPT = 0, 864, 1728, 2448, 2832
ROOM = 51200


def place(axis):
    at = lax.axis_index("row") if axis == 0 else 2 * lax.axis_index("colh") + lax.axis_index("core")
    last = 7 if axis == 0 else 15
    return at % 2 == 1, (at > 0).astype(F32), (at < last).astype(F32)


def beside(first, second):
    return jnp.concatenate([first.astype(F32), second.astype(F32)], axis=1)


def pack_x(active_hbm, feat_hbm, cot_hbm, p1, p2, active, feat, cot, sem):
    odd, _, _ = place(0)
    copies = [pltpu.make_async_copy(active_hbm, active, sem.at[0])]
    copies += [pltpu.make_async_copy(feat_hbm.at[k], feat.at[k], sem.at[1 + k]) for k in range(8)]
    copies += [pltpu.make_async_copy(cot_hbm.at[7 * k], cot.at[k], sem.at[9 + k]) for k in range(2)]
    for copy in copies:
        copy.start()
    for copy in copies:
        copy.wait()
    row = lax.broadcasted_iota(jnp.int32, (128, 64), 0)
    mask = jnp.where(row < 64, active[0], active[1]).astype(F32)
    row = lax.broadcasted_iota(jnp.int32, (16, 128), 0)
    ends = jnp.where(row < 8, active[0], active[1]).astype(F32).astype(BF16)
    for k in range(3):
        pair = beside(feat[2 * k + 1].astype(F32) * mask, feat[2 * k + 2].astype(F32) * mask).astype(BF16)
        p1[128 * k : 128 * k + 128] = pair
        p2[128 * k : 128 * k + 128] = pair
    for p, edge in ((p1, jnp.where(odd, 0, 1)), (p2, jnp.where(odd, 1, 0))):
        p[384:512] = beside(feat[7 * edge].astype(F32) * mask, cot[edge]).astype(BF16)
        p[512:528] = ends


def pack_y(cot, p1, p2, rz, rxz, xall, xmask, p3, p4):
    odd, v_lo, v_hi = place(0)

    def lo(rows):
        return jnp.where(odd, rz[rows].astype(F32), rxz[rows].astype(F32)) * v_lo

    def hi(rows):
        return jnp.where(odd, rxz[rows].astype(F32), rz[rows].astype(F32)) * v_hi

    for k in range(3):
        slab = slice(128 * k, 128 * k + 128)
        xall[k] = lo(slab).astype(BF16)
        xall[4 + k] = p1[slab]
        xall[8 + k] = hi(slab).astype(BF16)
        xall[12 + k] = beside(cot[2 * k + 1], cot[2 * k + 2]).astype(BF16)
    slab = slice(384, 512)
    edge_lo, edge_hi = lo(slab), hi(slab)
    first = jnp.where(odd, p1[slab].astype(F32), p2[slab].astype(F32))
    last = jnp.where(odd, p2[slab].astype(F32), p1[slab].astype(F32))
    xall[3] = beside(edge_lo[:, :64], first[:, :64]).astype(BF16)
    xall[7] = beside(last[:, :64], edge_hi[:, :64]).astype(BF16)
    xall[11] = beside(edge_lo[:, 64:], first[:, 64:]).astype(BF16)
    xall[15] = beside(last[:, 64:], edge_hi[:, 64:]).astype(BF16)
    xmask[0] = lo(slice(512, 528))
    xmask[1] = p1[512:528].astype(F32)
    xmask[2] = hi(slice(512, 528))
    odd_c, _, _ = place(1)
    for p, low in ((p3, odd_c), (p4, jnp.logical_not(odd_c))):
        for k in range(11):
            near = jnp.where(low, xall[k, 0:64].astype(F32), xall[k, 64:128].astype(F32))
            p[64 * k : 64 * k + 64] = near.astype(BF16)
        cols = []
        for k in range(11, 16):
            slab = xall[k].astype(F32)
            cols.append(jnp.where(low, slab[0:8], slab[120:128]))
        for k in range(3):
            cols.append(jnp.where(low, xmask[k, 0:8], xmask[k, 8:16]))
        p[704:768] = jnp.concatenate(cols, axis=0).astype(BF16)


def forward(
    xall, xmask, r3, r4, weights_hbm,
    decoded_hbm, slope_ef, g_skip, slope_ec, g_dc, s_in, s_pool, kept_hbm,
    mm, cc, s1, ee, s2, s3, slope_dc, s4, acc, acc1, weights, kept, decoded, w_sem, out_sem,
):
    cuts = (W1, W2, W3, W4L, W4E, W5L, W5S, WF)
    loads = []
    for k in range(7):
        rows = pl.ds(cuts[k], cuts[k + 1] - cuts[k])
        loads.append(pltpu.make_async_copy(weights_hbm.at[rows], weights.at[rows], w_sem.at[k]))
        loads[-1].start()
    stores = []

    def store(first, end):
        rows = pl.ds(first, end - first)
        stores.append(pltpu.make_async_copy(kept.at[rows], kept_hbm.at[rows], out_sem.at[len(stores)]))
        stores[-1].start()

    odd, v_lo, v_hi = place(1)

    def lo(at, rows):
        at = pl.ds(at, rows)
        return (jnp.where(odd, r3[at].astype(F32), r4[at].astype(F32)) * v_lo).reshape(rows // 8, 8, 128)

    def hi(at, rows):
        at = pl.ds(at, rows)
        return (jnp.where(odd, r4[at].astype(F32), r3[at].astype(F32)) * v_hi).reshape(rows // 8, 8, 128)

    extra_lo, extra_hi = lo(704, 64), hi(704, 64)
    for k in range(5):
        cc[k, 0] = extra_lo[k]
        cc[k, 1:17] = xall[11 + k].astype(F32).reshape(16, 8, 128)
        cc[k, 17] = extra_hi[k]
    for k in range(3):
        mm[k, 0:6] = jnp.broadcast_to(extra_lo[5 + k][None], (6, 8, 128))
        mm[k, 6:14] = jnp.broadcast_to(xmask[k, 0:8][None], (8, 8, 128))
        mm[k, 14:22] = jnp.broadcast_to(xmask[k, 8:16][None], (8, 8, 128))
        mm[k, 22:28] = jnp.broadcast_to(extra_hi[5 + k][None], (6, 8, 128))

    def spread(i, _):
        at = pl.multiple_of(64 * i, 64)
        v = jnp.concatenate([lo(at, 64), xall[i].astype(F32).reshape(16, 8, 128), hi(at, 64)], axis=0)
        s1[i] = taps_y(v[1:31], 28)

        @pl.when(jnp.logical_and(i >= 3, i < 8))
        def _():
            s_in[i - 3] = taps_y(v[7:25], 16)

        return 0

    lax.fori_loop(0, 11, spread, 0)

    loads[0].wait()

    def encode_dots(i, _):
        wide = jnp.concatenate([s1[pl.ds(5 * i, 5)], s1[pl.ds(5 * i + 1, 5)]], axis=2)
        acc1[pl.ds(pl.multiple_of(1120 * i, 1120), 1120)] = dot(wide.reshape(1120, 768), weights[W1:W2])
        return 0

    lax.fori_loop(0, 2, encode_dots, 0)

    def encode(i, _):
        pre = fold128(acc1[pl.ds(pl.multiple_of(224 * i, 224), 224)])
        mask = mm[jnp.where(i < 3, 0, jnp.where(i < 7, 1, 2))]
        act, slope = silu_parts(pre)
        v = bround(act * mask)
        ee[i] = v

        @pl.when(jnp.logical_and(i >= 3, i < 7))
        def _():
            slope_ef[i - 3] = (slope() * mask)[6:22].reshape(128, 128)

        s = v.reshape(14, 2, 8, 128)
        s = s[:, 0] + s[:, 1]
        s = s[..., :64] + s[..., 64:]
        v = bround(halve_z(s) * 0.125)
        s2[i] = taps_y(v, 12)

        @pl.when(jnp.logical_and(i >= 2, i < 8))
        def _():
            s_pool[i - 2] = taps_y(v[2:12], 8)

        return 0

    lax.fori_loop(0, 10, encode, 0)

    def mask_coarse(block, first, count):
        m = mm[block].reshape(14, 2, 8, 128)[first : first + count, 0]
        return jnp.where(z_of(m.shape) < 4, m, 0.0)

    loads[1].wait()

    def encode2(i, _):
        pre = jnp.zeros((384, 384), F32)
        for a in range(3):
            pre += dot(s2[pl.ds(4 * i + a, 4)].reshape(384, 192), weights[W2 + 192 * a : W2 + 192 * a + 192])
        pre = fold128(pre).reshape(4, 12, 8, 128)
        for k in range(4):
            x = 4 * i + k
            mask = mask_coarse(jnp.where(x < 2, 0, jnp.where(x < 6, 1, 2)), 1, 12)
            act, slope = silu_parts(pre[k])
            v = bround(act * mask)
            s3[x] = taps_y(v, 10)

            @pl.when(jnp.logical_and(x >= 1, x < 7))
            def _():
                slope_ec[x - 1] = (slope() * mask)[1:11].reshape(80, 128)
                kept[pl.ds(pl.multiple_of(COARSE + 64 * (x - 1), 64), 64)] = taps_y(v[1:11], 8)

        return 0

    lax.fori_loop(0, 2, encode2, 0)
    store(COARSE, KEPT)
    loads[2].wait()

    def decode2(i, _):
        pre = jnp.zeros((240, 384), F32)
        for a in range(3):
            pre += dot(s3[pl.ds(3 * i + a, 3)].reshape(240, 384), weights[W3 + 384 * a : W3 + 384 * a + 384])
        pre = fold128(pre).reshape(3, 10, 8, 128)
        for k in range(3):
            x = 3 * i + k
            mask = mask_coarse(jnp.where(x < 1, 0, jnp.where(x < 5, 1, 2)), 2, 10)
            act, slope = silu_parts(pre[k])
            v = double_z(bround(act * mask))
            up = jnp.concatenate([v[:, None], v[:, None]], axis=1).reshape(20, 8, 128)
            kept[pl.ds(pl.multiple_of(LIFT + 144 * x, 144), 144)] = taps_y(up, 18)

            @pl.when(jnp.logical_and(x >= 1, x < 5))
            def _():
                slope_dc[x - 1] = (slope() * mask)[1:9]

        return 0

    lax.fori_loop(0, 2, decode2, 0)

    def skip(i, _):
        kept[pl.ds(pl.multiple_of(SKIP + 144 * i, 144), 144)] = taps_y(ee[i + 2, 4:24], 18)
        return 0

    lax.fori_loop(0, 6, skip, 0)

    store(LIFT, GRAD)
    loads[3].wait()
    loads[4].wait()
    total = jnp.zeros((720, 384), F32)
    for p in range(2):
        for q in range(2):
            at = W4L + 384 * (2 * p + q)
            total += dot_n(kept[LIFT + 144 * p : LIFT + 144 * p + 720], weights[at : at + 384])
        at = W4E + 384 * p
        total += dot_n(kept[SKIP + 144 * p : SKIP + 144 * p + 720], weights[at : at + 384])
    acc[...] = total

    def decode(i, _):
        pre = fold128(acc[pl.ds(pl.multiple_of(144 * i, 144), 144)])
        lane = lax.broadcasted_iota(jnp.int32, (18, 8, 128), 2)
        before, after = jnp.where(i < 1, 0, 1), jnp.where(i < 4, 1, 2)
        mask = jnp.where(lane < 64, mm[before, 5:23], mm[after, 5:23])
        act, slope = silu_parts(pre)
        g = bround(cc[i] * mask * slope())
        s4[i] = taps_y(g, 16)
        out = (act * mask)[1:17].reshape(128, 128).astype(BF16)

        @pl.when(i > 0)
        def _():
            decoded[2 * i - 1] = out[:, :64]

        @pl.when(i < 4)
        def _():
            decoded[2 * i] = out[:, 64:]

        own = jnp.logical_and(jnp.logical_or(lane >= 64, i > 0), jnp.logical_or(lane < 64, i < 4))
        g = jnp.where(own, g, 0.0)
        zero = jnp.zeros((1, 8, 128), F32)
        kept[pl.ds(pl.multiple_of(GRAD + 144 * i, 144), 144)] = taps_z(
            jnp.concatenate([zero, g[1:17], zero], axis=0)
        )
        return 0

    lax.fori_loop(0, 5, decode, 0)
    store(GRAD, COARSE)
    stores.append(pltpu.make_async_copy(decoded, decoded_hbm, out_sem.at[3]))
    stores[-1].start()
    loads[5].wait()
    loads[6].wait()

    def back(i, _):
        wide = jnp.concatenate([s4[pl.ds(2 * i, 2)], s4[pl.ds(2 * i + 1, 2)]], axis=2).reshape(256, 768)
        g_skip[pl.ds(2 * i, 2)] = fold128(dot(wide, weights[W5S:WF])).reshape(2, 128, 128)
        up = dot(wide, weights[W5L : W5L + 768]) + dot(wide, weights[W5L + 768 : W5S])
        up = up.reshape(16, 2, 8, 384)
        g = halve_z(fold128((up[:, 0] + up[:, 1]).reshape(128, 384)))
        g = g.reshape(2, 8, 8, 128) * slope_dc[pl.ds(2 * i, 2)]
        g_dc[pl.ds(2 * i, 2)] = g.reshape(2, 64, 128).astype(BF16)
        return 0

    lax.fori_loop(0, 2, back, 0)
    for copy in stores:
        copy.wait()


def unhalve(both):
    return jnp.concatenate([both[:, :64], both[:, 64:]], axis=0)


def split_wire(wire, keep, send):
    rows = wire.shape[0] // 2
    core = lax.axis_index("core")
    keep[...] = wire[pl.ds(pl.multiple_of(core * rows, rows), rows)]
    send[...] = wire[pl.ds(pl.multiple_of((1 - core) * rows, rows), rows)]


A_SKIP, A_SKIP2, A_COARSE, A_END = 1728, 2304, 2592, 6048
B_FINE2, B_COARSE, B_END = 576, 864, 2592


def weights_decode(kept_hbm, g_dc, keep, send, wire, kept, sem):
    copies = []
    cuts = (LIFT, SKIP, GRAD, COARSE, KEPT)
    for k in range(4):
        rows = pl.ds(cuts[k], cuts[k + 1] - cuts[k])
        copies.append(pltpu.make_async_copy(kept_hbm.at[rows], kept.at[rows], sem.at[k]))
        copies[-1].start()
    for copy in copies:
        copy.wait()
    grad = kept[GRAD:COARSE]
    gc = taps_z(g_dc[...].astype(F32).reshape(32, 8, 128))
    wire[A_END:] = jnp.zeros((wire.shape[0] - A_END, 128), BF16)
    up = [(dot_t(grad, kept[LIFT + 144 * p : LIFT + 144 * p + 720]) * FACTOR).reshape(3, 2, 64, 384) for p in range(2)]
    same = [(dot_t(grad, kept[SKIP + 144 * p : SKIP + 144 * p + 720]) * FACTOR).reshape(3, 2, 64, 384) for p in range(2)]
    for a, (p, q) in enumerate(((0, 0), (0, 1), (1, 0))):
        p2, q2 = (0, 1) if a == 0 else (1, a - 1)
        lifted = (up[p][:, 0] + up[p2][:, 1]).reshape(192, 384).astype(BF16)
        for b in range(3):
            at = 64 * (9 * a + 3 * b)
            wire[at : at + 192] = lifted[:, 128 * b : 128 * b + 128]
        taps = []
        for b in range(3):
            lanes = slice(128 * b, 128 * b + 128)
            taps.append(add_halves(same[p][:, 0, :, lanes].reshape(192, 128), q, same[p2][:, 1, :, lanes].reshape(192, 128), q2))
        put_three(wire, A_SKIP + 192 * a, A_SKIP2 + 96 * a, taps)
        res = (dot_t(kept[COARSE + 64 * a : COARSE + 64 * a + 256], gc) * FACTOR).astype(BF16)
        for b in range(3):
            for c in range(3):
                at = A_COARSE + 128 * (9 * a + 3 * b + c)
                wire[at : at + 128] = res[128 * b : 128 * b + 128, 128 * c : 128 * c + 128]
    split_wire(wire, keep, send)


def add_halves(first, q, second, q2):
    low = (first if q == 0 else pltpu.roll(first, 64, 1)) + (second if q2 == 0 else pltpu.roll(second, 64, 1))
    high = (first if q == 1 else pltpu.roll(first, 64, 1)) + (second if q2 == 1 else pltpu.roll(second, 64, 1))
    return low, high


def put_three(wire, at, at2, taps):
    lane = lax.broadcasted_iota(jnp.int32, (192, 128), 1)
    wire[at : at + 192] = jnp.where(lane < 64, taps[0][0], taps[1][1]).astype(BF16)
    wire[at2 : at2 + 96] = jnp.where(lane[:96] < 64, taps[2][0][:96], taps[2][1][96:]).astype(BF16)


def back_encode(gx, slope_ec, s_pool, s_in, g_skip, slope_ef, weights, keep, send, s5, ge, gz, wire):
    def spread(x, _):
        s5[x] = taps_y(gx[x].astype(F32).reshape(12, 8, 128), 10)
        return 0

    lax.fori_loop(0, 8, spread, 0)
    acc = jnp.zeros((480, 384), F32)
    for a in range(3):
        acc += dot_n(s5[a : a + 6].reshape(480, 384), weights[W6 + 384 * a : W6 + 384 * a + 384])
    g_ec = bround(fold128(acc) * slope_ec[...].reshape(60, 8, 128)).reshape(6, 10, 8, 128)
    for x in range(6):
        ge[x] = taps_y(g_ec[x], 8)
    gc = taps_z(g_ec[1:5, 1:9].reshape(32, 8, 128))
    acc = jnp.zeros((256, 384), F32)
    for a in range(3):
        acc += dot_n(ge[a : a + 4].reshape(256, 384), weights[W7 + 384 * a : W7 + 384 * a + 384])
    up = double_z(fold128(acc) * 0.125)
    up = jnp.concatenate([up[:, None], up[:, None]], axis=1).reshape(4, 16, 8, 128)
    for x in range(4):
        g = (g_skip[x].reshape(16, 8, 128) + up[x]) * slope_ef[x].reshape(16, 8, 128)
        gz[x] = taps_z(bround(g))
    gf = gz[...].reshape(512, 384)
    wire[B_END:] = jnp.zeros((wire.shape[0] - B_END, 128), BF16)
    parts = [(dot_t(s_in[p : p + 4].reshape(512, 384), gf) * FACTOR).reshape(3, 2, 64, 384) for p in range(2)]
    for a, (p, q) in enumerate(((0, 0), (0, 1), (1, 0))):
        p2, q2 = (0, 1) if a == 0 else (1, a - 1)
        taps = []
        for c in range(3):
            lanes = slice(128 * c, 128 * c + 128)
            taps.append(add_halves(parts[p][:, q, :, lanes].reshape(192, 128), 0, parts[p2][:, q2, :, lanes].reshape(192, 128), 1))
        put_three(wire, 192 * a, B_FINE2 + 96 * a, taps)
        res = (dot_t(s_pool[a : a + 4].reshape(256, 192), gc) * FACTOR).astype(BF16)
        for b in range(3):
            for c in range(3):
                at = B_COARSE + 64 * (9 * a + 3 * b + c)
                wire[at : at + 64] = res[64 * b : 64 * b + 64, 128 * c : 128 * c + 128]
    split_wire(wire, keep, send)


def unpack(mine, other, df_hbm, dc_hbm, ef_hbm, ec_hbm, wire_a, wire_b, d_df, d_dc, d_ef, d_ec, sem):
    core = lax.axis_index("core")
    for wire, first in ((wire_a, 0), (wire_b, ROWS_A // 128)):
        rows = wire.shape[0] // 2
        each = rows // 64
        here = pl.ds(pl.multiple_of(core * rows, rows), rows)
        there = pl.ds(pl.multiple_of((1 - core) * rows, rows), rows)
        wire[here] = mine[:, first : first + each].reshape(rows, 128)
        wire[there] = other[:, first : first + each].reshape(rows, 128)
    stores = []

    def store(src, dst, rows):
        stores.append(pltpu.make_async_copy(src.at[rows], dst.at[rows], sem.at[len(stores)]))
        stores[-1].start()

    for a in range(3):
        taps = pl.ds(9 * a, 9)
        first = A_COARSE + 1152 * a
        d_dc[taps] = wire_a[first : first + 1152].astype(F32).reshape(9, 128, 128)
        store(d_dc, dc_hbm, taps)
    for a in range(3):
        taps = pl.ds(9 * a, 9)
        two = wire_a[A_SKIP + 192 * a : A_SKIP + 192 * a + 192].astype(F32)
        three = unhalve(wire_a[A_SKIP2 + 96 * a : A_SKIP2 + 96 * a + 96].astype(F32))
        skip = (two[:, :64], two[:, 64:], three)
        two = wire_b[192 * a : 192 * a + 192].astype(F32)
        three = unhalve(wire_b[B_FINE2 + 96 * a : B_FINE2 + 96 * a + 96].astype(F32))
        fine = (two[:, :64], two[:, 64:], three)
        for b in range(3):
            for c in range(3):
                k = 9 * a + 3 * b + c
                d_df[k, :, :128] = wire_a[64 * k : 64 * k + 64].astype(F32)
                d_df[k, :, 128:] = skip[b][64 * c : 64 * c + 64]
                d_ef[k] = fine[c][64 * b : 64 * b + 64]
        store(d_df, df_hbm, taps)
        store(d_ef, ef_hbm, taps)
        first = B_COARSE + 576 * a
        d_ec[taps] = wire_b[first : first + 576].astype(F32).reshape(9, 64, 128)
        store(d_ec, ec_hbm, taps)
    for copy in stores:
        copy.wait()


def arrange(e1, e2, d3, d4, wf_hbm, wb, wf, sem):
    for a in range(3):
        for b in range(3):
            coarse = slice(128 * b, 128 * b + 128)
            for c in range(3):
                k = 9 * a + 3 * b + c
                lanes = slice(128 * c, 128 * c + 128)
                wf[W2 + 192 * a + 64 * b : W2 + 192 * a + 64 * b + 64, lanes] = e2[k]
                wf[W3 + 384 * a + 128 * b : W3 + 384 * a + 128 * b + 128, lanes] = d3[k]
                at = 384 * a + 128 * c
                wb[W6 + at : W6 + at + 128, coarse] = d3[26 - k]
                wb[W7 + at : W7 + at + 64, coarse] = e2[26 - k]
                wb[W7 + at + 64 : W7 + at + 128, coarse] = e2[26 - k]
    none = jnp.zeros((64, 64), F32)

    def tap(ref, a, rest, lanes, turned=False):
        if a < 0 or a > 2:
            return none
        k = 9 * a + rest
        return ref[26 - k if turned else k, :, lanes].astype(F32)

    all_, low, high = slice(0, 64), slice(0, 128), slice(128, 192)
    for p in range(2):
        for b in range(3):
            for c in range(3):
                rest = 3 * b + c
                lanes = slice(128 * c, 128 * c + 128)
                for q in range(2):
                    at = 384 * p + 128 * b + 64 * q
                    a = 2 * p + q
                    wf[W1 + at : W1 + at + 64, lanes] = beside(tap(e1, a, rest, all_), tap(e1, a - 1, rest, all_)).astype(BF16)
                    wf[W5S + at : W5S + at + 64, lanes] = beside(
                        tap(d4, a, rest, high, True), tap(d4, a - 1, rest, high, True)
                    ).astype(BF16)
                    for o in range(2):
                        to = W5L + 768 * o + at
                        to2 = W4L + 384 * (2 * p + q) + 128 * c + 64 * o
                        coarse = slice(128 * b, 128 * b + 128)
                        if 0 <= a - o <= 2:
                            wf[to : to + 64, lanes] = d4[26 - 9 * (a - o) - rest, :, low]
                            wf[to2 : to2 + 64, coarse] = d4[9 * (a - o) + rest, :, low]
                        else:
                            wf[to : to + 64, lanes] = jnp.zeros((64, 128), BF16)
                            wf[to2 : to2 + 64, coarse] = jnp.zeros((64, 128), BF16)
                for o in range(2):
                    at = W4E + 384 * p + 128 * c + 64 * o
                    wf[at : at + 64, 128 * b : 128 * b + 128] = beside(
                        tap(d4, 2 * p - o, rest, high), tap(d4, 2 * p + 1 - o, rest, high)
                    ).astype(BF16)
    cuts = (W1, W2, W3, W4L, W4E, W5L, W5S, WF)
    copies = []
    for k in range(7):
        rows = pl.ds(cuts[k], cuts[k + 1] - cuts[k])
        copies.append(pltpu.make_async_copy(wf.at[rows], wf_hbm.at[rows], sem.at[k]))
        copies[-1].start()
    for copy in copies:
        copy.wait()


def swap(v, pairs):
    return lax.ppermute(v, ("row", "colh", "core"), pairs)


def body(
    features, block_active, encode_fine, encode_coarse, decode_coarse, decode_fine, out_cotangent
):
    row = lax.axis_index("row")
    core = lax.axis_index("core")
    col = 2 * lax.axis_index("colh") + core
    at = [(r, c) for r in range(8) for c in range(16)]

    def up(i, n):
        return (i + 1) % n if i % 2 else (i - 1) % n

    swap_z = [(16 * r + c, 16 * (r ^ 1) + c) for r, c in at]
    swap_xz = [(16 * r + c, 16 * up(r, 8) + c) for r, c in at]
    swap_core = [(16 * r + c, 16 * r + (c ^ 1)) for r, c in at]
    swap_yz = [(16 * r + c, 16 * r + up(c, 16)) for r, c in at]

    odd_r, odd_c = row % 2, core
    active = block_active.reshape(2)
    w_forward, w_backward = call(
        arrange,
        [((ROOM, 384), BF16, HB), ((WB, 384), BF16)],
        [VM] * 4,
        scratch=[pltpu.VMEM((WF, 384), BF16), pltpu.SemaphoreType.DMA((7,))],
    )(
        encode_fine.reshape(27, 64, 64),
        encode_coarse.reshape(27, 64, 128),
        decode_coarse.reshape(27, 128, 128),
        jnp.transpose(decode_fine, (0, 1, 2, 4, 3)).reshape(27, 64, 192),
    )

    feat = features.reshape(8, 128, 64)
    cot = out_cotangent.reshape(8, 128, 64)
    p1, p2 = call(
        pack_x,
        [((528, 128), BF16)] * 2,
        [HB] * 3,
        scratch=[
            pltpu.SMEM((2,), jnp.int32),
            pltpu.VMEM((8, 128, 64), BF16),
            pltpu.VMEM((2, 128, 64), BF16),
            pltpu.SemaphoreType.DMA((11,)),
        ],
    )(active, feat, cot)
    rz, rxz = swap(p1, swap_z), swap(p2, swap_xz)
    rz, w_forward, w_backward = lax.optimization_barrier((rz, w_forward, w_backward))
    xall, xmask, p3, p4 = call(
        pack_y,
        [((16, 128, 128), BF16), ((3, 16, 128), F32), ((768, 128), BF16), ((768, 128), BF16)],
        [VM] * 5,
        limit=8,
    )(cot, p1, p2, rz, rxz)
    r3, r4 = swap(p3, swap_core), swap(p4, swap_yz)

    decoded, slope_ef, g_skip, slope_ec, g_dc, s_in, s_pool, kept = call(
        forward,
        [
            ((8, 128, 64), BF16, HB),
            ((4, 128, 128), F32),
            ((4, 128, 128), F32),
            ((6, 80, 128), F32),
            ((4, 64, 128), BF16),
            ((5, 128, 384), BF16),
            ((6, 64, 192), BF16),
            ((ROOM, 384), BF16, HB),
        ],
        [VM] * 4 + [HB],
        scratch=[
            pltpu.VMEM((3, 28, 8, 128), F32),
            pltpu.VMEM((5, 18, 8, 128), F32),
            pltpu.VMEM((11, 224, 384), BF16),
            pltpu.VMEM((10, 28, 8, 128), F32),
            pltpu.VMEM((10, 96, 192), BF16),
            pltpu.VMEM((8, 80, 384), BF16),
            pltpu.VMEM((4, 8, 8, 128), F32),
            pltpu.VMEM((5, 128, 384), BF16),
            pltpu.VMEM((720, 384), F32),
            pltpu.VMEM((2240, 384), F32),
            pltpu.VMEM((WF, 384), BF16),
            pltpu.VMEM((KEPT, 384), BF16),
            pltpu.VMEM((8, 128, 64), BF16),
            pltpu.SemaphoreType.DMA((7,)),
            pltpu.SemaphoreType.DMA((4,)),
        ],
        flops=4_000_000_000,
        limit=26,
    )(xall, xmask, r3, r4, w_forward)

    is_odd = odd_r == 1
    q1 = swap(jnp.where(is_odd, g_dc[:2], g_dc[2:]), swap_z)
    q2 = swap(jnp.where(is_odd, g_dc[2:], g_dc[:2]), swap_xz)
    zero = jnp.zeros_like(q1)
    before = jnp.where(row > 0, jnp.where(is_odd, q1, q2), zero)
    after = jnp.where(row < 7, jnp.where(is_odd, q2, q1), zero)
    gx = jnp.concatenate([before, g_dc, after], axis=0)
    is_odd = odd_c == 1
    q3 = swap(jnp.where(is_odd, gx[:, :16], gx[:, 48:]), swap_core)
    q4 = swap(jnp.where(is_odd, gx[:, 48:], gx[:, :16]), swap_yz)
    zero = jnp.zeros_like(q3)
    before = jnp.where(col > 0, jnp.where(is_odd, q3, q4), zero)
    after = jnp.where(col < 15, jnp.where(is_odd, q4, q3), zero)
    gx = jnp.concatenate([before, gx, after], axis=1)

    keep_a, send_a = call(
        weights_decode,
        [((ROWS_A // 2, 128), BF16)] * 2,
        [HB, VM],
        scratch=[
            pltpu.VMEM((ROWS_A, 128), BF16),
            pltpu.VMEM((KEPT, 384), BF16),
            pltpu.SemaphoreType.DMA((4,)),
        ],
        flops=1_000_000_000,
        limit=26,
    )(kept, g_dc)
    got_a = swap(send_a, swap_core)
    gx, keep_a = lax.optimization_barrier((gx, keep_a))

    keep_b, send_b = call(
        back_encode,
        [((ROWS_B // 2, 128), BF16)] * 2,
        [VM] * 7,
        scratch=[
            pltpu.VMEM((8, 80, 384), BF16),
            pltpu.VMEM((6, 64, 384), BF16),
            pltpu.VMEM((4, 128, 384), BF16),
            pltpu.VMEM((ROWS_B, 128), BF16),
        ],
        flops=500_000_000,
        limit=20,
    )(gx, slope_ec, s_pool, s_in, g_skip, slope_ef, w_backward)
    got_b = swap(send_b, swap_core)

    chips = ("row", "colh")
    half = jnp.concatenate(
        [
            (keep.astype(F32) + got.astype(F32)).astype(BF16).reshape(64, -1, 128)
            for keep, got in ((keep_a, got_a), (keep_b, got_b))
        ],
        axis=1,
    )
    terms = lax.all_to_all(half, chips, 0, 0, tiled=True)
    total = jnp.sum(terms.astype(F32), axis=0).astype(BF16)
    mine = lax.all_to_all(jnp.broadcast_to(total[None], (64, CHUNK, 128)), chips, 0, 0, tiled=True)
    other = swap(mine, swap_core)
    shapes = ((27, 64, 192), (27, 128, 128), (27, 64, 64), (27, 64, 128))
    d_df, d_dc, d_ef, d_ec = call(
        unpack,
        [(shape, F32, HB) for shape in shapes],
        [VM] * 2,
        scratch=[pltpu.VMEM((ROWS_A, 128), BF16), pltpu.VMEM((ROWS_B, 128), BF16)]
        + [pltpu.VMEM(shape, F32) for shape in shapes]
        + [pltpu.SemaphoreType.DMA((12,))],
        limit=24,
    )(mine, other)
    return (
        decoded.reshape(8, 16, 8, 64),
        d_ef.reshape(3, 3, 3, 64, 64),
        d_ec.reshape(3, 3, 3, 64, 128),
        d_dc.reshape(3, 3, 3, 128, 128),
        jnp.transpose(d_df.reshape(3, 3, 3, 64, 192), (0, 1, 2, 4, 3)),
    )


def solution(mesh):
    split = Mesh(mesh.devices.reshape(8, 8, 2), ("row", "colh", "core"))
    field = P("row", ("colh", "core"), None, None)
    return jax.shard_map(
        body,
        mesh=split,
        in_specs=(field, P("row", ("colh", "core"), None), P(), P(), P(), P(), field),
        out_specs=(field, P(), P(), P(), P()),
        check_vma=False,
    )
```

```python
import functools
import math

import jax
import jax.numpy as jnp
from jax import lax
from jax.experimental import pallas as pl
from jax.experimental.pallas import tpu as pltpu
from jax.sharding import Mesh, PartitionSpec as P

F32 = jnp.float32
BF16 = jnp.bfloat16
MIB = 1024 * 1024
VM = pl.BlockSpec(memory_space=pltpu.VMEM)
HB = pl.BlockSpec(memory_space=pltpu.HBM)
FACTOR = 1.0 / math.sqrt(64 * 256 * 8)
CHUNK = 72
ROWS_A, ROWS_B = 6144, 3072


def call(kernel, outs, ins, scratch=(), flops=0, limit=58, aliases=None):
    return pl.pallas_call(
        kernel,
        out_shape=[jax.ShapeDtypeStruct(o[0], o[1]) for o in outs],
        in_specs=list(ins),
        out_specs=[o[2] if len(o) > 2 else VM for o in outs],
        scratch_shapes=list(scratch),
        input_output_aliases=aliases or {},
        compiler_params=pltpu.CompilerParams(vmem_limit_bytes=int(limit * MIB)),
        cost_estimate=pl.CostEstimate(flops=flops, bytes_accessed=4_000_000, transcendentals=0),
    )


def dot(lhs, rhs):
    return jnp.dot(lhs, rhs, preferred_element_type=F32)


def dot_n(lhs, rhs):
    return lax.dot_general(lhs, rhs, (((1,), (1,)), ((), ())), preferred_element_type=F32)


def dot_t(lhs, rhs):
    return lax.dot_general(lhs, rhs, (((0,), (0,)), ((), ())), preferred_element_type=F32)


def bround(v):
    return v.astype(BF16).astype(F32)


def z_of(shape):
    return lax.broadcasted_iota(jnp.int32, shape, len(shape) - 2)


def z_later(v):
    return jnp.where(z_of(v.shape) > 0, pltpu.roll(v, 1, 1), 0.0)


def z_earlier(v):
    return jnp.where(z_of(v.shape) < 7, pltpu.roll(v, 7, 1), 0.0)


def fold128(acc):
    rows = acc.shape[0]
    cube = acc.reshape(rows // 8, 8, 384)
    return z_later(cube[..., :128]) + cube[..., 128:256] + z_earlier(cube[..., 256:])


def taps_y(v, count):
    depth = v.shape[2]
    wide = jnp.concatenate([v[b : b + count] for b in range(3)], axis=2)
    return wide.reshape(count * 8, 3 * depth).astype(BF16)


def put_taps(ref, at, v, count):
    low = lax.broadcasted_iota(jnp.int32, (count, 8, 128), 2) < 64
    two = jnp.where(low, v[:count], v[1 : count + 1])
    ref[at, :, :128] = two.reshape(count * 8, 128).astype(BF16)
    ref[at, :, 128:] = v[2 : count + 2].reshape(count * 8, 128).astype(BF16)[:, :64]


def taps_z(g):
    wide = jnp.concatenate([z_earlier(g), g, z_later(g)], axis=2)
    return wide.reshape(g.shape[0] * 8, 3 * g.shape[2]).astype(BF16)


def halve_z(s):
    pair = s + pltpu.roll(s, 7, 1)
    z = z_of(s.shape)
    out = jnp.where(z == 0, pair, 0.0)
    for zc in (1, 2, 3):
        out = jnp.where(z == zc, pltpu.roll(pair, 8 - zc, 1), out)
    return out


def double_z(u):
    z = z_of(u.shape)
    out = u
    for shift in (1, 2, 3, 4):
        out = jnp.where((z + 1) // 2 == shift, pltpu.roll(u, shift, 1), out)
    return out


def silu_parts(v):
    sigma = 0.5 * jnp.tanh(0.5 * v) + 0.5
    act = v * sigma
    return act, lambda: sigma + act * (1.0 - sigma)


W1, W2, W3, W4L, W4E, W5L, W5S, WF = 0, 768, 1344, 2496, 4032, 4800, 6336, 7104
W6, W7, WB = 0, 1152, 2304
LIFT, SKIP, GRAD, COARSE, KEPT = 0, 864, 1728, 2448, 2832
ROOM = 51200


def place(axis):
    at = lax.axis_index("row") if axis == 0 else 2 * lax.axis_index("colh") + lax.axis_index("core")
    last = 7 if axis == 0 else 15
    return at % 2 == 1, (at > 0).astype(F32), (at < last).astype(F32)


def beside(first, second):
    return jnp.concatenate([first.astype(F32), second.astype(F32)], axis=1)


def pack_x(active_hbm, feat_hbm, cot_hbm, p1, p2, active, feat, cot, sem):
    odd, _, _ = place(0)
    copies = [pltpu.make_async_copy(active_hbm, active, sem.at[0])]
    copies += [pltpu.make_async_copy(feat_hbm.at[k], feat.at[k], sem.at[1 + k]) for k in range(8)]
    copies += [pltpu.make_async_copy(cot_hbm.at[7 * k], cot.at[k], sem.at[9 + k]) for k in range(2)]
    for copy in copies:
        copy.start()
    for copy in copies:
        copy.wait()
    row = lax.broadcasted_iota(jnp.int32, (128, 64), 0)
    mask = jnp.where(row < 64, active[0], active[1]).astype(F32)
    row = lax.broadcasted_iota(jnp.int32, (16, 128), 0)
    ends = jnp.where(row < 8, active[0], active[1]).astype(F32).astype(BF16)
    for k in range(3):
        pair = beside(feat[2 * k + 1].astype(F32) * mask, feat[2 * k + 2].astype(F32) * mask).astype(BF16)
        p1[128 * k : 128 * k + 128] = pair
        p2[128 * k : 128 * k + 128] = pair
    for p, edge in ((p1, jnp.where(odd, 0, 1)), (p2, jnp.where(odd, 1, 0))):
        p[384:512] = beside(feat[7 * edge].astype(F32) * mask, cot[edge]).astype(BF16)
        p[512:528] = ends


def pack_y(cot, p1, p2, rz, rxz, xall, xmask, p3, p4):
    odd, v_lo, v_hi = place(0)

    def lo(rows):
        return jnp.where(odd, rz[rows].astype(F32), rxz[rows].astype(F32)) * v_lo

    def hi(rows):
        return jnp.where(odd, rxz[rows].astype(F32), rz[rows].astype(F32)) * v_hi

    for k in range(3):
        slab = slice(128 * k, 128 * k + 128)
        xall[k] = lo(slab).astype(BF16)
        xall[4 + k] = p1[slab]
        xall[8 + k] = hi(slab).astype(BF16)
        xall[12 + k] = beside(cot[2 * k + 1], cot[2 * k + 2]).astype(BF16)
    slab = slice(384, 512)
    edge_lo, edge_hi = lo(slab), hi(slab)
    first = jnp.where(odd, p1[slab].astype(F32), p2[slab].astype(F32))
    last = jnp.where(odd, p2[slab].astype(F32), p1[slab].astype(F32))
    xall[3] = beside(edge_lo[:, :64], first[:, :64]).astype(BF16)
    xall[7] = beside(last[:, :64], edge_hi[:, :64]).astype(BF16)
    xall[11] = beside(edge_lo[:, 64:], first[:, 64:]).astype(BF16)
    xall[15] = beside(last[:, 64:], edge_hi[:, 64:]).astype(BF16)
    xmask[0] = lo(slice(512, 528))
    xmask[1] = p1[512:528].astype(F32)
    xmask[2] = hi(slice(512, 528))
    odd_c, _, _ = place(1)
    for p, low in ((p3, odd_c), (p4, jnp.logical_not(odd_c))):
        for k in range(11):
            near = jnp.where(low, xall[k, 0:64].astype(F32), xall[k, 64:128].astype(F32))
            p[64 * k : 64 * k + 64] = near.astype(BF16)
        cols = []
        for k in range(11, 16):
            slab = xall[k].astype(F32)
            cols.append(jnp.where(low, slab[0:8], slab[120:128]))
        for k in range(3):
            cols.append(jnp.where(low, xmask[k, 0:8], xmask[k, 8:16]))
        p[704:768] = jnp.concatenate(cols, axis=0).astype(BF16)


def forward(
    xall, xmask, r3, r4, weights_hbm,
    decoded_hbm, slope_ef, g_skip, slope_ec, g_dc, s_in, s_pool, kept_hbm,
    mm, cc, s1, ee, s2, s3, slope_dc, s4, acc, acc1, weights, kept, decoded, w_sem, out_sem,
):
    cuts = (W1, W2, W3, W4L, W4E, W5L, W5S, WF)
    loads = []
    for k in range(7):
        rows = pl.ds(cuts[k], cuts[k + 1] - cuts[k])
        loads.append(pltpu.make_async_copy(weights_hbm.at[rows], weights.at[rows], w_sem.at[k]))
        loads[-1].start()
    stores = []

    def store(first, end):
        rows = pl.ds(first, end - first)
        stores.append(pltpu.make_async_copy(kept.at[rows], kept_hbm.at[rows], out_sem.at[len(stores)]))
        stores[-1].start()

    odd, v_lo, v_hi = place(1)

    def lo(at, rows):
        at = pl.ds(at, rows)
        return (jnp.where(odd, r3[at].astype(F32), r4[at].astype(F32)) * v_lo).reshape(rows // 8, 8, 128)

    def hi(at, rows):
        at = pl.ds(at, rows)
        return (jnp.where(odd, r4[at].astype(F32), r3[at].astype(F32)) * v_hi).reshape(rows // 8, 8, 128)

    extra_lo, extra_hi = lo(704, 64), hi(704, 64)
    for k in range(5):
        cc[k, 0] = extra_lo[k]
        cc[k, 1:17] = xall[11 + k].astype(F32).reshape(16, 8, 128)
        cc[k, 17] = extra_hi[k]
    for k in range(3):
        mm[k, 0:6] = jnp.broadcast_to(extra_lo[5 + k][None], (6, 8, 128))
        mm[k, 6:14] = jnp.broadcast_to(xmask[k, 0:8][None], (8, 8, 128))
        mm[k, 14:22] = jnp.broadcast_to(xmask[k, 8:16][None], (8, 8, 128))
        mm[k, 22:28] = jnp.broadcast_to(extra_hi[5 + k][None], (6, 8, 128))

    def spread(i, _):
        at = pl.multiple_of(64 * i, 64)
        v = jnp.concatenate([lo(at, 64), xall[i].astype(F32).reshape(16, 8, 128), hi(at, 64)], axis=0)
        s1[i] = taps_y(v[1:31], 28)

        @pl.when(jnp.logical_and(i >= 3, i < 8))
        def _():
            s_in[i - 3] = taps_y(v[7:25], 16)

        return 0

    lax.fori_loop(0, 11, spread, 0)

    loads[0].wait()

    def encode_dots(i, _):
        wide = jnp.concatenate([s1[pl.ds(5 * i, 5)], s1[pl.ds(5 * i + 1, 5)]], axis=2)
        acc1[pl.ds(pl.multiple_of(1120 * i, 1120), 1120)] = dot(wide.reshape(1120, 768), weights[W1:W2])
        return 0

    lax.fori_loop(0, 2, encode_dots, 0)

    def encode(i, _):
        pre = fold128(acc1[pl.ds(pl.multiple_of(224 * i, 224), 224)])
        mask = mm[jnp.where(i < 3, 0, jnp.where(i < 7, 1, 2))]
        act, slope = silu_parts(pre)
        v = bround(act * mask)
        ee[i] = v

        @pl.when(jnp.logical_and(i >= 3, i < 7))
        def _():
            slope_ef[i - 3] = (slope() * mask)[6:22].reshape(128, 128)

        s = v.reshape(14, 2, 8, 128)
        s = s[:, 0] + s[:, 1]
        s = s + pltpu.roll(s, 64, 2)
        v = bround(halve_z(s) * 0.125)
        put_taps(s2, i, v, 12)

        @pl.when(jnp.logical_and(i >= 2, i < 8))
        def _():
            put_taps(s_pool, i - 2, v[2:12], 8)

        return 0

    lax.fori_loop(0, 10, encode, 0)

    def mask_coarse(block, first, count):
        m = mm[block].reshape(14, 2, 8, 128)[first : first + count, 0]
        return jnp.where(z_of(m.shape) < 4, m, 0.0)

    loads[1].wait()

    def encode2(i, _):
        pre = jnp.zeros((384, 384), F32)
        for a in range(3):
            pre += dot(s2[pl.ds(4 * i + a, 4)].reshape(384, 192), weights[W2 + 192 * a : W2 + 192 * a + 192])
        pre = fold128(pre).reshape(4, 12, 8, 128)
        for k in range(4):
            x = 4 * i + k
            mask = mask_coarse(jnp.where(x < 2, 0, jnp.where(x < 6, 1, 2)), 1, 12)
            act, slope = silu_parts(pre[k])
            v = bround(act * mask)
            s3[x] = taps_y(v, 10)

            @pl.when(jnp.logical_and(x >= 1, x < 7))
            def _():
                slope_ec[x - 1] = (slope() * mask)[1:11].reshape(80, 128)
                kept[pl.ds(pl.multiple_of(COARSE + 64 * (x - 1), 64), 64)] = taps_y(v[1:11], 8)

        return 0

    lax.fori_loop(0, 2, encode2, 0)
    store(COARSE, KEPT)
    loads[2].wait()

    def decode2(i, _):
        pre = jnp.zeros((240, 384), F32)
        for a in range(3):
            pre += dot(s3[pl.ds(3 * i + a, 3)].reshape(240, 384), weights[W3 + 384 * a : W3 + 384 * a + 384])
        pre = fold128(pre).reshape(3, 10, 8, 128)
        for k in range(3):
            x = 3 * i + k
            mask = mask_coarse(jnp.where(x < 1, 0, jnp.where(x < 5, 1, 2)), 2, 10)
            act, slope = silu_parts(pre[k])
            v = double_z(bround(act * mask))
            up = jnp.concatenate([v[:, None], v[:, None]], axis=1).reshape(20, 8, 128)
            kept[pl.ds(pl.multiple_of(LIFT + 144 * x, 144), 144)] = taps_y(up, 18)

            @pl.when(jnp.logical_and(x >= 1, x < 5))
            def _():
                slope_dc[x - 1] = (slope() * mask)[1:9]

        return 0

    lax.fori_loop(0, 2, decode2, 0)

    def skip(i, _):
        kept[pl.ds(pl.multiple_of(SKIP + 144 * i, 144), 144)] = taps_y(ee[i + 2, 4:24], 18)
        return 0

    lax.fori_loop(0, 6, skip, 0)

    store(LIFT, GRAD)
    loads[3].wait()
    loads[4].wait()
    def both(first):
        return jnp.concatenate([kept[first : first + 720], kept[first + 144 : first + 864]], axis=1)

    def taps(first, step):
        return jnp.concatenate([weights[first : first + 384], weights[first + step : first + step + 384]], axis=1)

    lifted = both(LIFT)
    total = dot_n(lifted, taps(W4L, 768)) + dot_n(lifted, taps(W4L + 384, 768)) + dot_n(both(SKIP), taps(W4E, 384))
    acc[...] = total

    def decode(i, _):
        pre = fold128(acc[pl.ds(pl.multiple_of(144 * i, 144), 144)])
        lane = lax.broadcasted_iota(jnp.int32, (18, 8, 128), 2)
        before, after = jnp.where(i < 1, 0, 1), jnp.where(i < 4, 1, 2)
        mask = jnp.where(lane < 64, mm[before, 5:23], mm[after, 5:23])
        act, slope = silu_parts(pre)
        g = bround(cc[i] * mask * slope())
        s4[i] = taps_y(g, 16)
        out = (act * mask)[1:17].reshape(128, 128).astype(BF16)

        @pl.when(i > 0)
        def _():
            decoded[2 * i - 1] = out[:, :64]

        @pl.when(i < 4)
        def _():
            decoded[2 * i] = out[:, 64:]

        own = jnp.logical_and(jnp.logical_or(lane >= 64, i > 0), jnp.logical_or(lane < 64, i < 4))
        g = jnp.where(own, g, 0.0)
        zero = jnp.zeros((1, 8, 128), F32)
        kept[pl.ds(pl.multiple_of(GRAD + 144 * i, 144), 144)] = taps_z(
            jnp.concatenate([zero, g[1:17], zero], axis=0)
        )
        return 0

    lax.fori_loop(0, 5, decode, 0)
    store(GRAD, COARSE)
    stores.append(pltpu.make_async_copy(decoded, decoded_hbm, out_sem.at[3]))
    stores[-1].start()
    loads[5].wait()
    loads[6].wait()

    def back(i, _):
        wide = jnp.concatenate([s4[pl.ds(2 * i, 2)], s4[pl.ds(2 * i + 1, 2)]], axis=2).reshape(256, 768)
        g_skip[pl.ds(2 * i, 2)] = fold128(dot(wide, weights[W5S:WF])).reshape(2, 128, 128)
        up = dot(wide, weights[W5L : W5L + 768]) + dot(wide, weights[W5L + 768 : W5S])
        up = up.reshape(16, 2, 8, 384)
        g = halve_z(fold128((up[:, 0] + up[:, 1]).reshape(128, 384)))
        g = g.reshape(2, 8, 8, 128) * slope_dc[pl.ds(2 * i, 2)]
        g_dc[pl.ds(2 * i, 2)] = g.reshape(2, 64, 128).astype(BF16)
        return 0

    lax.fori_loop(0, 2, back, 0)
    for copy in stores:
        copy.wait()


def unhalve(both):
    return jnp.concatenate([both[:, :64], both[:, 64:]], axis=0)


A_LIFT, A_SKIP, A_SKIP2, A_END = 1728, 2592, 2880, 3024
B_FINE, B_FINE2, B_END = 864, 1152, 1296


def put_parts(wire, first, rows, block):
    for h in range(2):
        wire[h, first : first + rows] = block[rows * h : rows * h + rows]


def put_three(wire, at, at2, taps):
    lane = lax.broadcasted_iota(jnp.int32, (192, 128), 1)
    two = jnp.where(lane < 64, taps[0][0], taps[1][1]).astype(BF16)
    for k in range(3):
        put_parts(wire, at + 32 * k, 32, two[64 * k : 64 * k + 64])
    for h in range(2):
        low = jnp.concatenate([taps[2][0][64 * k + 32 * h : 64 * k + 32 * h + 32] for k in range(3)], axis=0)
        high = jnp.concatenate([taps[2][1][64 * k + 32 * h : 64 * k + 32 * h + 32] for k in range(3)], axis=0)
        wire[h, at2 : at2 + 48] = jnp.where(lane[:48] < 64, low[:48], high[48:]).astype(BF16)


def split_wire(wire, end, keep, send):
    for h in range(2):
        wire[h, end:] = jnp.zeros((wire.shape[1] - end, 128), BF16)
    core = lax.axis_index("core")
    keep[...] = wire[core]
    send[...] = wire[1 - core]


def weights_decode(kept_hbm, g_dc, keep, send, wire, kept, sem):
    copies = []
    cuts = (LIFT, SKIP, GRAD, COARSE, KEPT)
    for k in range(4):
        rows = pl.ds(cuts[k], cuts[k + 1] - cuts[k])
        copies.append(pltpu.make_async_copy(kept_hbm.at[rows], kept.at[rows], sem.at[k]))
        copies[-1].start()
    for copy in copies:
        copy.wait()
    grad = kept[GRAD:COARSE]
    gc = taps_z(g_dc[...].astype(F32).reshape(32, 8, 128))
    up = [(dot_t(grad, kept[LIFT + 144 * p : LIFT + 144 * p + 720]) * FACTOR).reshape(3, 2, 64, 384) for p in range(2)]
    same = [(dot_t(grad, kept[SKIP + 144 * p : SKIP + 144 * p + 720]) * FACTOR).reshape(3, 2, 64, 384) for p in range(2)]
    for a, (p, q) in enumerate(((0, 0), (0, 1), (1, 0))):
        p2, q2 = (0, 1) if a == 0 else (1, a - 1)
        lifted = (up[p][:, 0] + up[p2][:, 1]).reshape(192, 384).astype(BF16)
        for b in range(3):
            for c in range(3):
                at = A_LIFT + 32 * (9 * a + 3 * b + c)
                put_parts(wire, at, 32, lifted[64 * c : 64 * c + 64, 128 * b : 128 * b + 128])
        taps = []
        for b in range(3):
            lanes = slice(128 * b, 128 * b + 128)
            taps.append(add_halves(same[p][:, 0, :, lanes].reshape(192, 128), q, same[p2][:, 1, :, lanes].reshape(192, 128), q2))
        put_three(wire, A_SKIP + 96 * a, A_SKIP2 + 48 * a, taps)
        res = (dot_t(kept[COARSE + 64 * a : COARSE + 64 * a + 256], gc) * FACTOR).astype(BF16)
        for b in range(3):
            for c in range(3):
                at = 64 * (9 * a + 3 * b + c)
                put_parts(wire, at, 64, res[128 * b : 128 * b + 128, 128 * c : 128 * c + 128])
    split_wire(wire, A_END, keep, send)


def add_halves(first, q, second, q2):
    low = (first if q == 0 else pltpu.roll(first, 64, 1)) + (second if q2 == 0 else pltpu.roll(second, 64, 1))
    high = (first if q == 1 else pltpu.roll(first, 64, 1)) + (second if q2 == 1 else pltpu.roll(second, 64, 1))
    return low, high


def back_encode(gx, slope_ec, s_pool, s_in, g_skip, slope_ef, weights, keep, send, s5, ge, gz, wire):
    def spread(x, _):
        s5[x] = taps_y(gx[x].astype(F32).reshape(12, 8, 128), 10)
        return 0

    lax.fori_loop(0, 8, spread, 0)
    acc = jnp.zeros((480, 384), F32)
    for a in range(3):
        acc += dot_n(s5[a : a + 6].reshape(480, 384), weights[W6 + 384 * a : W6 + 384 * a + 384])
    g_ec = bround(fold128(acc) * slope_ec[...].reshape(60, 8, 128)).reshape(6, 10, 8, 128)
    for x in range(6):
        ge[x] = taps_y(g_ec[x], 8)
    gc = taps_z(g_ec[1:5, 1:9].reshape(32, 8, 128))
    acc = jnp.zeros((256, 384), F32)
    for a in range(3):
        acc += dot_n(ge[a : a + 4].reshape(256, 384), weights[W7 + 384 * a : W7 + 384 * a + 384])
    up = double_z(fold128(acc) * 0.125)
    up = jnp.concatenate([up[:, None], up[:, None]], axis=1).reshape(4, 16, 8, 128)
    for x in range(4):
        g = (g_skip[x].reshape(16, 8, 128) + up[x]) * slope_ef[x].reshape(16, 8, 128)
        gz[x] = taps_z(bround(g))
    gf = gz[...].reshape(512, 384)
    parts = [(dot_t(s_in[p : p + 4].reshape(512, 384), gf) * FACTOR).reshape(3, 2, 64, 384) for p in range(2)]
    for a, (p, q) in enumerate(((0, 0), (0, 1), (1, 0))):
        p2, q2 = (0, 1) if a == 0 else (1, a - 1)
        taps = []
        for c in range(3):
            lanes = slice(128 * c, 128 * c + 128)
            taps.append(add_halves(parts[p][:, q, :, lanes].reshape(192, 128), 0, parts[p2][:, q2, :, lanes].reshape(192, 128), 1))
        put_three(wire, B_FINE + 96 * a, B_FINE2 + 48 * a, taps)
        res = (dot_t(s_pool[a : a + 4].reshape(256, 192), gc) * FACTOR).astype(BF16)
        for b in range(3):
            for c in range(3):
                at = 32 * (9 * a + 3 * b + c)
                put_parts(wire, at, 32, res[64 * b : 64 * b + 64, 128 * c : 128 * c + 128])
    split_wire(wire, B_END, keep, send)


def unpack(of_this_core, total, *refs):
    df_hbm, dc_hbm, ef_hbm, ec_hbm, d_df, d_dc, d_ef, d_ec, sem = refs[-9:]
    core = lax.axis_index("core")
    half = core if of_this_core else 1 - core
    wire_a = total[:, : ROWS_A // 128].reshape(ROWS_A // 2, 128)
    wire_b = total[:, ROWS_A // 128 :].reshape(ROWS_B // 2, 128)
    stores = []

    def store(src, dst, a):
        rows = src.shape[1]
        at = pl.ds(pl.multiple_of(half * rows, rows), rows)
        taps = pl.ds(9 * a, 9)
        stores.append(pltpu.make_async_copy(src.at[taps], dst.at[taps, at], sem.at[len(stores)]))
        stores[-1].start()

    def three(wire, at, at2):
        two = wire[at : at + 96].astype(F32)
        return two[:, :64], two[:, 64:], unhalve(wire[at2 : at2 + 48].astype(F32))

    for a in range(3):
        taps = slice(9 * a, 9 * a + 9)
        d_dc[taps] = wire_a[576 * a : 576 * a + 576].astype(F32).reshape(9, 64, 128)
        store(d_dc, dc_hbm, a)
        skip = three(wire_a, A_SKIP + 96 * a, A_SKIP2 + 48 * a)
        fine = three(wire_b, B_FINE + 96 * a, B_FINE2 + 48 * a)
        first = A_LIFT + 288 * a
        d_df[taps, :, :128] = wire_a[first : first + 288].astype(F32).reshape(9, 32, 128)
        for b in range(3):
            for c in range(3):
                k = 9 * a + 3 * b + c
                d_df[k, :, 128:] = skip[b][32 * c : 32 * c + 32]
                d_ef[k] = fine[c][32 * b : 32 * b + 32]
        store(d_df, df_hbm, a)
        store(d_ef, ef_hbm, a)
        d_ec[taps] = wire_b[288 * a : 288 * a + 288].astype(F32).reshape(9, 32, 128)
        store(d_ec, ec_hbm, a)
    for copy in stores:
        copy.wait()


def arrange_back(e2, d3, wb):
    for a in range(3):
        for b in range(3):
            coarse = slice(128 * b, 128 * b + 128)
            for c in range(3):
                k = 9 * a + 3 * b + c
                at = 384 * a + 128 * c
                wb[W6 + at : W6 + at + 128, coarse] = d3[26 - k]
                wb[W7 + at : W7 + at + 64, coarse] = e2[26 - k]
                wb[W7 + at + 64 : W7 + at + 128, coarse] = e2[26 - k]


def arrange(e1, e2, d3, d4, wf_hbm, wf, sem):
    for a in range(3):
        for b in range(3):
            coarse = slice(128 * b, 128 * b + 128)
            for c in range(3):
                k = 9 * a + 3 * b + c
                lanes = slice(128 * c, 128 * c + 128)
                wf[W2 + 192 * a + 64 * b : W2 + 192 * a + 64 * b + 64, lanes] = e2[k]
                wf[W3 + 384 * a + 128 * b : W3 + 384 * a + 128 * b + 128, lanes] = d3[k]
    none = jnp.zeros((64, 64), F32)

    def tap(ref, a, rest, lanes, turned=False):
        if a < 0 or a > 2:
            return none
        k = 9 * a + rest
        return ref[26 - k if turned else k, :, lanes].astype(F32)

    all_, low, high = slice(0, 64), slice(0, 128), slice(128, 192)
    for p in range(2):
        for b in range(3):
            for c in range(3):
                rest = 3 * b + c
                lanes = slice(128 * c, 128 * c + 128)
                for q in range(2):
                    at = 384 * p + 128 * b + 64 * q
                    a = 2 * p + q
                    wf[W1 + at : W1 + at + 64, lanes] = beside(tap(e1, a, rest, all_), tap(e1, a - 1, rest, all_)).astype(BF16)
                    wf[W5S + at : W5S + at + 64, lanes] = beside(
                        tap(d4, a, rest, high, True), tap(d4, a - 1, rest, high, True)
                    ).astype(BF16)
                    for o in range(2):
                        to = W5L + 768 * o + at
                        to2 = W4L + 384 * (2 * p + q) + 128 * c + 64 * o
                        coarse = slice(128 * b, 128 * b + 128)
                        if 0 <= a - o <= 2:
                            wf[to : to + 64, lanes] = d4[26 - 9 * (a - o) - rest, :, low]
                            wf[to2 : to2 + 64, coarse] = d4[9 * (a - o) + rest, :, low]
                        else:
                            wf[to : to + 64, lanes] = jnp.zeros((64, 128), BF16)
                            wf[to2 : to2 + 64, coarse] = jnp.zeros((64, 128), BF16)
                for o in range(2):
                    at = W4E + 384 * p + 128 * c + 64 * o
                    wf[at : at + 64, 128 * b : 128 * b + 128] = beside(
                        tap(d4, 2 * p - o, rest, high), tap(d4, 2 * p + 1 - o, rest, high)
                    ).astype(BF16)
    cuts = (W1, W2, W3, W4L, W4E, W5L, W5S, WF)
    copies = []
    for k in range(7):
        rows = pl.ds(cuts[k], cuts[k + 1] - cuts[k])
        copies.append(pltpu.make_async_copy(wf.at[rows], wf_hbm.at[rows], sem.at[k]))
        copies[-1].start()
    for copy in copies:
        copy.wait()


def swap(v, pairs):
    return lax.ppermute(v, ("row", "colh", "core"), pairs)


def body(
    features, block_active, encode_fine, encode_coarse, decode_coarse, decode_fine, out_cotangent
):
    row = lax.axis_index("row")
    core = lax.axis_index("core")
    col = 2 * lax.axis_index("colh") + core
    at = [(r, c) for r in range(8) for c in range(16)]

    def up(i, n):
        return (i + 1) % n if i % 2 else (i - 1) % n

    swap_z = [(16 * r + c, 16 * (r ^ 1) + c) for r, c in at]
    swap_xz = [(16 * r + c, 16 * up(r, 8) + c) for r, c in at]
    swap_core = [(16 * r + c, 16 * r + (c ^ 1)) for r, c in at]
    swap_yz = [(16 * r + c, 16 * r + up(c, 16)) for r, c in at]

    odd_r, odd_c = row % 2, core
    active = block_active.reshape(2)
    e2 = encode_coarse.reshape(27, 64, 128)
    d3 = decode_coarse.reshape(27, 128, 128)
    d4 = jnp.transpose(decode_fine, (0, 1, 2, 4, 3)).reshape(27, 64, 192)
    (w_forward,) = call(
        arrange,
        [((ROOM, 384), BF16, HB)],
        [VM] * 4,
        scratch=[pltpu.VMEM((WF, 384), BF16), pltpu.SemaphoreType.DMA((7,))],
    )(encode_fine.reshape(27, 64, 64), e2, d3, d4)
    (w_backward,) = call(arrange_back, [((WB, 384), BF16)], [VM] * 2)(e2, d3)

    feat = features.reshape(8, 128, 64)
    cot = out_cotangent.reshape(8, 128, 64)
    p1, p2 = call(
        pack_x,
        [((528, 128), BF16)] * 2,
        [HB] * 3,
        scratch=[
            pltpu.SMEM((2,), jnp.int32),
            pltpu.VMEM((8, 128, 64), BF16),
            pltpu.VMEM((2, 128, 64), BF16),
            pltpu.SemaphoreType.DMA((11,)),
        ],
    )(active, feat, cot)
    rz, rxz = swap(p1, swap_z), swap(p2, swap_xz)
    rz, w_forward = lax.optimization_barrier((rz, w_forward))
    xall, xmask, p3, p4 = call(
        pack_y,
        [((16, 128, 128), BF16), ((3, 16, 128), F32), ((768, 128), BF16), ((768, 128), BF16)],
        [VM] * 5,
        limit=8,
    )(cot, p1, p2, rz, rxz)
    r3, r4 = swap(p3, swap_core), swap(p4, swap_yz)
    r3, w_backward = lax.optimization_barrier((r3, w_backward))

    decoded, slope_ef, g_skip, slope_ec, g_dc, s_in, s_pool, kept = call(
        forward,
        [
            ((8, 128, 64), BF16, HB),
            ((4, 128, 128), F32),
            ((4, 128, 128), F32),
            ((6, 80, 128), F32),
            ((4, 64, 128), BF16),
            ((5, 128, 384), BF16),
            ((6, 64, 192), BF16),
            ((ROOM, 384), BF16, HB),
        ],
        [VM] * 4 + [HB],
        scratch=[
            pltpu.VMEM((3, 28, 8, 128), F32),
            pltpu.VMEM((5, 18, 8, 128), F32),
            pltpu.VMEM((11, 224, 384), BF16),
            pltpu.VMEM((10, 28, 8, 128), F32),
            pltpu.VMEM((10, 96, 192), BF16),
            pltpu.VMEM((8, 80, 384), BF16),
            pltpu.VMEM((4, 8, 8, 128), F32),
            pltpu.VMEM((5, 128, 384), BF16),
            pltpu.VMEM((720, 384), F32),
            pltpu.VMEM((2240, 384), F32),
            pltpu.VMEM((WF, 384), BF16),
            pltpu.VMEM((KEPT, 384), BF16),
            pltpu.VMEM((8, 128, 64), BF16),
            pltpu.SemaphoreType.DMA((7,)),
            pltpu.SemaphoreType.DMA((4,)),
        ],
        flops=4_000_000_000,
        limit=26,
    )(xall, xmask, r3, r4, w_forward)

    def add(keep, got):
        return (keep.astype(F32) + got.astype(F32)).astype(BF16).reshape(64, -1, 128)

    is_odd = odd_r == 1
    q1 = swap(jnp.where(is_odd, g_dc[:2], g_dc[2:]), swap_z)
    q2 = swap(jnp.where(is_odd, g_dc[2:], g_dc[:2]), swap_xz)
    zero = jnp.zeros_like(q1)
    before = jnp.where(row > 0, jnp.where(is_odd, q1, q2), zero)
    after = jnp.where(row < 7, jnp.where(is_odd, q2, q1), zero)
    gx = jnp.concatenate([before, g_dc, after], axis=0)
    is_odd = odd_c == 1
    q3 = swap(jnp.where(is_odd, gx[:, :16], gx[:, 48:]), swap_core)
    q4 = swap(jnp.where(is_odd, gx[:, 48:], gx[:, :16]), swap_yz)
    zero = jnp.zeros_like(q3)
    before = jnp.where(col > 0, jnp.where(is_odd, q3, q4), zero)
    after = jnp.where(col < 15, jnp.where(is_odd, q4, q3), zero)
    gx = jnp.concatenate([before, gx, after], axis=1)

    keep_a, send_a = call(
        weights_decode,
        [((ROWS_A // 2, 128), BF16)] * 2,
        [HB, VM],
        scratch=[
            pltpu.VMEM((2, ROWS_A // 2, 128), BF16),
            pltpu.VMEM((KEPT, 384), BF16),
            pltpu.SemaphoreType.DMA((4,)),
        ],
        flops=1_000_000_000,
        limit=26,
    )(kept, g_dc)
    half_a = add(keep_a, swap(send_a, swap_core))
    gx, keep_a = lax.optimization_barrier((gx, keep_a))

    keep_b, send_b = call(
        back_encode,
        [((ROWS_B // 2, 128), BF16)] * 2,
        [VM] * 7,
        scratch=[
            pltpu.VMEM((8, 80, 384), BF16),
            pltpu.VMEM((6, 64, 384), BF16),
            pltpu.VMEM((4, 128, 384), BF16),
            pltpu.VMEM((2, ROWS_B // 2, 128), BF16),
        ],
        flops=500_000_000,
        limit=20,
    )(gx, slope_ec, s_pool, s_in, g_skip, slope_ef, w_backward)
    half_b = add(keep_b, swap(send_b, swap_core))

    chips = ("row", "colh")
    half = jnp.concatenate([half_a, half_b], axis=1)
    terms = lax.all_to_all(half, chips, 0, 0, tiled=True)
    total = jnp.sum(terms.astype(F32), axis=0).astype(BF16)
    mine = lax.all_to_all(jnp.broadcast_to(total[None], (64, CHUNK, 128)), chips, 0, 0, tiled=True)
    other = swap(mine, swap_core)
    shapes = ((27, 64, 192), (27, 128, 128), (27, 64, 64), (27, 64, 128))
    halves = ((27, 32, 192), (27, 64, 128), (27, 32, 64), (27, 32, 128))
    grads = []
    for of_this_core, values in ((True, mine), (False, other)):
        grads = call(
            functools.partial(unpack, of_this_core),
            [(shape, F32, HB) for shape in shapes],
            [VM] + [HB] * len(grads),
            scratch=[pltpu.VMEM(shape, F32) for shape in halves] + [pltpu.SemaphoreType.DMA((12,))],
            limit=24,
            aliases={1 + k: k for k in range(len(grads))},
        )(values, *grads)
    d_df, d_dc, d_ef, d_ec = grads
    return (
        decoded.reshape(8, 16, 8, 64),
        d_ef.reshape(3, 3, 3, 64, 64),
        d_ec.reshape(3, 3, 3, 64, 128),
        d_dc.reshape(3, 3, 3, 128, 128),
        jnp.transpose(d_df.reshape(3, 3, 3, 64, 192), (0, 1, 2, 4, 3)),
    )


def solution(mesh):
    split = Mesh(mesh.devices.reshape(8, 8, 2), ("row", "colh", "core"))
    field = P("row", ("colh", "core"), None, None)
    return jax.shard_map(
        body,
        mesh=split,
        in_specs=(field, P("row", ("colh", "core"), None), P(), P(), P(), P(), field),
        out_specs=(field, P(), P(), P(), P()),
        check_vma=False,
    )
```

```python
import functools
import math

import jax
import jax.numpy as jnp
from jax import lax
from jax.experimental import pallas as pl
from jax.experimental.pallas import tpu as pltpu
from jax.sharding import Mesh, PartitionSpec as P

F32 = jnp.float32
BF16 = jnp.bfloat16
MIB = 1024 * 1024
VM = pl.BlockSpec(memory_space=pltpu.VMEM)
SM = pl.BlockSpec(memory_space=pltpu.SMEM)
HB = pl.BlockSpec(memory_space=pltpu.HBM)
FACTOR = 1.0 / math.sqrt(64 * 256 * 8)
CHUNK = 72
ROWS_F, ROWS_C, ROWS_B = 1296, 1728, 1296


def call(kernel, outs, ins, scratch=(), flops=0, limit=58, aliases=None):
    return pl.pallas_call(
        kernel,
        out_shape=[jax.ShapeDtypeStruct(o[0], o[1]) for o in outs],
        in_specs=list(ins),
        out_specs=[o[2] if len(o) > 2 else VM for o in outs],
        scratch_shapes=list(scratch),
        input_output_aliases=aliases or {},
        compiler_params=pltpu.CompilerParams(vmem_limit_bytes=int(limit * MIB)),
        cost_estimate=pl.CostEstimate(flops=flops, bytes_accessed=4_000_000, transcendentals=0),
    )


def dot(lhs, rhs):
    return jnp.dot(lhs, rhs, preferred_element_type=F32)


def dot_n(lhs, rhs):
    return lax.dot_general(lhs, rhs, (((1,), (1,)), ((), ())), preferred_element_type=F32)


def dot_t(lhs, rhs):
    return lax.dot_general(lhs, rhs, (((0,), (0,)), ((), ())), preferred_element_type=F32)


def bround(v):
    return v.astype(BF16).astype(F32)


def z_of(shape):
    return lax.broadcasted_iota(jnp.int32, shape, len(shape) - 2)


def z_later(v):
    return jnp.where(z_of(v.shape) > 0, pltpu.roll(v, 1, 1), 0.0)


def z_earlier(v):
    return jnp.where(z_of(v.shape) < 7, pltpu.roll(v, 7, 1), 0.0)


def fold128(acc):
    rows = acc.shape[0]
    cube = acc.reshape(rows // 8, 8, 384)
    return z_later(cube[..., :128]) + cube[..., 128:256] + z_earlier(cube[..., 256:])


def taps_y(v, count):
    depth = v.shape[2]
    wide = jnp.concatenate([v[b : b + count] for b in range(3)], axis=2)
    return wide.reshape(count * 8, 3 * depth).astype(BF16)


def put_taps(ref, at, v, count):
    low = lax.broadcasted_iota(jnp.int32, (count, 8, 128), 2) < 64
    two = jnp.where(low, v[:count], v[1 : count + 1])
    ref[at, :, :128] = two.reshape(count * 8, 128).astype(BF16)
    ref[at, :, 128:] = v[2 : count + 2].reshape(count * 8, 128).astype(BF16)


def taps_z(g):
    wide = jnp.concatenate([z_earlier(g), g, z_later(g)], axis=2)
    return wide.reshape(g.shape[0] * 8, 3 * g.shape[2]).astype(BF16)


def halve_z(s):
    pair = s + pltpu.roll(s, 7, 1)
    z = z_of(s.shape)
    out = jnp.where(z == 0, pair, 0.0)
    for zc in (1, 2, 3):
        out = jnp.where(z == zc, pltpu.roll(pair, 8 - zc, 1), out)
    return out


def double_z(u):
    z = z_of(u.shape)
    out = u
    for shift in (1, 2, 3, 4):
        out = jnp.where((z + 1) // 2 == shift, pltpu.roll(u, shift, 1), out)
    return out


def silu_parts(v):
    sigma = 0.5 * jnp.tanh(0.5 * v) + 0.5
    act = v * sigma
    return act, lambda: sigma + act * (1.0 - sigma)


def own(at, first, count):
    return jnp.where(jnp.logical_and(at >= first, at < first + count), at - first, count)


W1, W2, W3, W4L, W4E, W5L, W5S, WF = 0, 768, 1536, 2688, 4224, 4992, 6528, 7296
W6, W7, WB = 0, 1152, 2304
LIFT, SKIP, GRAD, COARSE, KEPT = 0, 864, 1728, 2448, 2832
SPARE = 2832
ROOM = 51200


def place(axis):
    at = lax.axis_index("row") if axis == 0 else 2 * lax.axis_index("colh") + lax.axis_index("core")
    last = 7 if axis == 0 else 15
    return at % 2 == 1, (at > 0).astype(F32), (at < last).astype(F32)


def beside(first, second):
    return jnp.concatenate([first.astype(F32), second.astype(F32)], axis=1)


def pack_x(active_hbm, feat_hbm, cot_hbm, p1, p2, active, feat, cot, sem):
    odd, _, _ = place(0)
    copies = [pltpu.make_async_copy(active_hbm, active, sem.at[0])]
    copies += [pltpu.make_async_copy(feat_hbm.at[k], feat.at[k], sem.at[1 + k]) for k in range(8)]
    copies += [pltpu.make_async_copy(cot_hbm.at[7 * k], cot.at[k], sem.at[9 + k]) for k in range(2)]
    for copy in copies:
        copy.start()
    for copy in copies:
        copy.wait()
    row = lax.broadcasted_iota(jnp.int32, (128, 64), 0)
    mask = jnp.where(row < 64, active[0], active[1]).astype(F32)
    row = lax.broadcasted_iota(jnp.int32, (16, 128), 0)
    ends = jnp.where(row < 8, active[0], active[1]).astype(F32).astype(BF16)
    for k in range(3):
        pair = beside(feat[2 * k + 1].astype(F32) * mask, feat[2 * k + 2].astype(F32) * mask).astype(BF16)
        p1[128 * k : 128 * k + 128] = pair
        p2[128 * k : 128 * k + 128] = pair
    for p, edge in ((p1, jnp.where(odd, 0, 1)), (p2, jnp.where(odd, 1, 0))):
        p[384:512] = beside(feat[7 * edge].astype(F32) * mask, cot[edge]).astype(BF16)
        p[512:528] = ends


def pack_y(cot, p1, p2, rz, rxz, xall, xmask, p3, p4):
    odd, v_lo, v_hi = place(0)

    def lo(rows):
        return jnp.where(odd, rz[rows].astype(F32), rxz[rows].astype(F32)) * v_lo

    def hi(rows):
        return jnp.where(odd, rxz[rows].astype(F32), rz[rows].astype(F32)) * v_hi

    for k in range(3):
        slab = slice(128 * k, 128 * k + 128)
        xall[k] = lo(slab).astype(BF16)
        xall[4 + k] = p1[slab]
        xall[8 + k] = hi(slab).astype(BF16)
        xall[12 + k] = beside(cot[2 * k + 1], cot[2 * k + 2]).astype(BF16)
    slab = slice(384, 512)
    edge_lo, edge_hi = lo(slab), hi(slab)
    first = jnp.where(odd, p1[slab].astype(F32), p2[slab].astype(F32))
    last = jnp.where(odd, p2[slab].astype(F32), p1[slab].astype(F32))
    xall[3] = beside(edge_lo[:, :64], first[:, :64]).astype(BF16)
    xall[7] = beside(last[:, :64], edge_hi[:, :64]).astype(BF16)
    xall[11] = beside(edge_lo[:, 64:], first[:, 64:]).astype(BF16)
    xall[15] = beside(last[:, 64:], edge_hi[:, 64:]).astype(BF16)
    xmask[0] = lo(slice(512, 528))
    xmask[1] = p1[512:528].astype(F32)
    xmask[2] = hi(slice(512, 528))
    odd_c, _, _ = place(1)
    for p, low in ((p3, odd_c), (p4, jnp.logical_not(odd_c))):
        for k in range(11):
            near = jnp.where(low, xall[k, 0:64].astype(F32), xall[k, 64:128].astype(F32))
            p[64 * k : 64 * k + 64] = near.astype(BF16)
        cols = []
        for k in range(11, 16):
            slab = xall[k].astype(F32)
            cols.append(jnp.where(low, slab[0:8], slab[120:128]))
        for k in range(3):
            cols.append(jnp.where(low, xmask[k, 0:8], xmask[k, 8:16]))
        p[704:768] = jnp.concatenate(cols, axis=0).astype(BF16)


def forward(
    xall, xmask, r3, r4, weights_hbm,
    decoded_hbm, slope_ef, g_skip, slope_ec, g_dc, s_in, s_pool, kept_hbm,
    mm, cc, s1, ee, s2, s3, slope_dc, s4, acc, weights, kept, decoded, w_sem, out_sem,
):
    cuts = (W1, W2, W3, W4L, W4E, W5L, W5S, WF)
    loads = []
    for k in range(7):
        rows = pl.ds(cuts[k], cuts[k + 1] - cuts[k])
        loads.append(pltpu.make_async_copy(weights_hbm.at[rows], weights.at[rows], w_sem.at[k]))
        loads[-1].start()
    stores = []

    def store(first, end):
        rows = pl.ds(first, end - first)
        stores.append(pltpu.make_async_copy(kept.at[rows], kept_hbm.at[rows], out_sem.at[len(stores)]))
        stores[-1].start()

    odd, v_lo, v_hi = place(1)

    def lo(at, rows):
        at = pl.ds(at, rows)
        return (jnp.where(odd, r3[at].astype(F32), r4[at].astype(F32)) * v_lo).reshape(rows // 8, 8, 128)

    def hi(at, rows):
        at = pl.ds(at, rows)
        return (jnp.where(odd, r4[at].astype(F32), r3[at].astype(F32)) * v_hi).reshape(rows // 8, 8, 128)

    extra_lo, extra_hi = lo(704, 64), hi(704, 64)
    for k in range(5):
        cc[k, 0] = extra_lo[k]
        cc[k, 1:17] = xall[11 + k].astype(F32).reshape(16, 8, 128)
        cc[k, 17] = extra_hi[k]
    for k in range(3):
        mm[k, 0:6] = jnp.broadcast_to(extra_lo[5 + k][None], (6, 8, 128))
        mm[k, 6:14] = jnp.broadcast_to(xmask[k, 0:8][None], (8, 8, 128))
        mm[k, 14:22] = jnp.broadcast_to(xmask[k, 8:16][None], (8, 8, 128))
        mm[k, 22:28] = jnp.broadcast_to(extra_hi[5 + k][None], (6, 8, 128))

    def spread(i, _):
        at = pl.multiple_of(64 * i, 64)
        v = jnp.concatenate([lo(at, 64), xall[i].astype(F32).reshape(16, 8, 128), hi(at, 64)], axis=0)
        s1[i] = taps_y(v[1:31], 28)

        s_in[own(i, 3, 5)] = taps_y(v[7:25], 16)
        return 0

    lax.fori_loop(0, 11, spread, 0)

    loads[0].wait()

    def encode(i, pre):
        mask = mm[jnp.where(i < 3, 0, jnp.where(i < 7, 1, 2))]
        act, slope = silu_parts(pre)
        v = bround(act * mask)
        ee[i] = v

        slope_ef[own(i, 3, 4)] = (slope() * mask)[6:22].reshape(128, 128)

        s = v.reshape(14, 2, 8, 128)
        s = s[:, 0] + s[:, 1]
        s = s + pltpu.roll(s, 64, 2)
        v = bround(halve_z(s) * 0.125)
        put_taps(s2, i, v, 12)

        put_taps(s_pool, own(i, 2, 6), v[2:12], 8)

    def encode_two(j, _):
        wide = jnp.concatenate([s1[pl.ds(2 * j, 2)], s1[pl.ds(2 * j + 1, 2)]], axis=2).reshape(448, 768)
        pre = fold128(dot(wide, weights[W1:W2])).reshape(2, 28, 8, 128)
        for k in range(2):
            encode(2 * j + k, pre[k])
        return 0

    lax.fori_loop(0, 5, encode_two, 0, unroll=True)

    def mask_coarse(block, first, count):
        m = mm[block].reshape(14, 2, 8, 128)[first : first + count, 0]
        return jnp.where(z_of(m.shape) < 4, m, 0.0)

    loads[1].wait()

    def encode2(i, _):
        wide = jnp.concatenate([s2[pl.ds(4 * i + a, 4)] for a in range(3)], axis=2).reshape(384, 768)
        pre = fold128(dot(wide, weights[W2:W3])).reshape(4, 12, 8, 128)
        for k in range(4):
            x = 4 * i + k
            mask = mask_coarse(jnp.where(x < 2, 0, jnp.where(x < 6, 1, 2)), 1, 12)
            act, slope = silu_parts(pre[k])
            v = bround(act * mask)
            s3[x] = taps_y(v, 10)

            slope_ec[own(x, 1, 6)] = (slope() * mask)[1:11].reshape(80, 128)
            kept[pl.ds(pl.multiple_of(COARSE + 64 * own(x, 1, 6), 16), 64)] = taps_y(v[1:11], 8)
        return 0

    lax.fori_loop(0, 2, encode2, 0, unroll=True)
    store(COARSE, KEPT)
    loads[2].wait()

    def decode2(i, _):
        wide = jnp.concatenate([s3[pl.ds(3 * i + a, 3)] for a in range(3)], axis=2).reshape(240, 1152)
        pre = fold128(dot(wide, weights[W3:W4L])).reshape(3, 10, 8, 128)
        for k in range(3):
            x = 3 * i + k
            mask = mask_coarse(jnp.where(x < 1, 0, jnp.where(x < 5, 1, 2)), 2, 10)
            act, slope = silu_parts(pre[k])
            v = double_z(bround(act * mask))
            up = jnp.concatenate([v[:, None], v[:, None]], axis=1).reshape(20, 8, 128)
            kept[pl.ds(pl.multiple_of(LIFT + 144 * x, 144), 144)] = taps_y(up, 18)

            slope_dc[own(x, 1, 4)] = (slope() * mask)[1:9]
        return 0

    lax.fori_loop(0, 2, decode2, 0, unroll=True)

    def skip(i, _):
        kept[pl.ds(pl.multiple_of(SKIP + 144 * i, 144), 144)] = taps_y(ee[i + 2, 4:24], 18)
        return 0

    lax.fori_loop(0, 6, skip, 0, unroll=True)

    store(LIFT, GRAD)
    loads[3].wait()
    loads[4].wait()
    def both(first):
        return jnp.concatenate([kept[first : first + 720], kept[first + 144 : first + 864]], axis=1)

    def taps(first, step):
        return jnp.concatenate([weights[first : first + 384], weights[first + step : first + step + 384]], axis=1)

    lifted = both(LIFT)
    wide = jnp.concatenate([lifted, lifted, both(SKIP)], axis=1)
    acc[...] = dot_n(wide, jnp.concatenate([taps(W4L, 768), taps(W4L + 384, 768), taps(W4E, 384)], axis=1))

    def decode(i, _):
        pre = fold128(acc[pl.ds(pl.multiple_of(144 * i, 144), 144)])
        lane = lax.broadcasted_iota(jnp.int32, (18, 8, 128), 2)
        before, after = jnp.where(i < 1, 0, 1), jnp.where(i < 4, 1, 2)
        mask = jnp.where(lane < 64, mm[before, 5:23], mm[after, 5:23])
        act, slope = silu_parts(pre)
        g = bround(cc[i] * mask * slope())
        s4[i] = taps_y(g, 16)
        out = (act * mask)[1:17].reshape(128, 128).astype(BF16)

        decoded[own(2 * i - 1, 0, 8)] = out[:, :64]
        decoded[own(2 * i, 0, 8)] = out[:, 64:]
        inside = jnp.logical_and(jnp.logical_or(lane >= 64, i > 0), jnp.logical_or(lane < 64, i < 4))
        g = jnp.where(inside, g, 0.0)
        zero = jnp.zeros((1, 8, 128), F32)
        kept[pl.ds(pl.multiple_of(GRAD + 144 * i, 144), 144)] = taps_z(
            jnp.concatenate([zero, g[1:17], zero], axis=0)
        )
        return 0

    lax.fori_loop(0, 5, decode, 0, unroll=True)
    store(GRAD, COARSE)
    stores.append(pltpu.make_async_copy(decoded.at[pl.ds(0, 8)], decoded_hbm, out_sem.at[3]))
    stores[-1].start()
    loads[5].wait()
    loads[6].wait()

    def back(i, _):
        wide = jnp.concatenate([s4[pl.ds(2 * i, 2)], s4[pl.ds(2 * i + 1, 2)]], axis=2).reshape(256, 768)
        g_skip[pl.ds(2 * i, 2)] = fold128(dot(wide, weights[W5S:WF])).reshape(2, 128, 128)
        up = dot(wide, weights[W5L : W5L + 768]) + dot(wide, weights[W5L + 768 : W5S])
        up = up.reshape(16, 2, 8, 384)
        g = halve_z(fold128((up[:, 0] + up[:, 1]).reshape(128, 384)))
        g = g.reshape(2, 8, 8, 128) * slope_dc[pl.ds(2 * i, 2)]
        g_dc[pl.ds(2 * i, 2)] = g.reshape(2, 64, 128).astype(BF16)
        return 0

    lax.fori_loop(0, 2, back, 0, unroll=True)
    for copy in stores:
        copy.wait()


def unhalve(both):
    return jnp.concatenate([both[:, :64], both[:, 64:]], axis=0)


A_SKIP, A_SKIP2 = 864, 1152
B_FINE, B_FINE2 = 864, 1152


def put_parts(wire, first, rows, block):
    for h in range(2):
        wire[h, first : first + rows] = block[rows * h : rows * h + rows]


def put_three(wire, at, at2, taps):
    lane = lax.broadcasted_iota(jnp.int32, (192, 128), 1)
    two = jnp.where(lane < 64, taps[0][0], taps[1][1]).astype(BF16)
    for k in range(3):
        put_parts(wire, at + 32 * k, 32, two[64 * k : 64 * k + 64])
    for h in range(2):
        low = jnp.concatenate([taps[2][0][64 * k + 32 * h : 64 * k + 32 * h + 32] for k in range(3)], axis=0)
        high = jnp.concatenate([taps[2][1][64 * k + 32 * h : 64 * k + 32 * h + 32] for k in range(3)], axis=0)
        wire[h, at2 : at2 + 48] = jnp.where(lane[:48] < 64, low[:48], high[48:]).astype(BF16)


def split_wire(wire, keep, send):
    core = lax.axis_index("core")
    keep[...] = wire[core]
    send[...] = wire[1 - core]


def fetch(kept_hbm, kept, first, end, sem):
    copy = pltpu.make_async_copy(kept_hbm.at[pl.ds(first, end - first)], kept, sem)
    copy.start()
    return copy


def weights_fine(kept_hbm, keep, send, token, wire, kept, sem):
    copies = [
        fetch(kept_hbm, kept.at[pl.ds(first, end - first)], first, end, sem.at[k])
        for k, (first, end) in enumerate(((LIFT, SKIP), (SKIP, GRAD), (GRAD, COARSE)))
    ]
    for copy in copies:
        copy.wait()
    grad = kept[GRAD:COARSE]
    up = [(dot_t(grad, kept[LIFT + 144 * p : LIFT + 144 * p + 720]) * FACTOR).reshape(3, 2, 64, 384) for p in range(2)]
    same = [(dot_t(grad, kept[SKIP + 144 * p : SKIP + 144 * p + 720]) * FACTOR).reshape(3, 2, 64, 384) for p in range(2)]
    for a, (p, q) in enumerate(((0, 0), (0, 1), (1, 0))):
        p2, q2 = (0, 1) if a == 0 else (1, a - 1)
        lifted = (up[p][:, 0] + up[p2][:, 1]).reshape(192, 384).astype(BF16)
        for b in range(3):
            for c in range(3):
                at = 32 * (9 * a + 3 * b + c)
                put_parts(wire, at, 32, lifted[64 * c : 64 * c + 64, 128 * b : 128 * b + 128])
        taps = []
        for b in range(3):
            lanes = slice(128 * b, 128 * b + 128)
            taps.append(add_halves(same[p][:, 0, :, lanes].reshape(192, 128), q, same[p2][:, 1, :, lanes].reshape(192, 128), q2))
        put_three(wire, A_SKIP + 96 * a, A_SKIP2 + 48 * a, taps)
    split_wire(wire, keep, send)
    token[0, 0] = jnp.int32(0)


def weights_coarse(kept_hbm, g_dc, keep, send, wire, kept, sem):
    copy = fetch(kept_hbm, kept, COARSE, KEPT, sem.at[0])
    gc = taps_z(g_dc[...].astype(F32).reshape(32, 8, 128))
    copy.wait()
    for a in range(3):
        res = (dot_t(kept[64 * a : 64 * a + 256], gc) * FACTOR).astype(BF16)
        for b in range(3):
            for c in range(3):
                at = 64 * (9 * a + 3 * b + c)
                put_parts(wire, at, 64, res[128 * b : 128 * b + 128, 128 * c : 128 * c + 128])
    split_wire(wire, keep, send)


def add_halves(first, q, second, q2):
    low = (first if q == 0 else pltpu.roll(first, 64, 1)) + (second if q2 == 0 else pltpu.roll(second, 64, 1))
    high = (first if q == 1 else pltpu.roll(first, 64, 1)) + (second if q2 == 1 else pltpu.roll(second, 64, 1))
    return low, high


def back_encode(gx, slope_ec, s_pool, s_in, g_skip, slope_ef, weights, keep, send, s5, ge, gz, wire):
    def spread(x, _):
        s5[x] = taps_y(gx[x].astype(F32).reshape(12, 8, 128), 10)
        return 0

    lax.fori_loop(0, 8, spread, 0)

    def taps(first):
        return jnp.concatenate([weights[first + 384 * a : first + 384 * a + 384] for a in range(3)], axis=1)

    acc = dot_n(jnp.concatenate([s5[a : a + 6] for a in range(3)], axis=2).reshape(480, 1152), taps(W6))
    g_ec = bround(fold128(acc) * slope_ec[0:6].reshape(60, 8, 128)).reshape(6, 10, 8, 128)
    for x in range(6):
        ge[x] = taps_y(g_ec[x], 8)
    gc = taps_z(g_ec[1:5, 1:9].reshape(32, 8, 128))
    acc = dot_n(jnp.concatenate([ge[a : a + 4] for a in range(3)], axis=2).reshape(256, 1152), taps(W7))
    up = double_z(fold128(acc) * 0.125)
    up = jnp.concatenate([up[:, None], up[:, None]], axis=1).reshape(4, 16, 8, 128)
    for x in range(4):
        g = (g_skip[x].reshape(16, 8, 128) + up[x]) * slope_ef[x].reshape(16, 8, 128)
        gz[x] = taps_z(bround(g))
    gf = gz[...].reshape(512, 384)
    parts = [(dot_t(s_in[p : p + 4].reshape(512, 384), gf) * FACTOR).reshape(3, 2, 64, 384) for p in range(2)]
    for a, (p, q) in enumerate(((0, 0), (0, 1), (1, 0))):
        p2, q2 = (0, 1) if a == 0 else (1, a - 1)
        taps = []
        for c in range(3):
            lanes = slice(128 * c, 128 * c + 128)
            taps.append(add_halves(parts[p][:, q, :, lanes].reshape(192, 128), 0, parts[p2][:, q2, :, lanes].reshape(192, 128), 1))
        put_three(wire, B_FINE + 96 * a, B_FINE2 + 48 * a, taps)
        res = (dot_t(s_pool[a : a + 4].reshape(256, 256), gc) * FACTOR).astype(BF16)
        for b in range(3):
            for c in range(3):
                at = 32 * (9 * a + 3 * b + c)
                put_parts(wire, at, 32, res[64 * b : 64 * b + 64, 128 * c : 128 * c + 128])
    split_wire(wire, keep, send)


def unpack(of_this_core, total, *refs):
    df_hbm, dc_hbm, ef_hbm, ec_hbm, d_df, d_dc, d_ef, d_ec, sem = refs[-9:]
    core = lax.axis_index("core")
    half = core if of_this_core else 1 - core
    wire = total[...].reshape(64 * CHUNK, 128)
    wire_a, wire_c, wire_b = wire[:ROWS_F], wire[ROWS_F : ROWS_F + ROWS_C], wire[ROWS_F + ROWS_C :]
    stores = []

    def store(src, dst, a):
        rows = src.shape[1]
        at = pl.ds(pl.multiple_of(half * rows, rows), rows)
        taps = pl.ds(9 * a, 9)
        stores.append(pltpu.make_async_copy(src.at[taps], dst.at[taps, at], sem.at[len(stores)]))
        stores[-1].start()

    def three(wire, at, at2):
        two = wire[at : at + 96].astype(F32)
        return two[:, :64], two[:, 64:], unhalve(wire[at2 : at2 + 48].astype(F32))

    for a in range(3):
        taps = slice(9 * a, 9 * a + 9)
        d_dc[taps] = wire_c[576 * a : 576 * a + 576].astype(F32).reshape(9, 64, 128)
        store(d_dc, dc_hbm, a)
        skip = three(wire_a, A_SKIP + 96 * a, A_SKIP2 + 48 * a)
        fine = three(wire_b, B_FINE + 96 * a, B_FINE2 + 48 * a)
        d_df[taps, :, :128] = wire_a[288 * a : 288 * a + 288].astype(F32).reshape(9, 32, 128)
        for b in range(3):
            for c in range(3):
                k = 9 * a + 3 * b + c
                d_df[k, :, 128:] = skip[b][32 * c : 32 * c + 32]
                d_ef[k] = fine[c][32 * b : 32 * b + 32]
        store(d_df, df_hbm, a)
        store(d_ef, ef_hbm, a)
        d_ec[taps] = wire_b[288 * a : 288 * a + 288].astype(F32).reshape(9, 32, 128)
        store(d_ec, ec_hbm, a)
    for copy in stores:
        copy.wait()


def arrange_back(e2, d3, wb):
    for a in range(3):
        for b in range(3):
            coarse = slice(128 * b, 128 * b + 128)
            for c in range(3):
                k = 9 * a + 3 * b + c
                at = 384 * a + 128 * c
                wb[W6 + at : W6 + at + 128, coarse] = d3[26 - k]
                wb[W7 + at : W7 + at + 64, coarse] = e2[26 - k]
                wb[W7 + at + 64 : W7 + at + 128, coarse] = e2[26 - k]


def arrange(e1, e2, d3, d4, wf_hbm, wf, sem):
    for a in range(3):
        for b in range(3):
            coarse = slice(128 * b, 128 * b + 128)
            for c in range(3):
                k = 9 * a + 3 * b + c
                lanes = slice(128 * c, 128 * c + 128)
                wf[W2 + 256 * a + 64 * b : W2 + 256 * a + 64 * b + 64, lanes] = e2[k]
                wf[W3 + 384 * a + 128 * b : W3 + 384 * a + 128 * b + 128, lanes] = d3[k]
        wf[W2 + 256 * a + 192 : W2 + 256 * a + 256] = jnp.zeros((64, 384), BF16)
    copies = []

    def copy_out(first, rows):
        at = pl.ds(first, rows)
        copies.append(pltpu.make_async_copy(wf.at[at], wf_hbm.at[at], sem.at[len(copies)]))
        copies[-1].start()

    copy_out(W2, W4L - W2)
    none = jnp.zeros((64, 64), F32)

    def tap(ref, a, rest, lanes, turned=False):
        if a < 0 or a > 2:
            return none
        k = 9 * a + rest
        return ref[26 - k if turned else k, :, lanes].astype(F32)

    all_, low, high = slice(0, 64), slice(0, 128), slice(128, 192)
    for p in range(2):
        for b in range(3):
            for c in range(3):
                rest = 3 * b + c
                lanes = slice(128 * c, 128 * c + 128)
                for q in range(2):
                    at = 384 * p + 128 * b + 64 * q
                    a = 2 * p + q
                    wf[W1 + at : W1 + at + 64, lanes] = beside(tap(e1, a, rest, all_), tap(e1, a - 1, rest, all_)).astype(BF16)
                    wf[W5S + at : W5S + at + 64, lanes] = beside(
                        tap(d4, a, rest, high, True), tap(d4, a - 1, rest, high, True)
                    ).astype(BF16)
                    for o in range(2):
                        to = W5L + 768 * o + at
                        to2 = W4L + 384 * (2 * p + q) + 128 * c + 64 * o
                        coarse = slice(128 * b, 128 * b + 128)
                        if 0 <= a - o <= 2:
                            wf[to : to + 64, lanes] = d4[26 - 9 * (a - o) - rest, :, low]
                            wf[to2 : to2 + 64, coarse] = d4[9 * (a - o) + rest, :, low]
                        else:
                            wf[to : to + 64, lanes] = jnp.zeros((64, 128), BF16)
                            wf[to2 : to2 + 64, coarse] = jnp.zeros((64, 128), BF16)
                for o in range(2):
                    at = W4E + 384 * p + 128 * c + 64 * o
                    wf[at : at + 64, 128 * b : 128 * b + 128] = beside(
                        tap(d4, 2 * p - o, rest, high), tap(d4, 2 * p + 1 - o, rest, high)
                    ).astype(BF16)
        for first, rows in ((W1, 384), (W4L, 768), (W4E, 384), (W5L, 384), (W5L + 384, 384), (W5S, 384)):
            copy_out(first + rows * p if first != W5L + 384 else W5L + 768 + 384 * p, rows)
    for copy in copies:
        copy.wait()


def swap(v, pairs):
    return lax.ppermute(v, ("row", "colh", "core"), pairs)


def body(
    features, block_active, encode_fine, encode_coarse, decode_coarse, decode_fine, out_cotangent
):
    row = lax.axis_index("row")
    core = lax.axis_index("core")
    col = 2 * lax.axis_index("colh") + core
    at = [(r, c) for r in range(8) for c in range(16)]

    def up(i, n):
        return (i + 1) % n if i % 2 else (i - 1) % n

    swap_z = [(16 * r + c, 16 * (r ^ 1) + c) for r, c in at]
    swap_xz = [(16 * r + c, 16 * up(r, 8) + c) for r, c in at]
    swap_core = [(16 * r + c, 16 * r + (c ^ 1)) for r, c in at]
    swap_yz = [(16 * r + c, 16 * r + up(c, 16)) for r, c in at]

    odd_r, odd_c = row % 2, core
    active = block_active.reshape(2)
    e2 = encode_coarse.reshape(27, 64, 128)
    d3 = decode_coarse.reshape(27, 128, 128)
    d4 = jnp.transpose(decode_fine, (0, 1, 2, 4, 3)).reshape(27, 64, 192)
    (w_forward,) = call(
        arrange,
        [((ROOM, 384), BF16, HB)],
        [VM] * 4,
        scratch=[pltpu.VMEM((WF, 384), BF16), pltpu.SemaphoreType.DMA((13,))],
    )(encode_fine.reshape(27, 64, 64), e2, d3, d4)
    (w_backward,) = call(arrange_back, [((WB, 384), BF16)], [VM] * 2)(e2, d3)

    feat = features.reshape(8, 128, 64)
    cot = out_cotangent.reshape(8, 128, 64)
    p1, p2 = call(
        pack_x,
        [((528, 128), BF16)] * 2,
        [HB] * 3,
        scratch=[
            pltpu.SMEM((2,), jnp.int32),
            pltpu.VMEM((8, 128, 64), BF16),
            pltpu.VMEM((2, 128, 64), BF16),
            pltpu.SemaphoreType.DMA((11,)),
        ],
    )(active, feat, cot)
    rz, rxz = swap(p1, swap_z), swap(p2, swap_xz)
    rz, w_forward = lax.optimization_barrier((rz, w_forward))
    xall, xmask, p3, p4 = call(
        pack_y,
        [((16, 128, 128), BF16), ((3, 16, 128), F32), ((768, 128), BF16), ((768, 128), BF16)],
        [VM] * 5,
        limit=8,
    )(cot, p1, p2, rz, rxz)
    r3, r4 = swap(p3, swap_core), swap(p4, swap_yz)
    r3, w_backward = lax.optimization_barrier((r3, w_backward))

    decoded, slope_ef, g_skip, slope_ec, g_dc, s_in, s_pool, kept = call(
        forward,
        [
            ((8, 128, 64), BF16, HB),
            ((5, 128, 128), F32),
            ((4, 128, 128), F32),
            ((7, 80, 128), F32),
            ((4, 64, 128), BF16),
            ((6, 128, 384), BF16),
            ((7, 64, 256), BF16),
            ((ROOM, 384), BF16, HB),
        ],
        [VM] * 4 + [HB],
        scratch=[
            pltpu.VMEM((3, 28, 8, 128), F32),
            pltpu.VMEM((5, 18, 8, 128), F32),
            pltpu.VMEM((11, 224, 384), BF16),
            pltpu.VMEM((10, 28, 8, 128), F32),
            pltpu.VMEM((10, 96, 256), BF16),
            pltpu.VMEM((8, 80, 384), BF16),
            pltpu.VMEM((5, 8, 8, 128), F32),
            pltpu.VMEM((5, 128, 384), BF16),
            pltpu.VMEM((720, 384), F32),
            pltpu.VMEM((WF, 384), BF16),
            pltpu.VMEM((SPARE + 64, 384), BF16),
            pltpu.VMEM((9, 128, 64), BF16),
            pltpu.SemaphoreType.DMA((7,)),
            pltpu.SemaphoreType.DMA((4,)),
        ],
        flops=4_000_000_000,
        limit=26,
    )(xall, xmask, r3, r4, w_forward)

    def add(keep, got):
        return (keep.astype(F32) + got.astype(F32)).astype(BF16)

    keep_f, send_f, token = call(
        weights_fine,
        [((ROWS_F, 128), BF16), ((ROWS_F, 128), BF16), ((1, 1), jnp.int32, SM)],
        [HB],
        scratch=[
            pltpu.VMEM((2, ROWS_F, 128), BF16),
            pltpu.VMEM((COARSE, 384), BF16),
            pltpu.SemaphoreType.DMA((3,)),
        ],
        flops=1_000_000_000,
        limit=26,
    )(kept)
    keep_c, send_c = call(
        weights_coarse,
        [((ROWS_C, 128), BF16)] * 2,
        [HB, VM],
        scratch=[
            pltpu.VMEM((2, ROWS_C, 128), BF16),
            pltpu.VMEM((KEPT - COARSE, 384), BF16),
            pltpu.SemaphoreType.DMA((1,)),
        ],
        flops=300_000_000,
        limit=26,
    )(kept, g_dc)

    is_odd = odd_r == 1
    q1 = swap(jnp.where(is_odd, g_dc[:2], g_dc[2:]), swap_z)
    q2 = swap(jnp.where(is_odd, g_dc[2:], g_dc[:2]), swap_xz)
    zero = jnp.zeros_like(q1)
    before = jnp.where(row > 0, jnp.where(is_odd, q1, q2), zero)
    after = jnp.where(row < 7, jnp.where(is_odd, q2, q1), zero)
    gx = jnp.concatenate([before, g_dc, after], axis=0)
    odd_c, token = lax.optimization_barrier((odd_c, token))
    is_odd = odd_c == 1
    q3 = swap(jnp.where(is_odd, gx[:, :16], gx[:, 48:]), swap_core)
    q4 = swap(jnp.where(is_odd, gx[:, 48:], gx[:, :16]), swap_yz)
    zero = jnp.zeros_like(q3)
    before = jnp.where(col > 0, jnp.where(is_odd, q3, q4), zero)
    after = jnp.where(col < 15, jnp.where(is_odd, q4, q3), zero)
    gx = jnp.concatenate([before, gx, after], axis=1)
    gx, keep_c = lax.optimization_barrier((gx, keep_c))


    keep_b, send_b = call(
        back_encode,
        [((ROWS_B, 128), BF16)] * 2,
        [VM] * 7,
        scratch=[
            pltpu.VMEM((8, 80, 384), BF16),
            pltpu.VMEM((6, 64, 384), BF16),
            pltpu.VMEM((4, 128, 384), BF16),
            pltpu.VMEM((2, ROWS_B, 128), BF16),
        ],
        flops=500_000_000,
        limit=20,
    )(gx, slope_ec, s_pool, s_in, g_skip, slope_ef, w_backward)
    sums = [add(keep, swap(send, swap_core)) for keep, send in ((keep_f, send_f), (keep_c, send_c), (keep_b, send_b))]

    chips = ("row", "colh")
    half = jnp.pad(jnp.concatenate(sums, axis=0), ((0, 64 * CHUNK - 4320), (0, 0))).reshape(64, CHUNK, 128)
    terms = lax.all_to_all(half, chips, 0, 0, tiled=True)
    total = jnp.sum(terms.astype(F32), axis=0).astype(BF16)
    mine = lax.all_to_all(jnp.broadcast_to(total[None], (64, CHUNK, 128)), chips, 0, 0, tiled=True)
    other = swap(mine, swap_core)
    shapes = ((27, 64, 192), (27, 128, 128), (27, 64, 64), (27, 64, 128))
    halves = ((27, 32, 192), (27, 64, 128), (27, 32, 64), (27, 32, 128))
    grads = []
    for of_this_core, values in ((True, mine), (False, other)):
        grads = call(
            functools.partial(unpack, of_this_core),
            [(shape, F32, HB) for shape in shapes],
            [VM] + [HB] * len(grads),
            scratch=[pltpu.VMEM(shape, F32) for shape in halves] + [pltpu.SemaphoreType.DMA((12,))],
            limit=24,
            aliases={1 + k: k for k in range(len(grads))},
        )(values, *grads)
    d_df, d_dc, d_ef, d_ec = grads
    return (
        decoded.reshape(8, 16, 8, 64),
        d_ef.reshape(3, 3, 3, 64, 64),
        d_ec.reshape(3, 3, 3, 64, 128),
        d_dc.reshape(3, 3, 3, 128, 128),
        jnp.transpose(d_df.reshape(3, 3, 3, 64, 192), (0, 1, 2, 4, 3)),
    )


def solution(mesh):
    split = Mesh(mesh.devices.reshape(8, 8, 2), ("row", "colh", "core"))
    field = P("row", ("colh", "core"), None, None)
    return jax.shard_map(
        body,
        mesh=split,
        in_specs=(field, P("row", ("colh", "core"), None), P(), P(), P(), P(), field),
        out_specs=(field, P(), P(), P(), P()),
        check_vma=False,
    )
```

```python
import functools
import math

import jax
import jax.numpy as jnp
from jax import lax
from jax.experimental import pallas as pl
from jax.experimental.pallas import tpu as pltpu
from jax.sharding import Mesh, PartitionSpec as P

F32 = jnp.float32
BF16 = jnp.bfloat16
MIB = 1024 * 1024
VM = pl.BlockSpec(memory_space=pltpu.VMEM)
SM = pl.BlockSpec(memory_space=pltpu.SMEM)
HB = pl.BlockSpec(memory_space=pltpu.HBM)
FACTOR = 1.0 / math.sqrt(64 * 256 * 8)
CHUNK = 72
ROWS_F, ROWS_C, ROWS_B = 1296, 1728, 1296


def call(kernel, outs, ins, scratch=(), flops=0, limit=58, aliases=None):
    return pl.pallas_call(
        kernel,
        out_shape=[jax.ShapeDtypeStruct(o[0], o[1]) for o in outs],
        in_specs=list(ins),
        out_specs=[o[2] if len(o) > 2 else VM for o in outs],
        scratch_shapes=list(scratch),
        input_output_aliases=aliases or {},
        compiler_params=pltpu.CompilerParams(vmem_limit_bytes=int(limit * MIB)),
        cost_estimate=pl.CostEstimate(flops=flops, bytes_accessed=4_000_000, transcendentals=0),
    )


def dot(lhs, rhs):
    return jnp.dot(lhs, rhs, preferred_element_type=F32)


def dot_n(lhs, rhs):
    return lax.dot_general(lhs, rhs, (((1,), (1,)), ((), ())), preferred_element_type=F32)


def dot_t(lhs, rhs):
    return lax.dot_general(lhs, rhs, (((0,), (0,)), ((), ())), preferred_element_type=F32)


def bround(v):
    return v.astype(BF16).astype(F32)


def z_of(shape):
    return lax.broadcasted_iota(jnp.int32, shape, len(shape) - 2)


def z_later(v):
    return jnp.where(z_of(v.shape) > 0, pltpu.roll(v, 1, 1), 0.0)


def z_earlier(v):
    return jnp.where(z_of(v.shape) < 7, pltpu.roll(v, 7, 1), 0.0)


def fold128(acc):
    rows = acc.shape[0]
    cube = acc.reshape(rows // 8, 8, 384)
    return z_later(cube[..., :128]) + cube[..., 128:256] + z_earlier(cube[..., 256:])


def taps_y(v, count):
    depth = v.shape[2]
    wide = jnp.concatenate([v[b : b + count] for b in range(3)], axis=2)
    return wide.reshape(count * 8, 3 * depth).astype(BF16)


def put_taps(ref, at, v, count):
    low = lax.broadcasted_iota(jnp.int32, (count, 8, 128), 2) < 64
    two = jnp.where(low, v[:count], v[1 : count + 1])
    ref[at, :, :128] = two.reshape(count * 8, 128).astype(BF16)
    ref[at, :, 128:] = v[2 : count + 2].reshape(count * 8, 128).astype(BF16)


def taps_z(g):
    wide = jnp.concatenate([z_earlier(g), g, z_later(g)], axis=2)
    return wide.reshape(g.shape[0] * 8, 3 * g.shape[2]).astype(BF16)


def halve_z(s):
    pair = s + pltpu.roll(s, 7, 1)
    z = z_of(s.shape)
    out = jnp.where(z == 0, pair, 0.0)
    for zc in (1, 2, 3):
        out = jnp.where(z == zc, pltpu.roll(pair, 8 - zc, 1), out)
    return out


def double_z(u):
    z = z_of(u.shape)
    out = u
    for shift in (1, 2, 3, 4):
        out = jnp.where((z + 1) // 2 == shift, pltpu.roll(u, shift, 1), out)
    return out


def silu_parts(v):
    sigma = 0.5 * jnp.tanh(0.5 * v) + 0.5
    act = v * sigma
    return act, lambda: sigma + act * (1.0 - sigma)


def own(at, first, count):
    return jnp.where(jnp.logical_and(at >= first, at < first + count), at - first, count)


W1, W2, W3, W4L, W4E, W5L, W5S, WF = 0, 768, 1536, 2688, 4224, 4992, 6528, 7296
W6, W7, WB = 0, 1152, 2304
LIFT, SKIP, GRAD, COARSE, KEPT = 0, 864, 1728, 2448, 2832
SPARE = 2832
ROOM = 51200


def place(axis):
    at = lax.axis_index("row") if axis == 0 else 2 * lax.axis_index("colh") + lax.axis_index("core")
    last = 7 if axis == 0 else 15
    return at % 2 == 1, (at > 0).astype(F32), (at < last).astype(F32)


def beside(first, second):
    return jnp.concatenate([first.astype(F32), second.astype(F32)], axis=1)


def pack_x(active_hbm, feat_hbm, cot_hbm, p1, p2, active, feat, cot, sem):
    odd, _, _ = place(0)
    copies = [pltpu.make_async_copy(active_hbm, active, sem.at[0])]
    copies += [pltpu.make_async_copy(feat_hbm.at[k], feat.at[k], sem.at[1 + k]) for k in range(8)]
    copies += [pltpu.make_async_copy(cot_hbm.at[7 * k], cot.at[k], sem.at[9 + k]) for k in range(2)]
    for copy in copies:
        copy.start()
    for copy in copies:
        copy.wait()
    row = lax.broadcasted_iota(jnp.int32, (128, 64), 0)
    mask = jnp.where(row < 64, active[0], active[1]).astype(F32)
    row = lax.broadcasted_iota(jnp.int32, (16, 128), 0)
    ends = jnp.where(row < 8, active[0], active[1]).astype(F32).astype(BF16)
    for k in range(3):
        pair = beside(feat[2 * k + 1].astype(F32) * mask, feat[2 * k + 2].astype(F32) * mask).astype(BF16)
        p1[128 * k : 128 * k + 128] = pair
        p2[128 * k : 128 * k + 128] = pair
    for p, edge in ((p1, jnp.where(odd, 0, 1)), (p2, jnp.where(odd, 1, 0))):
        p[384:512] = beside(feat[7 * edge].astype(F32) * mask, cot[edge]).astype(BF16)
        p[512:528] = ends


def pack_y(cot, p1, p2, rz, rxz, xall, xmask, p3, p4):
    odd, v_lo, v_hi = place(0)

    def lo(rows):
        return jnp.where(odd, rz[rows].astype(F32), rxz[rows].astype(F32)) * v_lo

    def hi(rows):
        return jnp.where(odd, rxz[rows].astype(F32), rz[rows].astype(F32)) * v_hi

    for k in range(3):
        slab = slice(128 * k, 128 * k + 128)
        xall[k] = lo(slab).astype(BF16)
        xall[4 + k] = p1[slab]
        xall[8 + k] = hi(slab).astype(BF16)
        xall[12 + k] = beside(cot[2 * k + 1], cot[2 * k + 2]).astype(BF16)
    slab = slice(384, 512)
    edge_lo, edge_hi = lo(slab), hi(slab)
    first = jnp.where(odd, p1[slab].astype(F32), p2[slab].astype(F32))
    last = jnp.where(odd, p2[slab].astype(F32), p1[slab].astype(F32))
    xall[3] = beside(edge_lo[:, :64], first[:, :64]).astype(BF16)
    xall[7] = beside(last[:, :64], edge_hi[:, :64]).astype(BF16)
    xall[11] = beside(edge_lo[:, 64:], first[:, 64:]).astype(BF16)
    xall[15] = beside(last[:, 64:], edge_hi[:, 64:]).astype(BF16)
    xmask[0] = lo(slice(512, 528))
    xmask[1] = p1[512:528].astype(F32)
    xmask[2] = hi(slice(512, 528))
    odd_c, _, _ = place(1)
    for p, low in ((p3, odd_c), (p4, jnp.logical_not(odd_c))):
        for k in range(11):
            near = jnp.where(low, xall[k, 0:64].astype(F32), xall[k, 64:128].astype(F32))
            p[64 * k : 64 * k + 64] = near.astype(BF16)
        cols = []
        for k in range(11, 16):
            slab = xall[k].astype(F32)
            cols.append(jnp.where(low, slab[0:8], slab[120:128]))
        for k in range(3):
            cols.append(jnp.where(low, xmask[k, 0:8], xmask[k, 8:16]))
        p[704:768] = jnp.concatenate(cols, axis=0).astype(BF16)


def forward(
    xall, xmask, r3, r4, weights_hbm,
    decoded_hbm, slope_ef, g_skip, slope_ec, g_dc, s_in, s_pool, kept_hbm,
    mm, cc, s1, ee, s2, s3, slope_dc, s4, acc, weights, kept, decoded, w_sem, out_sem,
):
    cuts = (W1, W2, W3, W4L, W4E, W5L, W5S, WF)
    loads = []
    for k in range(7):
        rows = pl.ds(cuts[k], cuts[k + 1] - cuts[k])
        loads.append(pltpu.make_async_copy(weights_hbm.at[rows], weights.at[rows], w_sem.at[k]))
    loads[0].start()
    stores = []

    def store(first, end):
        rows = pl.ds(first, end - first)
        stores.append(pltpu.make_async_copy(kept.at[rows], kept_hbm.at[rows], out_sem.at[len(stores)]))
        stores[-1].start()

    odd, v_lo, v_hi = place(1)

    def lo(at, rows):
        at = pl.ds(at, rows)
        return (jnp.where(odd, r3[at].astype(F32), r4[at].astype(F32)) * v_lo).reshape(rows // 8, 8, 128)

    def hi(at, rows):
        at = pl.ds(at, rows)
        return (jnp.where(odd, r4[at].astype(F32), r3[at].astype(F32)) * v_hi).reshape(rows // 8, 8, 128)

    extra_lo, extra_hi = lo(704, 64), hi(704, 64)
    for k in range(5):
        cc[k, 0] = extra_lo[k]
        cc[k, 1:17] = xall[11 + k].astype(F32).reshape(16, 8, 128)
        cc[k, 17] = extra_hi[k]
    for k in range(3):
        mm[k, 0:6] = jnp.broadcast_to(extra_lo[5 + k][None], (6, 8, 128))
        mm[k, 6:14] = jnp.broadcast_to(xmask[k, 0:8][None], (8, 8, 128))
        mm[k, 14:22] = jnp.broadcast_to(xmask[k, 8:16][None], (8, 8, 128))
        mm[k, 22:28] = jnp.broadcast_to(extra_hi[5 + k][None], (6, 8, 128))

    def spread(i, _):
        at = pl.multiple_of(64 * i, 64)
        v = jnp.concatenate([lo(at, 64), xall[i].astype(F32).reshape(16, 8, 128), hi(at, 64)], axis=0)
        s1[i] = taps_y(v[1:31], 28)

        s_in[own(i, 3, 5)] = taps_y(v[7:25], 16)
        return 0

    lax.fori_loop(0, 11, spread, 0, unroll=True)
    for copy in loads[1:]:
        copy.start()

    loads[0].wait()

    def encode(i, pre):
        mask = mm[jnp.where(i < 3, 0, jnp.where(i < 7, 1, 2))]
        act, slope = silu_parts(pre)
        v = bround(act * mask)
        ee[i] = v

        slope_ef[own(i, 3, 4)] = (slope() * mask)[6:22].reshape(128, 128)

        s = v.reshape(14, 2, 8, 128)
        s = s[:, 0] + s[:, 1]
        s = s + pltpu.roll(s, 64, 2)
        v = bround(halve_z(s) * 0.125)
        put_taps(s2, i, v, 12)

        put_taps(s_pool, own(i, 2, 6), v[2:12], 8)

    def encode_two(j, _):
        wide = jnp.concatenate([s1[pl.ds(2 * j, 2)], s1[pl.ds(2 * j + 1, 2)]], axis=2).reshape(448, 768)
        pre = fold128(dot(wide, weights[W1:W2])).reshape(2, 28, 8, 128)
        for k in range(2):
            encode(2 * j + k, pre[k])
        return 0

    lax.fori_loop(0, 5, encode_two, 0, unroll=True)

    def mask_coarse(block, first, count):
        m = mm[block].reshape(14, 2, 8, 128)[first : first + count, 0]
        return jnp.where(z_of(m.shape) < 4, m, 0.0)

    loads[1].wait()

    def encode2(i, _):
        wide = jnp.concatenate([s2[pl.ds(4 * i + a, 4)] for a in range(3)], axis=2).reshape(384, 768)
        pre = fold128(dot(wide, weights[W2:W3])).reshape(4, 12, 8, 128)
        for k in range(4):
            x = 4 * i + k
            mask = mask_coarse(jnp.where(x < 2, 0, jnp.where(x < 6, 1, 2)), 1, 12)
            act, slope = silu_parts(pre[k])
            v = bround(act * mask)
            s3[x] = taps_y(v, 10)

            slope_ec[own(x, 1, 6)] = (slope() * mask)[1:11].reshape(80, 128)
            kept[pl.ds(pl.multiple_of(COARSE + 64 * own(x, 1, 6), 16), 64)] = taps_y(v[1:11], 8)
        return 0

    lax.fori_loop(0, 2, encode2, 0, unroll=True)
    store(COARSE, KEPT)
    loads[2].wait()

    def decode2(i, _):
        wide = jnp.concatenate([s3[pl.ds(3 * i + a, 3)] for a in range(3)], axis=2).reshape(240, 1152)
        pre = fold128(dot(wide, weights[W3:W4L])).reshape(3, 10, 8, 128)
        for k in range(3):
            x = 3 * i + k
            mask = mask_coarse(jnp.where(x < 1, 0, jnp.where(x < 5, 1, 2)), 2, 10)
            act, slope = silu_parts(pre[k])
            v = double_z(bround(act * mask))
            up = jnp.concatenate([v[:, None], v[:, None]], axis=1).reshape(20, 8, 128)
            kept[pl.ds(pl.multiple_of(LIFT + 144 * x, 144), 144)] = taps_y(up, 18)

            slope_dc[own(x, 1, 4)] = (slope() * mask)[1:9]
        return 0

    lax.fori_loop(0, 2, decode2, 0, unroll=True)

    def skip(i, _):
        kept[pl.ds(pl.multiple_of(SKIP + 144 * i, 144), 144)] = taps_y(ee[i + 2, 4:24], 18)
        return 0

    lax.fori_loop(0, 6, skip, 0, unroll=True)

    store(LIFT, GRAD)
    loads[3].wait()
    loads[4].wait()
    def both(first):
        return jnp.concatenate([kept[first : first + 720], kept[first + 144 : first + 864]], axis=1)

    def taps(first, step):
        return jnp.concatenate([weights[first : first + 384], weights[first + step : first + step + 384]], axis=1)

    lifted = both(LIFT)
    wide = jnp.concatenate([lifted, lifted, both(SKIP)], axis=1)
    acc[...] = dot_n(wide, jnp.concatenate([taps(W4L, 768), taps(W4L + 384, 768), taps(W4E, 384)], axis=1))

    def decode(i, _):
        pre = fold128(acc[pl.ds(pl.multiple_of(144 * i, 144), 144)])
        lane = lax.broadcasted_iota(jnp.int32, (18, 8, 128), 2)
        before, after = jnp.where(i < 1, 0, 1), jnp.where(i < 4, 1, 2)
        mask = jnp.where(lane < 64, mm[before, 5:23], mm[after, 5:23])
        act, slope = silu_parts(pre)
        g = bround(cc[i] * mask * slope())
        s4[i] = taps_y(g, 16)
        out = (act * mask)[1:17].reshape(128, 128).astype(BF16)

        decoded[own(2 * i - 1, 0, 8)] = out[:, :64]
        decoded[own(2 * i, 0, 8)] = out[:, 64:]
        inside = jnp.logical_and(jnp.logical_or(lane >= 64, i > 0), jnp.logical_or(lane < 64, i < 4))
        g = jnp.where(inside, g, 0.0)
        zero = jnp.zeros((1, 8, 128), F32)
        kept[pl.ds(pl.multiple_of(GRAD + 144 * i, 144), 144)] = taps_z(
            jnp.concatenate([zero, g[1:17], zero], axis=0)
        )
        return 0

    lax.fori_loop(0, 5, decode, 0, unroll=True)
    store(GRAD, COARSE)
    stores.append(pltpu.make_async_copy(decoded.at[pl.ds(0, 8)], decoded_hbm, out_sem.at[3]))
    stores[-1].start()
    loads[5].wait()
    loads[6].wait()

    def back(i, _):
        wide = jnp.concatenate([s4[pl.ds(2 * i, 2)], s4[pl.ds(2 * i + 1, 2)]], axis=2).reshape(256, 768)
        g_skip[pl.ds(2 * i, 2)] = fold128(dot(wide, weights[W5S:WF])).reshape(2, 128, 128)
        up = dot(wide, weights[W5L : W5L + 768]) + dot(wide, weights[W5L + 768 : W5S])
        up = up.reshape(16, 2, 8, 384)
        g = halve_z(fold128((up[:, 0] + up[:, 1]).reshape(128, 384)))
        g = g.reshape(2, 8, 8, 128) * slope_dc[pl.ds(2 * i, 2)]
        g_dc[pl.ds(2 * i, 2)] = g.reshape(2, 64, 128).astype(BF16)
        return 0

    lax.fori_loop(0, 2, back, 0, unroll=True)
    for copy in stores:
        copy.wait()


def unhalve(both):
    return jnp.concatenate([both[:, :64], both[:, 64:]], axis=0)


A_SKIP, A_SKIP2 = 864, 1152
B_FINE, B_FINE2 = 864, 1152


def put_parts(wire, first, rows, block):
    for h in range(2):
        wire[h, first : first + rows] = block[rows * h : rows * h + rows]


def put_three(wire, at, at2, taps):
    lane = lax.broadcasted_iota(jnp.int32, (192, 128), 1)
    two = jnp.where(lane < 64, taps[0][0], taps[1][1]).astype(BF16)
    for k in range(3):
        put_parts(wire, at + 32 * k, 32, two[64 * k : 64 * k + 64])
    for h in range(2):
        low = jnp.concatenate([taps[2][0][64 * k + 32 * h : 64 * k + 32 * h + 32] for k in range(3)], axis=0)
        high = jnp.concatenate([taps[2][1][64 * k + 32 * h : 64 * k + 32 * h + 32] for k in range(3)], axis=0)
        wire[h, at2 : at2 + 48] = jnp.where(lane[:48] < 64, low[:48], high[48:]).astype(BF16)


def split_wire(wire, keep, send):
    core = lax.axis_index("core")
    keep[...] = wire[core]
    send[...] = wire[1 - core]


def fetch(kept_hbm, kept, first, end, sem):
    copy = pltpu.make_async_copy(kept_hbm.at[pl.ds(first, end - first)], kept, sem)
    copy.start()
    return copy


def weights_fine(kept_hbm, keep, send, wire, kept, sem):
    copies = [
        fetch(kept_hbm, kept.at[pl.ds(first, end - first)], first, end, sem.at[k])
        for k, (first, end) in enumerate(((LIFT, SKIP), (SKIP, GRAD), (GRAD, COARSE)))
    ]
    for copy in copies:
        copy.wait()
    grad = kept[GRAD:COARSE]
    up = [(dot_t(grad, kept[LIFT + 144 * p : LIFT + 144 * p + 720]) * FACTOR).reshape(3, 2, 64, 384) for p in range(2)]
    same = [(dot_t(grad, kept[SKIP + 144 * p : SKIP + 144 * p + 720]) * FACTOR).reshape(3, 2, 64, 384) for p in range(2)]
    for a, (p, q) in enumerate(((0, 0), (0, 1), (1, 0))):
        p2, q2 = (0, 1) if a == 0 else (1, a - 1)
        lifted = (up[p][:, 0] + up[p2][:, 1]).reshape(192, 384).astype(BF16)
        for b in range(3):
            for c in range(3):
                at = 32 * (9 * a + 3 * b + c)
                put_parts(wire, at, 32, lifted[64 * c : 64 * c + 64, 128 * b : 128 * b + 128])
        taps = []
        for b in range(3):
            lanes = slice(128 * b, 128 * b + 128)
            taps.append(add_halves(same[p][:, 0, :, lanes].reshape(192, 128), q, same[p2][:, 1, :, lanes].reshape(192, 128), q2))
        put_three(wire, A_SKIP + 96 * a, A_SKIP2 + 48 * a, taps)
    split_wire(wire, keep, send)


def weights_coarse(kept_hbm, g_dc, keep, send, token, wire, kept, sem):
    copy = fetch(kept_hbm, kept, COARSE, KEPT, sem.at[0])
    gc = taps_z(g_dc[...].astype(F32).reshape(32, 8, 128))
    copy.wait()
    for a in range(3):
        res = (dot_t(kept[64 * a : 64 * a + 256], gc) * FACTOR).astype(BF16)
        for b in range(3):
            for c in range(3):
                at = 64 * (9 * a + 3 * b + c)
                put_parts(wire, at, 64, res[128 * b : 128 * b + 128, 128 * c : 128 * c + 128])
    split_wire(wire, keep, send)
    token[0, 0] = jnp.int32(0)


def add_halves(first, q, second, q2):
    low = (first if q == 0 else pltpu.roll(first, 64, 1)) + (second if q2 == 0 else pltpu.roll(second, 64, 1))
    high = (first if q == 1 else pltpu.roll(first, 64, 1)) + (second if q2 == 1 else pltpu.roll(second, 64, 1))
    return low, high


def back_encode(gx, slope_ec, s_pool, s_in, g_skip, slope_ef, weights, keep, send, s5, ge, gz, wire):
    for x in range(8):
        s5[x] = taps_y(gx[x].astype(F32).reshape(12, 8, 128), 10)

    def taps(first):
        return jnp.concatenate([weights[first + 384 * a : first + 384 * a + 384] for a in range(3)], axis=1)

    acc = dot_n(jnp.concatenate([s5[a : a + 6] for a in range(3)], axis=2).reshape(480, 1152), taps(W6))
    g_ec = bround(fold128(acc) * slope_ec[0:6].reshape(60, 8, 128)).reshape(6, 10, 8, 128)
    for x in range(6):
        ge[x] = taps_y(g_ec[x], 8)
    gc = taps_z(g_ec[1:5, 1:9].reshape(32, 8, 128))
    acc = dot_n(jnp.concatenate([ge[a : a + 4] for a in range(3)], axis=2).reshape(256, 1152), taps(W7))
    up = double_z(fold128(acc) * 0.125)
    up = jnp.concatenate([up[:, None], up[:, None]], axis=1).reshape(4, 16, 8, 128)
    for x in range(4):
        g = (g_skip[x].reshape(16, 8, 128) + up[x]) * slope_ef[x].reshape(16, 8, 128)
        gz[x] = taps_z(bround(g))
    gf = gz[...].reshape(512, 384)
    parts = [(dot_t(s_in[p : p + 4].reshape(512, 384), gf) * FACTOR).reshape(3, 2, 64, 384) for p in range(2)]
    for a, (p, q) in enumerate(((0, 0), (0, 1), (1, 0))):
        p2, q2 = (0, 1) if a == 0 else (1, a - 1)
        taps = []
        for c in range(3):
            lanes = slice(128 * c, 128 * c + 128)
            taps.append(add_halves(parts[p][:, q, :, lanes].reshape(192, 128), 0, parts[p2][:, q2, :, lanes].reshape(192, 128), 1))
        put_three(wire, B_FINE + 96 * a, B_FINE2 + 48 * a, taps)
        res = (dot_t(s_pool[a : a + 4].reshape(256, 256), gc) * FACTOR).astype(BF16)
        for b in range(3):
            for c in range(3):
                at = 32 * (9 * a + 3 * b + c)
                put_parts(wire, at, 32, res[64 * b : 64 * b + 64, 128 * c : 128 * c + 128])
    split_wire(wire, keep, send)


def unpack(of_this_core, total, *refs):
    df_hbm, dc_hbm, ef_hbm, ec_hbm, d_df, d_dc, d_ef, d_ec, sem = refs[-9:]
    core = lax.axis_index("core")
    half = core if of_this_core else 1 - core
    wire = total[...].reshape(64 * CHUNK, 128)
    wire_a, wire_c, wire_b = wire[:ROWS_F], wire[ROWS_F : ROWS_F + ROWS_C], wire[ROWS_F + ROWS_C :]
    stores = []

    def store(src, dst, a):
        rows = src.shape[1]
        at = pl.ds(pl.multiple_of(half * rows, rows), rows)
        taps = pl.ds(9 * a, 9)
        stores.append(pltpu.make_async_copy(src.at[taps], dst.at[taps, at], sem.at[len(stores)]))
        stores[-1].start()

    def three(wire, at, at2):
        two = wire[at : at + 96].astype(F32)
        return two[:, :64], two[:, 64:], unhalve(wire[at2 : at2 + 48].astype(F32))

    for a in range(3):
        taps = slice(9 * a, 9 * a + 9)
        d_dc[taps] = wire_c[576 * a : 576 * a + 576].astype(F32).reshape(9, 64, 128)
        store(d_dc, dc_hbm, a)
        skip = three(wire_a, A_SKIP + 96 * a, A_SKIP2 + 48 * a)
        fine = three(wire_b, B_FINE + 96 * a, B_FINE2 + 48 * a)
        d_df[taps, :, :128] = wire_a[288 * a : 288 * a + 288].astype(F32).reshape(9, 32, 128)
        for b in range(3):
            for c in range(3):
                k = 9 * a + 3 * b + c
                d_df[k, :, 128:] = skip[b][32 * c : 32 * c + 32]
                d_ef[k] = fine[c][32 * b : 32 * b + 32]
        store(d_df, df_hbm, a)
        store(d_ef, ef_hbm, a)
        d_ec[taps] = wire_b[288 * a : 288 * a + 288].astype(F32).reshape(9, 32, 128)
        store(d_ec, ec_hbm, a)
    for copy in stores:
        copy.wait()


def arrange_back(e2, d3, wb):
    for a in range(3):
        for b in range(3):
            coarse = slice(128 * b, 128 * b + 128)
            for c in range(3):
                k = 9 * a + 3 * b + c
                at = 384 * a + 128 * c
                wb[W6 + at : W6 + at + 128, coarse] = d3[26 - k]
                wb[W7 + at : W7 + at + 64, coarse] = e2[26 - k]
                wb[W7 + at + 64 : W7 + at + 128, coarse] = e2[26 - k]


def arrange(e1, e2, d3, d4, wf_hbm, wf, sem):
    for a in range(3):
        for b in range(3):
            coarse = slice(128 * b, 128 * b + 128)
            for c in range(3):
                k = 9 * a + 3 * b + c
                lanes = slice(128 * c, 128 * c + 128)
                wf[W2 + 256 * a + 64 * b : W2 + 256 * a + 64 * b + 64, lanes] = e2[k]
                wf[W3 + 384 * a + 128 * b : W3 + 384 * a + 128 * b + 128, lanes] = d3[k]
        wf[W2 + 256 * a + 192 : W2 + 256 * a + 256] = jnp.zeros((64, 384), BF16)
    copies = []

    def copy_out(first, rows):
        at = pl.ds(first, rows)
        copies.append(pltpu.make_async_copy(wf.at[at], wf_hbm.at[at], sem.at[len(copies)]))
        copies[-1].start()

    copy_out(W2, W4L - W2)
    none = jnp.zeros((64, 64), F32)

    def tap(ref, a, rest, lanes, turned=False):
        if a < 0 or a > 2:
            return none
        k = 9 * a + rest
        return ref[26 - k if turned else k, :, lanes].astype(F32)

    all_, low, high = slice(0, 64), slice(0, 128), slice(128, 192)
    for p in range(2):
        for b in range(3):
            for c in range(3):
                rest = 3 * b + c
                lanes = slice(128 * c, 128 * c + 128)
                for q in range(2):
                    at = 384 * p + 128 * b + 64 * q
                    a = 2 * p + q
                    wf[W1 + at : W1 + at + 64, lanes] = beside(tap(e1, a, rest, all_), tap(e1, a - 1, rest, all_)).astype(BF16)
                    wf[W5S + at : W5S + at + 64, lanes] = beside(
                        tap(d4, a, rest, high, True), tap(d4, a - 1, rest, high, True)
                    ).astype(BF16)
                    for o in range(2):
                        to = W5L + 768 * o + at
                        to2 = W4L + 384 * (2 * p + q) + 128 * c + 64 * o
                        coarse = slice(128 * b, 128 * b + 128)
                        if 0 <= a - o <= 2:
                            wf[to : to + 64, lanes] = d4[26 - 9 * (a - o) - rest, :, low]
                            wf[to2 : to2 + 64, coarse] = d4[9 * (a - o) + rest, :, low]
                        else:
                            wf[to : to + 64, lanes] = jnp.zeros((64, 128), BF16)
                            wf[to2 : to2 + 64, coarse] = jnp.zeros((64, 128), BF16)
                for o in range(2):
                    at = W4E + 384 * p + 128 * c + 64 * o
                    wf[at : at + 64, 128 * b : 128 * b + 128] = beside(
                        tap(d4, 2 * p - o, rest, high), tap(d4, 2 * p + 1 - o, rest, high)
                    ).astype(BF16)
        for first, rows in ((W1, 384), (W4L, 768), (W4E, 384), (W5L, 384), (W5L + 384, 384), (W5S, 384)):
            copy_out(first + rows * p if first != W5L + 384 else W5L + 768 + 384 * p, rows)
    for copy in copies:
        copy.wait()


def swap(v, pairs):
    return lax.ppermute(v, ("row", "colh", "core"), pairs)


def body(
    features, block_active, encode_fine, encode_coarse, decode_coarse, decode_fine, out_cotangent
):
    row = lax.axis_index("row")
    core = lax.axis_index("core")
    col = 2 * lax.axis_index("colh") + core
    at = [(r, c) for r in range(8) for c in range(16)]

    def up(i, n):
        return (i + 1) % n if i % 2 else (i - 1) % n

    swap_z = [(16 * r + c, 16 * (r ^ 1) + c) for r, c in at]
    swap_xz = [(16 * r + c, 16 * up(r, 8) + c) for r, c in at]
    swap_core = [(16 * r + c, 16 * r + (c ^ 1)) for r, c in at]
    swap_yz = [(16 * r + c, 16 * r + up(c, 16)) for r, c in at]

    odd_r, odd_c = row % 2, core
    active = block_active.reshape(2)
    e2 = encode_coarse.reshape(27, 64, 128)
    d3 = decode_coarse.reshape(27, 128, 128)
    d4 = jnp.transpose(decode_fine, (0, 1, 2, 4, 3)).reshape(27, 64, 192)
    (w_forward,) = call(
        arrange,
        [((ROOM, 384), BF16, HB)],
        [VM] * 4,
        scratch=[pltpu.VMEM((WF, 384), BF16), pltpu.SemaphoreType.DMA((13,))],
    )(encode_fine.reshape(27, 64, 64), e2, d3, d4)
    (w_backward,) = call(arrange_back, [((WB, 384), BF16)], [VM] * 2)(e2, d3)

    feat = features.reshape(8, 128, 64)
    cot = out_cotangent.reshape(8, 128, 64)
    p1, p2 = call(
        pack_x,
        [((528, 128), BF16)] * 2,
        [HB] * 3,
        scratch=[
            pltpu.SMEM((2,), jnp.int32),
            pltpu.VMEM((8, 128, 64), BF16),
            pltpu.VMEM((2, 128, 64), BF16),
            pltpu.SemaphoreType.DMA((11,)),
        ],
    )(active, feat, cot)
    rxz = swap(p2, swap_xz)
    rz = swap(p1, swap_z)
    rz, w_forward = lax.optimization_barrier((rz, w_forward))
    xall, xmask, p3, p4 = call(
        pack_y,
        [((16, 128, 128), BF16), ((3, 16, 128), F32), ((768, 128), BF16), ((768, 128), BF16)],
        [VM] * 5,
        limit=8,
    )(cot, p1, p2, rz, rxz)
    r4 = swap(p4, swap_yz)
    r3 = swap(p3, swap_core)
    r3, w_backward = lax.optimization_barrier((r3, w_backward))

    decoded, slope_ef, g_skip, slope_ec, g_dc, s_in, s_pool, kept = call(
        forward,
        [
            ((8, 128, 64), BF16, HB),
            ((5, 128, 128), F32),
            ((4, 128, 128), F32),
            ((7, 80, 128), F32),
            ((4, 64, 128), BF16),
            ((6, 128, 384), BF16),
            ((7, 64, 256), BF16),
            ((ROOM, 384), BF16, HB),
        ],
        [VM] * 4 + [HB],
        scratch=[
            pltpu.VMEM((3, 28, 8, 128), F32),
            pltpu.VMEM((5, 18, 8, 128), F32),
            pltpu.VMEM((11, 224, 384), BF16),
            pltpu.VMEM((10, 28, 8, 128), F32),
            pltpu.VMEM((10, 96, 256), BF16),
            pltpu.VMEM((8, 80, 384), BF16),
            pltpu.VMEM((5, 8, 8, 128), F32),
            pltpu.VMEM((5, 128, 384), BF16),
            pltpu.VMEM((720, 384), F32),
            pltpu.VMEM((WF, 384), BF16),
            pltpu.VMEM((SPARE + 64, 384), BF16),
            pltpu.VMEM((9, 128, 64), BF16),
            pltpu.SemaphoreType.DMA((7,)),
            pltpu.SemaphoreType.DMA((4,)),
        ],
        flops=4_000_000_000,
        limit=26,
    )(xall, xmask, r3, r4, w_forward)

    def add(keep, got):
        return (keep.astype(F32) + got.astype(F32)).astype(BF16)

    keep_f, send_f = call(
        weights_fine,
        [((ROWS_F, 128), BF16)] * 2,
        [HB],
        scratch=[
            pltpu.VMEM((2, ROWS_F, 128), BF16),
            pltpu.VMEM((COARSE, 384), BF16),
            pltpu.SemaphoreType.DMA((3,)),
        ],
        flops=1_000_000_000,
        limit=26,
    )(kept)
    keep_c, send_c, token = call(
        weights_coarse,
        [((ROWS_C, 128), BF16), ((ROWS_C, 128), BF16), ((1, 1), jnp.int32, SM)],
        [HB, VM],
        scratch=[
            pltpu.VMEM((2, ROWS_C, 128), BF16),
            pltpu.VMEM((KEPT - COARSE, 384), BF16),
            pltpu.SemaphoreType.DMA((1,)),
        ],
        flops=300_000_000,
        limit=26,
    )(kept, g_dc)

    is_odd = odd_r == 1
    q2 = swap(jnp.where(is_odd, g_dc[2:], g_dc[:2]), swap_xz)
    q1 = swap(jnp.where(is_odd, g_dc[:2], g_dc[2:]), swap_z)
    zero = jnp.zeros_like(q1)
    before = jnp.where(row > 0, jnp.where(is_odd, q1, q2), zero)
    after = jnp.where(row < 7, jnp.where(is_odd, q2, q1), zero)
    gx = jnp.concatenate([before, g_dc, after], axis=0)
    is_odd = odd_c + token[0, 0] == 1
    q4 = swap(jnp.where(is_odd, gx[:, 48:], gx[:, :16]), swap_yz)
    q3 = swap(jnp.where(is_odd, gx[:, :16], gx[:, 48:]), swap_core)
    zero = jnp.zeros_like(q3)
    before = jnp.where(col > 0, jnp.where(is_odd, q3, q4), zero)
    after = jnp.where(col < 15, jnp.where(is_odd, q4, q3), zero)
    gx = jnp.concatenate([before, gx, after], axis=1)
    gx, keep_f = lax.optimization_barrier((gx, keep_f))


    keep_b, send_b = call(
        back_encode,
        [((ROWS_B, 128), BF16)] * 2,
        [VM] * 7,
        scratch=[
            pltpu.VMEM((8, 80, 384), BF16),
            pltpu.VMEM((6, 64, 384), BF16),
            pltpu.VMEM((4, 128, 384), BF16),
            pltpu.VMEM((2, ROWS_B, 128), BF16),
        ],
        flops=500_000_000,
        limit=20,
    )(gx, slope_ec, s_pool, s_in, g_skip, slope_ef, w_backward)
    sums = [add(keep, swap(send, swap_core)) for keep, send in ((keep_f, send_f), (keep_c, send_c), (keep_b, send_b))]

    chips = ("row", "colh")
    half = jnp.pad(jnp.concatenate(sums, axis=0), ((0, 64 * CHUNK - 4320), (0, 0))).reshape(64, CHUNK, 128)
    terms = lax.all_to_all(half, chips, 0, 0, tiled=True)
    total = jnp.sum(terms.astype(F32), axis=0).astype(BF16)
    mine = lax.all_to_all(jnp.broadcast_to(total[None], (64, CHUNK, 128)), chips, 0, 0, tiled=True)
    other = swap(mine, swap_core)
    shapes = ((27, 64, 192), (27, 128, 128), (27, 64, 64), (27, 64, 128))
    halves = ((27, 32, 192), (27, 64, 128), (27, 32, 64), (27, 32, 128))
    grads = []
    for of_this_core, values in ((True, mine), (False, other)):
        grads = call(
            functools.partial(unpack, of_this_core),
            [(shape, F32, HB) for shape in shapes],
            [VM] + [HB] * len(grads),
            scratch=[pltpu.VMEM(shape, F32) for shape in halves] + [pltpu.SemaphoreType.DMA((12,))],
            limit=24,
            aliases={1 + k: k for k in range(len(grads))},
        )(values, *grads)
    d_df, d_dc, d_ef, d_ec = grads
    return (
        decoded.reshape(8, 16, 8, 64),
        d_ef.reshape(3, 3, 3, 64, 64),
        d_ec.reshape(3, 3, 3, 64, 128),
        d_dc.reshape(3, 3, 3, 128, 128),
        jnp.transpose(d_df.reshape(3, 3, 3, 64, 192), (0, 1, 2, 4, 3)),
    )


def solution(mesh):
    split = Mesh(mesh.devices.reshape(8, 8, 2), ("row", "colh", "core"))
    field = P("row", ("colh", "core"), None, None)
    return jax.shard_map(
        body,
        mesh=split,
        in_specs=(field, P("row", ("colh", "core"), None), P(), P(), P(), P(), field),
        out_specs=(field, P(), P(), P(), P()),
        check_vma=False,
    )
```

```python
import functools
import math

import jax
import jax.numpy as jnp
from jax import lax
from jax.experimental import pallas as pl
from jax.experimental.pallas import tpu as pltpu
from jax.sharding import Mesh, PartitionSpec as P

F32 = jnp.float32
BF16 = jnp.bfloat16
MIB = 1024 * 1024
VM = pl.BlockSpec(memory_space=pltpu.VMEM)
SM = pl.BlockSpec(memory_space=pltpu.SMEM)
HB = pl.BlockSpec(memory_space=pltpu.HBM)
FACTOR = 1.0 / math.sqrt(64 * 256 * 8)
CHUNK = 72
ROWS_F, ROWS_C, ROWS_B = 1296, 1728, 1296


def call(kernel, outs, ins, scratch=(), flops=0, limit=58, aliases=None):
    return pl.pallas_call(
        kernel,
        out_shape=[jax.ShapeDtypeStruct(o[0], o[1]) for o in outs],
        in_specs=list(ins),
        out_specs=[o[2] if len(o) > 2 else VM for o in outs],
        scratch_shapes=list(scratch),
        input_output_aliases=aliases or {},
        compiler_params=pltpu.CompilerParams(vmem_limit_bytes=int(limit * MIB)),
        cost_estimate=pl.CostEstimate(flops=flops, bytes_accessed=4_000_000, transcendentals=0),
    )


def dot(lhs, rhs):
    return jnp.dot(lhs, rhs, preferred_element_type=F32)


def dot_n(lhs, rhs):
    return lax.dot_general(lhs, rhs, (((1,), (1,)), ((), ())), preferred_element_type=F32)


def dot_t(lhs, rhs):
    return lax.dot_general(lhs, rhs, (((0,), (0,)), ((), ())), preferred_element_type=F32)


def bround(v):
    return v.astype(BF16).astype(F32)


def z_of(shape):
    return lax.broadcasted_iota(jnp.int32, shape, len(shape) - 2)


def z_later(v):
    return jnp.where(z_of(v.shape) > 0, pltpu.roll(v, 1, 1), 0.0)


def z_earlier(v):
    return jnp.where(z_of(v.shape) < 7, pltpu.roll(v, 7, 1), 0.0)


def fold128(acc):
    rows = acc.shape[0]
    cube = acc.reshape(rows // 8, 8, 384)
    return z_later(cube[..., :128]) + cube[..., 128:256] + z_earlier(cube[..., 256:])


def taps_y(v, count):
    depth = v.shape[2]
    wide = jnp.concatenate([v[b : b + count] for b in range(3)], axis=2)
    return wide.reshape(count * 8, 3 * depth).astype(BF16)


def put_taps(ref, at, v, count):
    low = lax.broadcasted_iota(jnp.int32, (count, 8, 128), 2) < 64
    two = jnp.where(low, v[:count], v[1 : count + 1])
    ref[at, :, :128] = two.reshape(count * 8, 128).astype(BF16)
    ref[at, :, 128:] = v[2 : count + 2].reshape(count * 8, 128).astype(BF16)


def taps_z(g):
    wide = jnp.concatenate([z_earlier(g), g, z_later(g)], axis=2)
    return wide.reshape(g.shape[0] * 8, 3 * g.shape[2]).astype(BF16)


def halve_z(s):
    pair = s + pltpu.roll(s, 7, 1)
    z = z_of(s.shape)
    out = jnp.where(z == 0, pair, 0.0)
    for zc in (1, 2, 3):
        out = jnp.where(z == zc, pltpu.roll(pair, 8 - zc, 1), out)
    return out


def double_z(u):
    z = z_of(u.shape)
    out = u
    for shift in (1, 2, 3, 4):
        out = jnp.where((z + 1) // 2 == shift, pltpu.roll(u, shift, 1), out)
    return out


def silu_parts(v):
    sigma = 0.5 * jnp.tanh(0.5 * v) + 0.5
    act = v * sigma
    return act, lambda: sigma + act * (1.0 - sigma)


def own(at, first, count):
    return jnp.where(jnp.logical_and(at >= first, at < first + count), at - first, count)


W1, W2, W3, W4L, W4E, W5L, W5S, WF = 0, 768, 1536, 2688, 4224, 4992, 6528, 7296
W6, W7, WB = 0, 1152, 2304
LIFT, SKIP, GRAD, COARSE, KEPT = 0, 864, 1728, 2448, 2832
SPARE = 2832
ROOM = 51200


def place(axis):
    at = lax.axis_index("row") if axis == 0 else 2 * lax.axis_index("colh") + lax.axis_index("core")
    last = 7 if axis == 0 else 15
    return at % 2 == 1, (at > 0).astype(F32), (at < last).astype(F32)


def beside(first, second):
    return jnp.concatenate([first.astype(F32), second.astype(F32)], axis=1)


def pack_x(active_hbm, feat_hbm, cot_hbm, p1, p2, active, feat, cot, sem):
    odd, _, _ = place(0)
    copies = [pltpu.make_async_copy(active_hbm, active, sem.at[0])]
    copies += [pltpu.make_async_copy(feat_hbm.at[k], feat.at[k], sem.at[1 + k]) for k in range(8)]
    copies += [pltpu.make_async_copy(cot_hbm.at[7 * k], cot.at[k], sem.at[9 + k]) for k in range(2)]
    for copy in copies:
        copy.start()
    copies[0].wait()
    row = lax.broadcasted_iota(jnp.int32, (128, 64), 0)
    mask = jnp.where(row < 64, active[0], active[1]).astype(F32)
    row = lax.broadcasted_iota(jnp.int32, (16, 128), 0)
    ends = jnp.where(row < 8, active[0], active[1]).astype(F32).astype(BF16)
    for k in range(3):
        copies[2 + 2 * k].wait()
        copies[3 + 2 * k].wait()
        pair = beside(feat[2 * k + 1].astype(F32) * mask, feat[2 * k + 2].astype(F32) * mask).astype(BF16)
        p1[128 * k : 128 * k + 128] = pair
        p2[128 * k : 128 * k + 128] = pair
    for k in (1, 8, 9, 10):
        copies[k].wait()
    for p, edge in ((p1, jnp.where(odd, 0, 1)), (p2, jnp.where(odd, 1, 0))):
        p[384:512] = beside(feat[7 * edge].astype(F32) * mask, cot[edge]).astype(BF16)
        p[512:528] = ends


def pack_y(cot, p1, p2, rz, rxz, xall, xmask, p3, p4):
    odd, v_lo, v_hi = place(0)

    def lo(rows):
        return jnp.where(odd, rz[rows].astype(F32), rxz[rows].astype(F32)) * v_lo

    def hi(rows):
        return jnp.where(odd, rxz[rows].astype(F32), rz[rows].astype(F32)) * v_hi

    for k in range(3):
        slab = slice(128 * k, 128 * k + 128)
        xall[k] = lo(slab).astype(BF16)
        xall[4 + k] = p1[slab]
        xall[8 + k] = hi(slab).astype(BF16)
        xall[12 + k] = beside(cot[2 * k + 1], cot[2 * k + 2]).astype(BF16)
    slab = slice(384, 512)
    edge_lo, edge_hi = lo(slab), hi(slab)
    first = jnp.where(odd, p1[slab].astype(F32), p2[slab].astype(F32))
    last = jnp.where(odd, p2[slab].astype(F32), p1[slab].astype(F32))
    xall[3] = beside(edge_lo[:, :64], first[:, :64]).astype(BF16)
    xall[7] = beside(last[:, :64], edge_hi[:, :64]).astype(BF16)
    xall[11] = beside(edge_lo[:, 64:], first[:, 64:]).astype(BF16)
    xall[15] = beside(last[:, 64:], edge_hi[:, 64:]).astype(BF16)
    xmask[0] = lo(slice(512, 528))
    xmask[1] = p1[512:528].astype(F32)
    xmask[2] = hi(slice(512, 528))
    odd_c, _, _ = place(1)
    for p, low in ((p3, odd_c), (p4, jnp.logical_not(odd_c))):
        for k in range(11):
            near = jnp.where(low, xall[k, 0:64].astype(F32), xall[k, 64:128].astype(F32))
            p[64 * k : 64 * k + 64] = near.astype(BF16)
        cols = []
        for k in range(11, 16):
            slab = xall[k].astype(F32)
            cols.append(jnp.where(low, slab[0:8], slab[120:128]))
        for k in range(3):
            cols.append(jnp.where(low, xmask[k, 0:8], xmask[k, 8:16]))
        p[704:768] = jnp.concatenate(cols, axis=0).astype(BF16)


def forward(
    xall, xmask, r3, r4, weights_hbm,
    decoded_hbm, slope_ef, g_skip, slope_ec, g_dc, s_in, s_pool, kept_hbm,
    mm, cc, s1, ee, s2, s3, slope_dc, s4, acc, weights, kept, decoded, w_sem, out_sem,
):
    cuts = (W1, W2, W3, W4L, W4E, W5L, W5S, WF)
    loads = []
    for k in range(7):
        rows = pl.ds(cuts[k], cuts[k + 1] - cuts[k])
        loads.append(pltpu.make_async_copy(weights_hbm.at[rows], weights.at[rows], w_sem.at[k]))
    loads[0].start()
    stores = []

    def store(first, end):
        rows = pl.ds(first, end - first)
        stores.append(pltpu.make_async_copy(kept.at[rows], kept_hbm.at[rows], out_sem.at[len(stores)]))
        stores[-1].start()

    odd, v_lo, v_hi = place(1)

    def lo(at, rows):
        at = pl.ds(at, rows)
        return (jnp.where(odd, r3[at].astype(F32), r4[at].astype(F32)) * v_lo).reshape(rows // 8, 8, 128)

    def hi(at, rows):
        at = pl.ds(at, rows)
        return (jnp.where(odd, r4[at].astype(F32), r3[at].astype(F32)) * v_hi).reshape(rows // 8, 8, 128)

    extra_lo, extra_hi = lo(704, 64), hi(704, 64)
    for k in range(5):
        cc[k, 0] = extra_lo[k]
        cc[k, 1:17] = xall[11 + k].astype(F32).reshape(16, 8, 128)
        cc[k, 17] = extra_hi[k]
    for k in range(3):
        mm[k, 0:6] = jnp.broadcast_to(extra_lo[5 + k][None], (6, 8, 128))
        mm[k, 6:14] = jnp.broadcast_to(xmask[k, 0:8][None], (8, 8, 128))
        mm[k, 14:22] = jnp.broadcast_to(xmask[k, 8:16][None], (8, 8, 128))
        mm[k, 22:28] = jnp.broadcast_to(extra_hi[5 + k][None], (6, 8, 128))

    def spread(i, _):
        at = pl.multiple_of(64 * i, 64)
        v = jnp.concatenate([lo(at, 64), xall[i].astype(F32).reshape(16, 8, 128), hi(at, 64)], axis=0)
        s1[i] = taps_y(v[1:31], 28)

        s_in[own(i, 3, 5)] = taps_y(v[7:25], 16)
        return 0

    lax.fori_loop(0, 11, spread, 0, unroll=True)
    for copy in loads[1:]:
        copy.start()

    loads[0].wait()

    def encode(i, pre):
        mask = mm[jnp.where(i < 3, 0, jnp.where(i < 7, 1, 2))]
        act, slope = silu_parts(pre)
        v = bround(act * mask)
        ee[i] = v

        slope_ef[own(i, 3, 4)] = (slope() * mask)[6:22].reshape(128, 128)

        s = v.reshape(14, 2, 8, 128)
        s = s[:, 0] + s[:, 1]
        s = s + pltpu.roll(s, 64, 2)
        v = bround(halve_z(s) * 0.125)
        put_taps(s2, i, v, 12)

        put_taps(s_pool, own(i, 2, 6), v[2:12], 8)

    def encode_two(j, _):
        wide = jnp.concatenate([s1[pl.ds(2 * j, 2)], s1[pl.ds(2 * j + 1, 2)]], axis=2).reshape(448, 768)
        pre = fold128(dot(wide, weights[W1:W2])).reshape(2, 28, 8, 128)
        for k in range(2):
            encode(2 * j + k, pre[k])
        return 0

    lax.fori_loop(0, 5, encode_two, 0, unroll=True)

    def mask_coarse(block, first, count):
        m = mm[block].reshape(14, 2, 8, 128)[first : first + count, 0]
        return jnp.where(z_of(m.shape) < 4, m, 0.0)

    loads[1].wait()

    def encode2(i, _):
        wide = jnp.concatenate([s2[pl.ds(4 * i + a, 4)] for a in range(3)], axis=2).reshape(384, 768)
        pre = fold128(dot(wide, weights[W2:W3])).reshape(4, 12, 8, 128)
        for k in range(4):
            x = 4 * i + k
            mask = mask_coarse(jnp.where(x < 2, 0, jnp.where(x < 6, 1, 2)), 1, 12)
            act, slope = silu_parts(pre[k])
            v = bround(act * mask)
            s3[x] = taps_y(v, 10)

            slope_ec[own(x, 1, 6)] = (slope() * mask)[1:11].reshape(80, 128)
            kept[pl.ds(pl.multiple_of(COARSE + 64 * own(x, 1, 6), 16), 64)] = taps_y(v[1:11], 8)
        return 0

    lax.fori_loop(0, 2, encode2, 0, unroll=True)
    store(COARSE, KEPT)
    loads[2].wait()

    def decode2(i, _):
        wide = jnp.concatenate([s3[pl.ds(3 * i + a, 3)] for a in range(3)], axis=2).reshape(240, 1152)
        pre = fold128(dot(wide, weights[W3:W4L])).reshape(3, 10, 8, 128)
        for k in range(3):
            x = 3 * i + k
            mask = mask_coarse(jnp.where(x < 1, 0, jnp.where(x < 5, 1, 2)), 2, 10)
            act, slope = silu_parts(pre[k])
            v = double_z(bround(act * mask))
            up = jnp.concatenate([v[:, None], v[:, None]], axis=1).reshape(20, 8, 128)
            kept[pl.ds(pl.multiple_of(LIFT + 144 * x, 144), 144)] = taps_y(up, 18)

            slope_dc[own(x, 1, 4)] = (slope() * mask)[1:9]
        return 0

    lax.fori_loop(0, 2, decode2, 0, unroll=True)

    def skip(i, _):
        kept[pl.ds(pl.multiple_of(SKIP + 144 * i, 144), 144)] = taps_y(ee[i + 2, 4:24], 18)
        return 0

    lax.fori_loop(0, 6, skip, 0, unroll=True)

    store(LIFT, GRAD)
    loads[3].wait()
    loads[4].wait()
    def both(first):
        return jnp.concatenate([kept[first : first + 720], kept[first + 144 : first + 864]], axis=1)

    def taps(first, step):
        return jnp.concatenate([weights[first : first + 384], weights[first + step : first + step + 384]], axis=1)

    lifted = both(LIFT)
    wide = jnp.concatenate([lifted, lifted, both(SKIP)], axis=1)
    wide_taps = jnp.concatenate([taps(W4L, 768), taps(W4L + 384, 768), taps(W4E, 384)], axis=1)
    acc[0:288] = dot_n(wide[0:288], wide_taps)
    acc[288:720] = dot_n(wide[288:720], wide_taps)

    def decode(i, _):
        pre = fold128(acc[pl.ds(pl.multiple_of(144 * i, 144), 144)])
        lane = lax.broadcasted_iota(jnp.int32, (18, 8, 128), 2)
        before, after = jnp.where(i < 1, 0, 1), jnp.where(i < 4, 1, 2)
        mask = jnp.where(lane < 64, mm[before, 5:23], mm[after, 5:23])
        act, slope = silu_parts(pre)
        g = bround(cc[i] * mask * slope())
        s4[i] = taps_y(g, 16)
        out = (act * mask)[1:17].reshape(128, 128).astype(BF16)

        decoded[own(2 * i - 1, 0, 8)] = out[:, :64]
        decoded[own(2 * i, 0, 8)] = out[:, 64:]
        inside = jnp.logical_and(jnp.logical_or(lane >= 64, i > 0), jnp.logical_or(lane < 64, i < 4))
        g = jnp.where(inside, g, 0.0)
        zero = jnp.zeros((1, 8, 128), F32)
        kept[pl.ds(pl.multiple_of(GRAD + 144 * i, 144), 144)] = taps_z(
            jnp.concatenate([zero, g[1:17], zero], axis=0)
        )
        return 0

    lax.fori_loop(0, 5, decode, 0, unroll=True)
    store(GRAD, COARSE)
    stores.append(pltpu.make_async_copy(decoded.at[pl.ds(0, 8)], decoded_hbm, out_sem.at[3]))
    stores[-1].start()
    loads[5].wait()
    loads[6].wait()

    def back(i, _):
        wide = jnp.concatenate([s4[pl.ds(2 * i, 2)], s4[pl.ds(2 * i + 1, 2)]], axis=2).reshape(256, 768)
        g_skip[pl.ds(2 * i, 2)] = fold128(dot(wide, weights[W5S:WF])).reshape(2, 128, 128)
        up = dot(wide, weights[W5L : W5L + 768]) + dot(wide, weights[W5L + 768 : W5S])
        up = up.reshape(16, 2, 8, 384)
        g = halve_z(fold128((up[:, 0] + up[:, 1]).reshape(128, 384)))
        g = g.reshape(2, 8, 8, 128) * slope_dc[pl.ds(2 * i, 2)]
        g_dc[pl.ds(2 * i, 2)] = g.reshape(2, 64, 128).astype(BF16)
        return 0

    lax.fori_loop(0, 2, back, 0, unroll=True)
    for copy in stores:
        copy.wait()


def unhalve(both):
    return jnp.concatenate([both[:, :64], both[:, 64:]], axis=0)


A_SKIP, A_SKIP2 = 864, 1152
B_FINE, B_FINE2 = 864, 1152


def put_parts(wire, first, rows, block):
    for h in range(2):
        wire[h, first : first + rows] = block[rows * h : rows * h + rows]


def put_three(wire, at, at2, taps):
    lane = lax.broadcasted_iota(jnp.int32, (192, 128), 1)
    two = jnp.where(lane < 64, taps[0][0], taps[1][1]).astype(BF16)
    for k in range(3):
        put_parts(wire, at + 32 * k, 32, two[64 * k : 64 * k + 64])
    for h in range(2):
        low = jnp.concatenate([taps[2][0][64 * k + 32 * h : 64 * k + 32 * h + 32] for k in range(3)], axis=0)
        high = jnp.concatenate([taps[2][1][64 * k + 32 * h : 64 * k + 32 * h + 32] for k in range(3)], axis=0)
        wire[h, at2 : at2 + 48] = jnp.where(lane[:48] < 64, low[:48], high[48:]).astype(BF16)


def split_wire(wire, keep, send):
    core = lax.axis_index("core")
    keep[...] = wire[core]
    send[...] = wire[1 - core]


def fetch(kept_hbm, kept, first, end, sem):
    copy = pltpu.make_async_copy(kept_hbm.at[pl.ds(first, end - first)], kept, sem)
    copy.start()
    return copy


def weights_fine(kept_hbm, keep, send, wire, kept, sem):
    copies = [
        fetch(kept_hbm, kept.at[pl.ds(first, end - first)], first, end, sem.at[k])
        for k, (first, end) in enumerate(((GRAD, COARSE), (LIFT, SKIP), (SKIP, GRAD)))
    ]
    copies[0].wait()
    copies[1].wait()
    grad = kept[GRAD:COARSE]
    up = [(dot_t(grad, kept[LIFT + 144 * p : LIFT + 144 * p + 720]) * FACTOR).reshape(3, 2, 64, 384) for p in range(2)]
    copies[2].wait()
    same = [(dot_t(grad, kept[SKIP + 144 * p : SKIP + 144 * p + 720]) * FACTOR).reshape(3, 2, 64, 384) for p in range(2)]
    for a, (p, q) in enumerate(((0, 0), (0, 1), (1, 0))):
        p2, q2 = (0, 1) if a == 0 else (1, a - 1)
        lifted = (up[p][:, 0] + up[p2][:, 1]).reshape(192, 384).astype(BF16)
        for b in range(3):
            for c in range(3):
                at = 32 * (9 * a + 3 * b + c)
                put_parts(wire, at, 32, lifted[64 * c : 64 * c + 64, 128 * b : 128 * b + 128])
        taps = []
        for b in range(3):
            lanes = slice(128 * b, 128 * b + 128)
            taps.append(add_halves(same[p][:, 0, :, lanes].reshape(192, 128), q, same[p2][:, 1, :, lanes].reshape(192, 128), q2))
        put_three(wire, A_SKIP + 96 * a, A_SKIP2 + 48 * a, taps)
    split_wire(wire, keep, send)


def weights_coarse(kept_hbm, g_dc, keep, send, token, wire, kept, sem):
    copy = fetch(kept_hbm, kept, COARSE, KEPT, sem.at[0])
    gc = taps_z(g_dc[...].astype(F32).reshape(32, 8, 128))
    copy.wait()
    for a in range(3):
        res = (dot_t(kept[64 * a : 64 * a + 256], gc) * FACTOR).astype(BF16)
        for b in range(3):
            for c in range(3):
                at = 64 * (9 * a + 3 * b + c)
                put_parts(wire, at, 64, res[128 * b : 128 * b + 128, 128 * c : 128 * c + 128])
    split_wire(wire, keep, send)
    token[0, 0] = jnp.int32(0)


def add_halves(first, q, second, q2):
    low = (first if q == 0 else pltpu.roll(first, 64, 1)) + (second if q2 == 0 else pltpu.roll(second, 64, 1))
    high = (first if q == 1 else pltpu.roll(first, 64, 1)) + (second if q2 == 1 else pltpu.roll(second, 64, 1))
    return low, high


def back_encode(gx, slope_ec, s_pool, s_in, g_skip, slope_ef, weights, keep, send, s5, ge, gz, wire):
    for x in range(8):
        s5[x] = taps_y(gx[x].astype(F32).reshape(12, 8, 128), 10)

    def taps(first):
        return jnp.concatenate([weights[first + 384 * a : first + 384 * a + 384] for a in range(3)], axis=1)

    acc = dot_n(jnp.concatenate([s5[a : a + 6] for a in range(3)], axis=2).reshape(480, 1152), taps(W6))
    g_ec = bround(fold128(acc) * slope_ec[0:6].reshape(60, 8, 128)).reshape(6, 10, 8, 128)
    for x in range(6):
        ge[x] = taps_y(g_ec[x], 8)
    gc = taps_z(g_ec[1:5, 1:9].reshape(32, 8, 128))
    acc = dot_n(jnp.concatenate([ge[a : a + 4] for a in range(3)], axis=2).reshape(256, 1152), taps(W7))
    up = double_z(fold128(acc) * 0.125)
    up = jnp.concatenate([up[:, None], up[:, None]], axis=1).reshape(4, 16, 8, 128)
    for x in range(4):
        g = (g_skip[x].reshape(16, 8, 128) + up[x]) * slope_ef[x].reshape(16, 8, 128)
        gz[x] = taps_z(bround(g))
    gf = gz[...].reshape(512, 384)
    parts = [(dot_t(s_in[p : p + 4].reshape(512, 384), gf) * FACTOR).reshape(3, 2, 64, 384) for p in range(2)]
    for a, (p, q) in enumerate(((0, 0), (0, 1), (1, 0))):
        p2, q2 = (0, 1) if a == 0 else (1, a - 1)
        taps = []
        for c in range(3):
            lanes = slice(128 * c, 128 * c + 128)
            taps.append(add_halves(parts[p][:, q, :, lanes].reshape(192, 128), 0, parts[p2][:, q2, :, lanes].reshape(192, 128), 1))
        put_three(wire, B_FINE + 96 * a, B_FINE2 + 48 * a, taps)
        res = (dot_t(s_pool[a : a + 4].reshape(256, 256), gc) * FACTOR).astype(BF16)
        for b in range(3):
            for c in range(3):
                at = 32 * (9 * a + 3 * b + c)
                put_parts(wire, at, 32, res[64 * b : 64 * b + 64, 128 * c : 128 * c + 128])
    split_wire(wire, keep, send)


def unpack(of_this_core, total, *refs):
    df_hbm, dc_hbm, ef_hbm, ec_hbm, d_df, d_dc, d_ef, d_ec, sem = refs[-9:]
    core = lax.axis_index("core")
    half = core if of_this_core else 1 - core
    wire = total[...].reshape(64 * CHUNK, 128)
    wire_a, wire_c, wire_b = wire[:ROWS_F], wire[ROWS_F : ROWS_F + ROWS_C], wire[ROWS_F + ROWS_C :]
    stores = []

    def store(src, dst, a):
        rows = src.shape[1]
        at = pl.ds(pl.multiple_of(half * rows, rows), rows)
        taps = pl.ds(9 * a, 9)
        stores.append(pltpu.make_async_copy(src.at[taps], dst.at[taps, at], sem.at[len(stores)]))
        stores[-1].start()

    def three(wire, at, at2):
        two = wire[at : at + 96].astype(F32)
        return two[:, :64], two[:, 64:], unhalve(wire[at2 : at2 + 48].astype(F32))

    for a in range(3):
        taps = slice(9 * a, 9 * a + 9)
        d_dc[taps] = wire_c[576 * a : 576 * a + 576].astype(F32).reshape(9, 64, 128)
        store(d_dc, dc_hbm, a)
        skip = three(wire_a, A_SKIP + 96 * a, A_SKIP2 + 48 * a)
        fine = three(wire_b, B_FINE + 96 * a, B_FINE2 + 48 * a)
        d_df[taps, :, :128] = wire_a[288 * a : 288 * a + 288].astype(F32).reshape(9, 32, 128)
        for b in range(3):
            for c in range(3):
                k = 9 * a + 3 * b + c
                d_df[k, :, 128:] = skip[b][32 * c : 32 * c + 32]
                d_ef[k] = fine[c][32 * b : 32 * b + 32]
        store(d_df, df_hbm, a)
        store(d_ef, ef_hbm, a)
        d_ec[taps] = wire_b[288 * a : 288 * a + 288].astype(F32).reshape(9, 32, 128)
        store(d_ec, ec_hbm, a)
    for copy in stores:
        copy.wait()


def arrange_back(e2, d3, wb):
    for a in range(3):
        for b in range(3):
            coarse = slice(128 * b, 128 * b + 128)
            for c in range(3):
                k = 9 * a + 3 * b + c
                at = 384 * a + 128 * c
                wb[W6 + at : W6 + at + 128, coarse] = d3[26 - k]
                wb[W7 + at : W7 + at + 64, coarse] = e2[26 - k]
                wb[W7 + at + 64 : W7 + at + 128, coarse] = e2[26 - k]


def arrange(e1, e2, d3, d4, wf_hbm, wf, sem):
    for a in range(3):
        for b in range(3):
            coarse = slice(128 * b, 128 * b + 128)
            for c in range(3):
                k = 9 * a + 3 * b + c
                lanes = slice(128 * c, 128 * c + 128)
                wf[W2 + 256 * a + 64 * b : W2 + 256 * a + 64 * b + 64, lanes] = e2[k]
                wf[W3 + 384 * a + 128 * b : W3 + 384 * a + 128 * b + 128, lanes] = d3[k]
        wf[W2 + 256 * a + 192 : W2 + 256 * a + 256] = jnp.zeros((64, 384), BF16)
    copies = []

    def copy_out(first, rows):
        at = pl.ds(first, rows)
        copies.append(pltpu.make_async_copy(wf.at[at], wf_hbm.at[at], sem.at[len(copies)]))
        copies[-1].start()

    copy_out(W2, W4L - W2)
    none = jnp.zeros((64, 64), F32)

    def tap(ref, a, rest, lanes, turned=False):
        if a < 0 or a > 2:
            return none
        k = 9 * a + rest
        return ref[26 - k if turned else k, :, lanes].astype(F32)

    all_, low, high = slice(0, 64), slice(0, 128), slice(128, 192)
    for p in range(2):
        for b in range(3):
            for c in range(3):
                rest = 3 * b + c
                lanes = slice(128 * c, 128 * c + 128)
                for q in range(2):
                    at = 384 * p + 128 * b + 64 * q
                    a = 2 * p + q
                    wf[W1 + at : W1 + at + 64, lanes] = beside(tap(e1, a, rest, all_), tap(e1, a - 1, rest, all_)).astype(BF16)
                    wf[W5S + at : W5S + at + 64, lanes] = beside(
                        tap(d4, a, rest, high, True), tap(d4, a - 1, rest, high, True)
                    ).astype(BF16)
                    for o in range(2):
                        to = W5L + 768 * o + at
                        to2 = W4L + 384 * (2 * p + q) + 128 * c + 64 * o
                        coarse = slice(128 * b, 128 * b + 128)
                        if 0 <= a - o <= 2:
                            wf[to : to + 64, lanes] = d4[26 - 9 * (a - o) - rest, :, low]
                            wf[to2 : to2 + 64, coarse] = d4[9 * (a - o) + rest, :, low]
                        else:
                            wf[to : to + 64, lanes] = jnp.zeros((64, 128), BF16)
                            wf[to2 : to2 + 64, coarse] = jnp.zeros((64, 128), BF16)
                for o in range(2):
                    at = W4E + 384 * p + 128 * c + 64 * o
                    wf[at : at + 64, 128 * b : 128 * b + 128] = beside(
                        tap(d4, 2 * p - o, rest, high), tap(d4, 2 * p + 1 - o, rest, high)
                    ).astype(BF16)
        for first, rows in ((W1, 384), (W4L, 768), (W4E, 384), (W5L, 384), (W5L + 384, 384), (W5S, 384)):
            copy_out(first + rows * p if first != W5L + 384 else W5L + 768 + 384 * p, rows)
    for copy in copies:
        copy.wait()


def swap(v, pairs):
    return lax.ppermute(v, ("row", "colh", "core"), pairs)


def body(
    features, block_active, encode_fine, encode_coarse, decode_coarse, decode_fine, out_cotangent
):
    row = lax.axis_index("row")
    core = lax.axis_index("core")
    col = 2 * lax.axis_index("colh") + core
    at = [(r, c) for r in range(8) for c in range(16)]

    def up(i, n):
        return (i + 1) % n if i % 2 else (i - 1) % n

    swap_z = [(16 * r + c, 16 * (r ^ 1) + c) for r, c in at]
    swap_xz = [(16 * r + c, 16 * up(r, 8) + c) for r, c in at]
    swap_core = [(16 * r + c, 16 * r + (c ^ 1)) for r, c in at]
    swap_yz = [(16 * r + c, 16 * r + up(c, 16)) for r, c in at]

    odd_r, odd_c = row % 2, core
    active = block_active.reshape(2)
    e2 = encode_coarse.reshape(27, 64, 128)
    d3 = decode_coarse.reshape(27, 128, 128)
    d4 = jnp.transpose(decode_fine, (0, 1, 2, 4, 3)).reshape(27, 64, 192)
    (w_forward,) = call(
        arrange,
        [((ROOM, 384), BF16, HB)],
        [VM] * 4,
        scratch=[pltpu.VMEM((WF, 384), BF16), pltpu.SemaphoreType.DMA((13,))],
    )(encode_fine.reshape(27, 64, 64), e2, d3, d4)
    (w_backward,) = call(arrange_back, [((WB, 384), BF16)], [VM] * 2)(e2, d3)

    feat = features.reshape(8, 128, 64)
    cot = out_cotangent.reshape(8, 128, 64)
    p1, p2 = call(
        pack_x,
        [((528, 128), BF16)] * 2,
        [HB] * 3,
        scratch=[
            pltpu.SMEM((2,), jnp.int32),
            pltpu.VMEM((8, 128, 64), BF16),
            pltpu.VMEM((2, 128, 64), BF16),
            pltpu.SemaphoreType.DMA((11,)),
        ],
    )(active, feat, cot)
    rxz = swap(p2, swap_xz)
    rz = swap(p1, swap_z)
    rz, w_forward = lax.optimization_barrier((rz, w_forward))
    xall, xmask, p3, p4 = call(
        pack_y,
        [((16, 128, 128), BF16), ((3, 16, 128), F32), ((768, 128), BF16), ((768, 128), BF16)],
        [VM] * 5,
        limit=8,
    )(cot, p1, p2, rz, rxz)
    r4 = swap(p4, swap_yz)
    r3 = swap(p3, swap_core)
    r3, w_backward = lax.optimization_barrier((r3, w_backward))

    decoded, slope_ef, g_skip, slope_ec, g_dc, s_in, s_pool, kept = call(
        forward,
        [
            ((8, 128, 64), BF16, HB),
            ((5, 128, 128), F32),
            ((4, 128, 128), F32),
            ((7, 80, 128), F32),
            ((4, 64, 128), BF16),
            ((6, 128, 384), BF16),
            ((7, 64, 256), BF16),
            ((ROOM, 384), BF16, HB),
        ],
        [VM] * 4 + [HB],
        scratch=[
            pltpu.VMEM((3, 28, 8, 128), F32),
            pltpu.VMEM((5, 18, 8, 128), F32),
            pltpu.VMEM((11, 224, 384), BF16),
            pltpu.VMEM((10, 28, 8, 128), F32),
            pltpu.VMEM((10, 96, 256), BF16),
            pltpu.VMEM((8, 80, 384), BF16),
            pltpu.VMEM((5, 8, 8, 128), F32),
            pltpu.VMEM((5, 128, 384), BF16),
            pltpu.VMEM((720, 384), F32),
            pltpu.VMEM((WF, 384), BF16),
            pltpu.VMEM((SPARE + 64, 384), BF16),
            pltpu.VMEM((9, 128, 64), BF16),
            pltpu.SemaphoreType.DMA((7,)),
            pltpu.SemaphoreType.DMA((4,)),
        ],
        flops=4_000_000_000,
        limit=26,
    )(xall, xmask, r3, r4, w_forward)

    def add(keep, got):
        return (keep.astype(F32) + got.astype(F32)).astype(BF16)

    keep_f, send_f = call(
        weights_fine,
        [((ROWS_F, 128), BF16)] * 2,
        [HB],
        scratch=[
            pltpu.VMEM((2, ROWS_F, 128), BF16),
            pltpu.VMEM((COARSE, 384), BF16),
            pltpu.SemaphoreType.DMA((3,)),
        ],
        flops=1_000_000_000,
        limit=26,
    )(kept)
    keep_c, send_c, token = call(
        weights_coarse,
        [((ROWS_C, 128), BF16), ((ROWS_C, 128), BF16), ((1, 1), jnp.int32, SM)],
        [HB, VM],
        scratch=[
            pltpu.VMEM((2, ROWS_C, 128), BF16),
            pltpu.VMEM((KEPT - COARSE, 384), BF16),
            pltpu.SemaphoreType.DMA((1,)),
        ],
        flops=300_000_000,
        limit=26,
    )(kept, g_dc)

    is_odd = odd_r == 1
    q2 = swap(jnp.where(is_odd, g_dc[2:], g_dc[:2]), swap_xz)
    q1 = swap(jnp.where(is_odd, g_dc[:2], g_dc[2:]), swap_z)
    zero = jnp.zeros_like(q1)
    before = jnp.where(row > 0, jnp.where(is_odd, q1, q2), zero)
    after = jnp.where(row < 7, jnp.where(is_odd, q2, q1), zero)
    gx = jnp.concatenate([before, g_dc, after], axis=0)
    is_odd = odd_c + token[0, 0] == 1
    q4 = swap(jnp.where(is_odd, gx[:, 48:], gx[:, :16]), swap_yz)
    q3 = swap(jnp.where(is_odd, gx[:, :16], gx[:, 48:]), swap_core)
    zero = jnp.zeros_like(q3)
    before = jnp.where(col > 0, jnp.where(is_odd, q3, q4), zero)
    after = jnp.where(col < 15, jnp.where(is_odd, q4, q3), zero)
    gx = jnp.concatenate([before, gx, after], axis=1)
    gx, keep_f = lax.optimization_barrier((gx, keep_f))


    keep_b, send_b = call(
        back_encode,
        [((ROWS_B, 128), BF16)] * 2,
        [VM] * 7,
        scratch=[
            pltpu.VMEM((8, 80, 384), BF16),
            pltpu.VMEM((6, 64, 384), BF16),
            pltpu.VMEM((4, 128, 384), BF16),
            pltpu.VMEM((2, ROWS_B, 128), BF16),
        ],
        flops=500_000_000,
        limit=20,
    )(gx, slope_ec, s_pool, s_in, g_skip, slope_ef, w_backward)
    sums = [add(keep, swap(send, swap_core)) for keep, send in ((keep_f, send_f), (keep_c, send_c), (keep_b, send_b))]

    chips = ("row", "colh")
    half = jnp.pad(jnp.concatenate(sums, axis=0), ((0, 64 * CHUNK - 4320), (0, 0))).reshape(64, CHUNK, 128)
    terms = lax.all_to_all(half, chips, 0, 0, tiled=True)
    total = jnp.sum(terms.astype(F32), axis=0).astype(BF16)
    mine = lax.all_to_all(jnp.broadcast_to(total[None], (64, CHUNK, 128)), chips, 0, 0, tiled=True)
    other = swap(mine, swap_core)
    shapes = ((27, 64, 192), (27, 128, 128), (27, 64, 64), (27, 64, 128))
    halves = ((27, 32, 192), (27, 64, 128), (27, 32, 64), (27, 32, 128))
    grads = []
    for of_this_core, values in ((True, mine), (False, other)):
        grads = call(
            functools.partial(unpack, of_this_core),
            [(shape, F32, HB) for shape in shapes],
            [VM] + [HB] * len(grads),
            scratch=[pltpu.VMEM(shape, F32) for shape in halves] + [pltpu.SemaphoreType.DMA((12,))],
            limit=24,
            aliases={1 + k: k for k in range(len(grads))},
        )(values, *grads)
    d_df, d_dc, d_ef, d_ec = grads
    return (
        decoded.reshape(8, 16, 8, 64),
        d_ef.reshape(3, 3, 3, 64, 64),
        d_ec.reshape(3, 3, 3, 64, 128),
        d_dc.reshape(3, 3, 3, 128, 128),
        jnp.transpose(d_df.reshape(3, 3, 3, 64, 192), (0, 1, 2, 4, 3)),
    )


def solution(mesh):
    split = Mesh(mesh.devices.reshape(8, 8, 2), ("row", "colh", "core"))
    field = P("row", ("colh", "core"), None, None)
    return jax.shard_map(
        body,
        mesh=split,
        in_specs=(field, P("row", ("colh", "core"), None), P(), P(), P(), P(), field),
        out_specs=(field, P(), P(), P(), P()),
        check_vma=False,
    )
```
